32 devices in a mesh: dp: 4 (over x, core), seq: 8 (over z, y).
Axes of the slice: x: 2, y: 2, z: 4, core: 2. Of those that a mesh axis runs over, the one named last changes fastest.
Arguments:
- tokens: bfloat16 [16384, 1536], P(('dp', 'seq')), may hold values from -6 to 6
- segment_ids: int32 [16384], P(('dp', 'seq')), may hold values from 0 to 31, never falling along the last dimension, each value on 1 to 1024 neighbouring positions
- in_proj: bfloat16 [1536, 6448], P(('dp', 'seq')), may hold values from -0.15625 to 0.15625
- conv_weight: bfloat16 [4, 3328], P(None, ('dp', 'seq')), may hold values from -3 to 3
- conv_bias: bfloat16 [3328], P(('dp', 'seq')), may hold values from -2 to 2
- out_proj: bfloat16 [3072, 1536], P(('dp', 'seq')), may hold values from -0.109375 to 0.109375
- norm_gain: bfloat16 [1536], P(('dp', 'seq')), may hold values from 0.099609375 to 1.8984375
- gate_gain: bfloat16 [3072], P(('dp', 'seq')), may hold values from 0.099609375 to 1.8984375
- a_log: float32 [48], replicated, may hold values from -4 to 1.5
- dt_bias: float32 [48], replicated, may hold values from -7 to -3
- skip_d: float32 [48], replicated, may hold values from 0.5 to 1.5
- cotangent: bfloat16 [16384, 1536], P(('dp', 'seq')), may hold values from -6 to 6
Outputs:
- output: bfloat16 [16384, 1536], P(('dp', 'seq'))
- grad_tokens: float32 [16384, 1536], P(('dp', 'seq'))
- grad_in_proj: float32 [1536, 6448], P(('dp', 'seq'))
- grad_conv_weight: float32 [4, 3328], P(None, ('dp', 'seq'))
- grad_conv_bias: float32 [3328], P(('dp', 'seq'))
- grad_out_proj: float32 [3072, 1536], P(('dp', 'seq'))
- grad_norm_gain: float32 [1536], P(('dp', 'seq'))
- grad_gate_gain: float32 [3072], P(('dp', 'seq'))
- grad_a_log: float32 [48], replicated
- grad_dt_bias: float32 [48], replicated
- grad_skip_d: float32 [48], replicated
The draws below stay inside these ranges and needn't reach their ends.
Inputs may be any that keep to these rules, and one draw needn't show every extreme that they name: `segment_ids`: segment ids never fall along the tokens; each segment holds 1 to 1024 tokens and one holds exactly 1024.
All inputs are finite; a program needn't handle non-finite values.
Results may differ from the reference program's by a relative error of at most 0.0088.
Values may be sent and summed in bfloat16 or wider, within the bound.
No kernel may reach another device: no remote copies, remote signals or barrier semaphores. Data moves between devices by JAX's collectives and lax.ppermute only.
A program may use at most 256 MiB of HBM per device.

```python
import math
import jax
import jax.numpy as jnp
import numpy as np
from jax import lax

D = 1536
INNER = 3072
HEADDIM = 64
STATE = 128
CONV = 4
GROUP = 256
TOK_DEV = 512
HEADS = 48
XBC = 3328
PROJ = 6448
LENGTH = 4096
TOKENS = 16384
N_DP = 4
DEVICES = 32


def steps_of(key, extent, shards, low, top_value):
    def one(dim, shards_of):
        steps = jax.random.uniform(jax.random.fold_in(jax.random.fold_in(key, 6), dim), (shards_of,), jnp.float32, low / len(shards), top_value / len(shards))
        return jnp.repeat(jnp.exp(steps), extent[dim] // shards_of).reshape((-1,) + (1,) * (len(extent) - dim - 1))

    level = one(*shards[0])
    for cut in shards[1:]:
        level = level * one(*cut)
    return level


def split_up(count, total, most, skew):
    weights = [(1 << 20) // math.isqrt(standing ** skew) + 1 for standing in range(2, count + 1)]
    surplus, holding = total - most - (count - 1), [1] * (count - 1)
    while surplus > 0:
        candidates = [i for i in range(count - 1) if holding[i] < most]
        mass, budget = sum([weights[i] for i in candidates]), surplus
        for i in candidates:
            more = min(most - holding[i], max(1, budget * weights[i] // mass), surplus)
            holding[i] = holding[i] + more
            surplus = surplus - more
    return np.array([most] + holding)


def ragged(key, number_of, total, bound, slope):
    if number_of == 2:
        one = jax.random.randint(key, (), max(1, total - bound), min(bound, total - 1) + 1)
        return jnp.stack([one, total - one])
    tallies = jnp.asarray(split_up(number_of, total, bound, slope), jnp.int32)
    pairs = (number_of - 1) // 2
    donor, receiver = tallies[1:1 + 2 * pairs:2], tallies[2:2 + 2 * pairs:2]
    margin = jnp.minimum(donor - 1, bound - receiver)
    moved = jax.random.randint(jax.random.fold_in(key, 1), (pairs,), 0, 1 << 20) % (margin + 1)
    tallies = tallies.at[1:1 + 2 * pairs:2].set(donor - moved).at[2:2 + 2 * pairs:2].set(receiver + moved)
    return tallies[jax.random.permutation(jax.random.fold_in(key, 2), number_of)]


def normal_values(rng, extent, scale, reach, cuts=(), kind=jnp.bfloat16):
    values = scale * jax.random.normal(rng, extent, jnp.float32)
    if cuts:
        values = values * steps_of(rng, extent, cuts, -0.22, 0.18)
    return jnp.clip(values, -reach, reach).astype(kind)


def setup_inputs(seed: int = 0) -> dict:
    arg_keys = jax.random.split(jax.random.key(seed), 13)
    return {
        "tokens": normal_values(arg_keys[0], (TOKENS, D), 1.0, 6.0, ((0, 32),)),
        "segment_ids": jnp.searchsorted(jnp.cumsum(ragged(arg_keys[1], DEVICES, TOKENS, 2 * TOK_DEV, 2)), jnp.arange(TOKENS), side="right").astype(jnp.int32),
        "in_proj": normal_values(arg_keys[2], (D, PROJ), D ** -0.5, 0.15625, ((0, 32),)),
        "conv_weight": normal_values(arg_keys[3], (CONV, XBC), CONV ** -0.5, 3.0, ((1, 32),)),
        "conv_bias": normal_values(arg_keys[4], (XBC,), 0.5, 2.0, ((0, 32),)),
        "out_proj": normal_values(arg_keys[5], (INNER, D), INNER ** -0.5, 0.109375, ((0, 32),)),
        "norm_gain": jnp.clip(1.0 + 0.18 * jax.random.normal(arg_keys[6], (D,), jnp.float32), 0.099609375, 1.8984375).astype(jnp.bfloat16),
        "gate_gain": jnp.clip(1.0 + 0.18 * jax.random.normal(arg_keys[7], (INNER,), jnp.float32), 0.099609375, 1.8984375).astype(jnp.bfloat16),
        "a_log": jnp.clip(jax.random.uniform(arg_keys[8], (HEADS,), jnp.float32, -4.0, 1.5), -4.0, 1.5),
        "dt_bias": jnp.clip(jax.random.uniform(arg_keys[9], (HEADS,), jnp.float32, -7.0, -3.0), -7.0, -3.0),
        "skip_d": jnp.clip(jax.random.uniform(arg_keys[10], (HEADS,), jnp.float32, 0.5, 1.5), 0.5, 1.5),
        "cotangent": normal_values(arg_keys[11], (TOKENS, D), 1.0, 6.0, ((0, 32),)),
    }


EPSILON = 1e-05
PRECISE = lax.Precision.HIGHEST

@jax.custom_vjp
def low(v):
    return lax.optimization_barrier(v.astype(jnp.bfloat16)).astype(jnp.float32)

@jax.custom_vjp
def low_back(v):
    return v

def low_keep(v):
    return (low(v), None)

def low_pass(kept, grad):
    return (grad,)

def back_keep(v):
    return (v, None)

def back_low(kept, grad):
    return (low(grad),)
low.defvjp(low_keep, low_pass)
low_back.defvjp(back_keep, back_low)

def rms_scale(values, gain):
    return values * lax.rsqrt(lax.optimization_barrier(jnp.mean(values * values, axis=-1, keepdims=True)) + EPSILON) * gain

def gated_norm(mixed_y, gate_z, gain):
    return rms_scale(mixed_y * jax.nn.silu(gate_z), gain)

def convolve(raw_xbc, seg_ids, kernel, bias_term):
    summed = bias_term + kernel[CONV - 1] * raw_xbc
    for offset in range(1, CONV):
        shifted = jnp.concatenate([jnp.zeros((offset, raw_xbc.shape[1]), raw_xbc.dtype), raw_xbc[:-offset]], 0)
        shifted_ids = jnp.concatenate([jnp.full((offset,), -1, jnp.int32), seg_ids[:-offset]], 0)
        summed = summed + jnp.where((shifted_ids == seg_ids)[:, None], kernel[CONV - 1 - offset] * shifted, 0.0)
    return jax.nn.silu(summed)

def group_step(running, inputs):
    carry_state, prev_seg = running
    values_x, keys_b, reads_c, step_dt, decay_log, seg_ids = inputs
    cumulative = jnp.cumsum(decay_log, axis=0)
    positions = jnp.arange(seg_ids.shape[0])
    inside = (seg_ids[:, None] == seg_ids[None, :]) & (positions[:, None] >= positions[None, :])
    spread_log = jnp.where(inside[:, :, None], cumulative[:, None, :] - cumulative[None, :, :], 0.0)
    decays = jnp.where(inside[:, :, None], jnp.exp(spread_log), 0.0)
    scores = jnp.dot(reads_c, keys_b.T, precision=PRECISE)
    mixing = scores[:, :, None] * decays * step_dt[None, :, :]
    within = jnp.einsum('ijh,jhp->ihp', mixing, values_x, precision=PRECISE)
    carried = jnp.where((seg_ids == prev_seg)[:, None], jnp.exp(cumulative), 0.0)
    from_state = jnp.einsum('in,hpn->ihp', reads_c, carry_state, precision=PRECISE) * carried[:, :, None]
    final_seg = seg_ids[-1]
    weights_end = jnp.where((seg_ids == final_seg)[:, None], jnp.exp(cumulative[-1][None, :] - cumulative), 0.0) * step_dt
    added_state = jnp.einsum('jh,jhp,jn->hpn', weights_end, values_x, keys_b, precision=PRECISE)
    retain = jnp.where(final_seg == prev_seg, jnp.exp(cumulative[-1]), 0.0)
    new_state = retain[:, None, None] * carry_state + added_state
    return ((new_state, final_seg), within + from_state)

def forward(stream, seg_ids, in_proj, conv_weight, conv_bias, out_proj, norm_gain, gate_gain, a_log, dt_bias, skip_d):
    normed_in = low(rms_scale(stream, norm_gain))
    projected = low_back(jnp.dot(normed_in, in_proj, precision=PRECISE))
    gate_z = projected[:, :INNER]
    raw_xbc = low(projected[:, INNER:INNER + XBC])
    step_dt = jax.nn.softplus(projected[:, INNER + XBC:] + dt_bias)
    decay_log = -jnp.exp(a_log) * step_dt
    conv_out = convolve(raw_xbc, seg_ids, conv_weight, conv_bias)
    values_x = conv_out[:, :INNER].reshape(-1, HEADS, HEADDIM)
    keys_b = conv_out[:, INNER:INNER + STATE]
    reads_c = conv_out[:, INNER + STATE:]
    blocks = values_x.shape[0] // GROUP
    pieces = tuple((item.reshape((blocks, GROUP) + item.shape[1:]) for item in (values_x, keys_b, reads_c, step_dt, decay_log, seg_ids)))
    start = (jnp.zeros((HEADS, HEADDIM, STATE), jnp.float32), jnp.array(-1, jnp.int32))
    _, mixed_y = lax.scan(jax.checkpoint(group_step), start, pieces)
    mixed_y = mixed_y.reshape(values_x.shape) + skip_d[None, :, None] * values_x
    normed_out = low(gated_norm(mixed_y.reshape(-1, INNER), gate_z, gate_gain))
    return stream + jnp.dot(normed_out, out_proj, precision=PRECISE)

def reference(tokens, segment_ids, in_proj, conv_weight, conv_bias, out_proj, norm_gain, gate_gain, a_log, dt_bias, skip_d, cotangent):
    params = tuple((item.astype(jnp.float32) for item in (in_proj, conv_weight, conv_bias, out_proj, norm_gain, gate_gain))) + (a_log, dt_bias, skip_d)
    streams = tokens.astype(jnp.float32).reshape(N_DP, LENGTH, D)
    seg_rows = segment_ids.reshape(N_DP, LENGTH)
    pulls = cotangent.astype(jnp.float32).reshape(N_DP, LENGTH, D)

    def per_sequence(totals, sequence):
        stream, seg_ids, upstream = sequence

        def apply(values, *weights):
            return forward(values, seg_ids, *weights)
        result, pull_back = jax.vjp(apply, stream, *params)
        grads = pull_back(upstream)
        totals = tuple((total + grad for total, grad in zip(totals, grads[1:])))
        return (totals, (result, grads[0]))
    zeros = tuple((jnp.zeros_like(item) for item in params))
    totals, (results, grad_streams) = lax.scan(per_sequence, zeros, (streams, seg_rows, pulls))
    return (results.reshape(TOKENS, D).astype(jnp.bfloat16), grad_streams.reshape(TOKENS, D)) + totals
```

```python
from functools import partial

import jax
import jax.numpy as jnp
from jax import lax
from jax.experimental import pallas as pl
from jax.experimental.pallas import tpu as pltpu
from jax.sharding import Mesh
from jax.sharding import PartitionSpec as P

INNER = 3072
HEADDIM = 64
STATE = 128
CONV = 4
GROUP = 256
HEADS = 48
XBC = 3328
LONGEST = 1024
HALO = 16

EPSILON = 1e-05
PRECISE = lax.Precision.HIGHEST
BF = jnp.bfloat16
F32 = jnp.float32
NEVER = -1e30

CUM, DT, REACH, CARRY, ENDN, LASTW = 0, 16, 32, 48, 64, 80
SAME, SEG = 96, 100


def shift(v, axis, step):
    n = lax.axis_size(axis)
    return lax.ppermute(v, axis, [(i, (i + step) % n) for i in range(n)])


def along(v, step):
    n = lax.axis_size("a") * lax.axis_size("b")
    route = [(i, i + step) for i in range(n) if 0 <= i + step < n]
    return lax.ppermute(v, ("a", "b"), route)


def to_peer(v, sx, sc):
    n = lax.axis_size("x")
    route = [(x * 2 + c, ((x + sx) % n) * 2 + (c ^ sc)) for x in range(n) for c in range(2)]
    return lax.ppermute(v, ("x", "core"), route)


def peers():
    return [(sx, sc) for sx in range(lax.axis_size("x")) for sc in range(2)]


def group_of(sx, sc):
    x, c, n = lax.axis_index("x"), lax.axis_index("core"), lax.axis_size("x")
    return lax.rem(x + sx + n, n) * 2 + (c + sc) % 2


def gather_group(v):
    slots = []
    for sx in range(lax.axis_size("x")):
        here = v if sx == 0 else shift(v, "x", sx)
        slots += [here, shift(here, "core", 1)]
    return slots


def sum_to_owner(slots):
    total = None
    for sx in range(lax.axis_size("x")):
        both = slots[2 * sx] + shift(slots[2 * sx + 1].astype(BF), "core", 1).astype(F32)
        part = both if sx == 0 else shift(both.astype(BF), "x", -sx).astype(F32)
        total = part if total is None else total + part
    return total


def sum_over_group(v):
    n = lax.axis_size("x")
    v = v.reshape((n, 2) + v.shape[1:])
    v = v + shift(v, "core", 1)[:, ::-1]
    total = v
    for step in range(1, n):
        total = total + jnp.roll(shift(v, "x", step), step, axis=0)
    return total.reshape((n * 2,) + v.shape[2:])


def gather_blocks(block):
    na, nb = lax.axis_size("a"), lax.axis_size("b")
    a, b = lax.axis_index("a"), lax.axis_index("b")
    whole = jnp.zeros((block.shape[0], na * nb) + block.shape[1:], block.dtype)
    for sa in range(na):
        here = block if sa == 0 else shift(block, "a", sa)
        for sb in range(nb):
            held = here if sb == 0 else shift(here, "b", sb)
            place = lax.rem(a - sa + na, na) * nb + lax.rem(b - sb + nb, nb)
            whole = lax.dynamic_update_slice_in_dim(whole, held[:, None], place, 1)
    return whole


def sum_blocks(grad, block_rows):
    na, nb = lax.axis_size("a"), lax.axis_size("b")
    a, b = lax.axis_index("a"), lax.axis_index("b")

    def part(ra, rb):
        place = lax.rem(a + ra, na) * nb + lax.rem(b + rb, nb)
        return lax.dynamic_slice_in_dim(grad, place, 1, 1)[:, 0]

    total = None
    for ra in range(na):
        held = part(ra, 0)
        for rb in range(1, nb):
            held = held + shift(part(ra, rb).astype(BF), "b", rb).astype(F32)
        got = held if ra == 0 else shift(held.astype(BF), "a", ra).astype(F32)
        total = got if total is None else total + got
    return total


def sum_everywhere(v):
    for axis in ("core", "x", "b", "a"):
        step, n = 1, lax.axis_size(axis)
        while step < n:
            v = v + lax.ppermute(v, axis, [(i, i ^ step) for i in range(n)])
            step *= 2
    return v


def nn(a, b):
    return lax.dot_general(a, b, (((1,), (0,)), ((), ())), preferred_element_type=F32)


def nt(a, b):
    return lax.dot_general(a, b, (((1,), (1,)), ((), ())), preferred_element_type=F32)


def tn(a, b):
    return lax.dot_general(a, b, (((0,), (0,)), ((), ())), preferred_element_type=F32)


def column(table, at):
    lane = lax.broadcasted_iota(jnp.int32, table.shape, 1)
    return jnp.sum(jnp.where(lane == at, table, 0.0), axis=1, keepdims=True)


def low_half(shape):
    return lax.broadcasted_iota(jnp.int32, shape, 1) < HEADDIM


def spread(table, kind, pair):
    first, second = column(table, kind + 2 * pair), column(table, kind + 2 * pair + 1)
    return jnp.where(low_half(table.shape), first, second)


def convolved(ext, taps, same):
    rows = ext.shape[0] - HALO
    pre = taps[CONV : CONV + 1] + taps[CONV - 1 : CONV] * ext[HALO:]
    for k in range(1, CONV):
        pre = pre + same[k - 1] * (taps[CONV - 1 - k : CONV - k] * ext[HALO - k : HALO - k + rows])
    return pre


def extended(halo, main):
    return jnp.concatenate([halo.astype(F32), main.astype(F32)], axis=0)


def conv_kernel(xh_ref, xm_ref, bh_ref, bm_ref, tx_ref, tb_ref, ct_ref, x_ref, bc_ref, own_ref):
    pair = pl.program_id(1)
    table = ct_ref[0]
    same = [table[:, SAME + k : SAME + k + 1] for k in range(CONV - 1)]

    @pl.when(pair == 0)
    def _():
        pre = convolved(extended(bh_ref[0], bm_ref[0]), tb_ref[...], same)
        bc_ref[0] = (pre * jax.nn.sigmoid(pre)).astype(BF)

    pre = convolved(extended(xh_ref[0], xm_ref[0]), tx_ref[...], same)
    x = pre * jax.nn.sigmoid(pre)
    x_ref[0] = x
    weighted = (spread(table, LASTW, pair) * x).astype(BF)
    own_ref[0] = tn(bc_ref[0, :, :STATE], weighted)


def causal(table, segrow, chunk, transposed):
    seg_c = table[chunk * GROUP : (chunk + 1) * GROUP, SEG : SEG + 1]
    seg_r = segrow[:, chunk * GROUP : (chunk + 1) * GROUP]
    down = lax.broadcasted_iota(jnp.int32, (GROUP, GROUP), 0)
    right = lax.broadcasted_iota(jnp.int32, (GROUP, GROUP), 1)
    order = (down <= right) if transposed else (down >= right)
    return jnp.where((seg_c == seg_r) & order, 0.0, NEVER)


def forward_kernel(x_ref, bc_ref, ct_ref, rt_ref, ln_ref, y_ref, score, mask):
    pair = pl.program_id(1)
    table = ct_ref[0]
    chunks = x_ref.shape[1] // GROUP

    @pl.when(pair == 0)
    def _():
        for c in range(chunks):
            rows = slice(c * GROUP, (c + 1) * GROUP)
            score[c] = nt(bc_ref[0, rows, STATE:], bc_ref[0, rows, :STATE])
            mask[c] = causal(table, rt_ref[0, 16:17, :], c, False)

    x = x_ref[0]
    xd = x * spread(table, DT, pair)
    half = low_half(xd.shape)
    parts = [jnp.where(half, xd, 0.0).astype(BF), jnp.where(half, 0.0, xd).astype(BF)]
    cums = [column(table, CUM + 2 * pair + e) for e in range(2)]
    carry = spread(table, CARRY, pair)
    ending = (spread(table, ENDN, pair) * xd).astype(BF)
    skip = ln_ref[0, 0:1, :]
    state = None
    for c in range(chunks):
        rows = slice(c * GROUP, (c + 1) * GROUP)
        y = skip * x[rows]
        for e in range(2):
            row = rt_ref[0, pl.ds(2 * pair + e, 1), rows]
            mixing = score[c] * jnp.exp(cums[e][rows] - row + mask[c])
            y = y + nn(mixing.astype(BF), parts[e][rows])
        if c:
            y = y + carry[rows] * nn(bc_ref[0, rows, STATE:], state.astype(BF))
        y_ref[0, rows, :] = y
        if c + 1 < chunks:
            added = tn(bc_ref[0, rows, :STATE], ending[rows])
            state = added if c == 0 else ln_ref[0, 1 + c : 2 + c, :] * state + added


def gate_kernel(yl_ref, bc_ref, inc_ref, z_ref, dn_ref, gain_ref, ct_ref, y_ref, sums_ref):
    pair = pl.program_id(1)
    y = yl_ref[0] + spread(ct_ref[0], REACH, pair) * nn(bc_ref[0, :, STATE:], inc_ref[0].astype(BF))
    y_ref[0] = y
    z = z_ref[0]
    gated = y * (z * jax.nn.sigmoid(z))
    squares = jnp.sum(gated * gated, axis=1, keepdims=True)
    pulled = jnp.sum(dn_ref[0] * gain_ref[0:1, :] * gated, axis=1, keepdims=True)
    lane = lax.broadcasted_iota(jnp.int32, (y.shape[0], 128), 1)
    both = jnp.where(lane == 0, squares, jnp.where(lane == 1, pulled, 0.0))

    @pl.when(pair == 0)
    def _():
        sums_ref[0] = both

    @pl.when(pair > 0)
    def _():
        sums_ref[0] += both


def gate_back_kernel(
    y_ref, z_ref, dn_ref, gain_ref, sums_ref, bc_ref, ct_ref, out_ref, dy_ref, dz_ref, pull_ref, gg_ref
):
    seq, pair = pl.program_id(0), pl.program_id(1)
    gain = gain_ref[0:1, :]
    y, z, dn = y_ref[0], z_ref[0], dn_ref[0]
    sig = jax.nn.sigmoid(z)
    silu = z * sig
    gated = y * silu
    r = lax.rsqrt(sums_ref[0, :, 0:1] * (1.0 / INNER) + EPSILON)
    unit = gated * r
    out_ref[0] = (unit * gain).astype(BF)
    dg = r * (dn * gain - unit * (r * (1.0 / INNER) * sums_ref[0, :, 1:2]))
    dy = dg * silu
    dy_ref[0] = dy
    dz_ref[0] = (dg * y * (sig * (1.0 + z * (1.0 - sig)))).astype(BF)
    pull_ref[0] = tn(bc_ref[0, :, STATE:], (spread(ct_ref[0], REACH, pair) * dy).astype(BF))
    gg_ref[0] = jnp.broadcast_to(jnp.sum(dn * unit, axis=0, keepdims=True), gg_ref.shape[1:])


def conv_back(d_conv, ext, taps, same):
    rows, width = d_conv.shape
    pre = convolved(ext, taps, same)
    sig = jax.nn.sigmoid(pre)
    d_pre = d_conv * (sig * (1.0 + pre * (1.0 - sig)))
    d_ext = jnp.concatenate(
        [jnp.zeros((HALO, width), F32), taps[CONV - 1 : CONV] * d_pre], axis=0
    )
    grads = [None] * 8
    grads[CONV - 1] = jnp.sum(d_pre * ext[HALO:], axis=0, keepdims=True)
    grads[CONV] = jnp.sum(d_pre, axis=0, keepdims=True)
    for k in range(1, CONV):
        kept = same[k - 1] * d_pre
        grads[CONV - 1 - k] = jnp.sum(kept * ext[HALO - k : HALO - k + rows], axis=0, keepdims=True)
        d_ext = d_ext + taps[CONV - 1 - k : CONV - k] * jnp.concatenate(
            [jnp.zeros((HALO - k, width), F32), kept, jnp.zeros((k, width), F32)], axis=0
        )
    grads = [g if g is not None else jnp.zeros((1, width), F32) for g in grads]
    return d_ext[HALO:].astype(BF), d_ext[:HALO].astype(BF), jnp.concatenate(grads, axis=0)


def backward_kernel(
    x_ref, bc_ref, dy_ref, inc_ref, adj_ref, ct_ref, rt_ref, ln_ref,
    xh_ref, xm_ref, bh_ref, bm_ref, tx_ref, tb_ref,
    dxm_ref, dxh_ref, dbm_ref, dbh_ref, tab_ref, gx_ref, gb_ref, gs_ref,
    score, mask, d_score, d_bc,
):
    pair, pairs = pl.program_id(1), pl.num_programs(1)
    table = ct_ref[0]
    chunks = x_ref.shape[1] // GROUP
    down = lax.broadcasted_iota(jnp.int32, (GROUP, GROUP), 0)
    right = lax.broadcasted_iota(jnp.int32, (GROUP, GROUP), 1)
    before = (right < down).astype(BF)
    upto = (right >= down).astype(BF)
    same = [table[:, SAME + k : SAME + k + 1] for k in range(CONV - 1)]

    @pl.when(pair == 0)
    def _():
        for c in range(chunks):
            rows = slice(c * GROUP, (c + 1) * GROUP)
            score[c] = nt(bc_ref[0, rows, :STATE], bc_ref[0, rows, STATE:])
            mask[c] = causal(table, rt_ref[0, 16:17, :], c, True)
        d_score[...] = jnp.zeros_like(d_score)
        d_bc[...] = jnp.zeros_like(d_bc)
        tab_ref[...] = jnp.zeros_like(tab_ref)

    x, dy = x_ref[0], dy_ref[0]
    dyb = dy.astype(BF)
    half = low_half(x.shape)
    dt = spread(table, DT, pair)
    xd = x * dt
    parts = [jnp.where(half, xd, 0.0).astype(BF), jnp.where(half, 0.0, xd).astype(BF)]
    cums = [column(table, CUM + 2 * pair + e) for e in range(2)]
    pulled = spread(table, CARRY, pair) * dy
    pulled_b = pulled.astype(BF)
    endn = spread(table, ENDN, pair)
    ending = endn * xd
    ending_b = ending.astype(BF)
    skip = ln_ref[0, 0:1, :]
    gs_ref[0] = jnp.broadcast_to(jnp.sum(dy * x, axis=0, keepdims=True), gs_ref.shape[1:])

    def part(c):
        return slice(c * GROUP, (c + 1) * GROUP)

    states, adjoints = [inc_ref[0]], [adj_ref[0]]
    for c in range(chunks - 1):
        added = tn(bc_ref[0, part(c), :STATE], ending_b[part(c)])
        states.append(ln_ref[0, 1 + c : 2 + c, :] * states[-1] + added)
    for c in range(chunks - 1, 0, -1):
        added = tn(bc_ref[0, part(c), STATE:], pulled_b[part(c)])
        adjoints.insert(0, ln_ref[0, 1 + c : 2 + c, :] * adjoints[0] + added)

    lane = lax.broadcasted_iota(jnp.int32, (GROUP, 128), 1)
    d_x = []
    for c in range(chunks):
        rows = part(c)
        keys, reads = bc_ref[0, rows, :STATE], bc_ref[0, rows, STATE:]
        state_b, adj_b = states[c].astype(BF), adjoints[c].astype(BF)
        from_state = pulled[rows] * nn(reads, state_b)
        to_end = nn(keys, adj_b)
        into_state = ending[rows] * to_end
        across = nn(upto, from_state.astype(BF)) + nn(before, into_state.astype(BF))
        across = across + ln_ref[0, 1 + c : 2 + c, :] * jnp.sum(
            states[c] * adjoints[c], axis=0, keepdims=True
        )
        d_bc[rows, :STATE] += nt(ending_b[rows], adj_b)
        d_bc[rows, STATE:] += nt(pulled_b[rows], state_b)
        d_xd, d_scores = [], None
        d_log = []
        for e in range(2):
            row = rt_ref[0, pl.ds(2 * pair + e, 1), rows]
            decay = jnp.exp(row - cums[e][rows] + mask[c])
            weighted = decay * nt(parts[e][rows], dyb[rows])
            d_scores = weighted if d_scores is None else d_scores + weighted
            d_xd.append(nn((score[c] * decay).astype(BF), dyb[rows]))
            crossing = nn(before, (score[c] * weighted).astype(BF))
            d_log.append(jnp.sum(jnp.where(right >= down, crossing, 0.0), axis=1, keepdims=True))
        d_score[c] += d_scores
        u = jnp.where(half[rows], d_xd[0], d_xd[1]) + endn[rows] * to_end
        d_x.append(dt[rows] * u + skip * dy[rows])
        d_step = x[rows] * u
        here = half[rows]
        new = jnp.zeros((GROUP, 128), F32)
        for e in range(2):
            keep = here if e == 0 else jnp.logical_not(here)
            log_e = d_log[e] + jnp.sum(jnp.where(keep, across, 0.0), axis=1, keepdims=True)
            step_e = jnp.sum(jnp.where(keep, d_step, 0.0), axis=1, keepdims=True)
            new = new + jnp.where(lane == 2 * pair + e, log_e, 0.0)
            new = new + jnp.where(lane == 16 + 2 * pair + e, step_e, 0.0)
        tab_ref[0, rows, :] += new

    main, halo, grads = conv_back(
        jnp.concatenate(d_x, axis=0), extended(xh_ref[0], xm_ref[0]), tx_ref[...], same
    )
    dxm_ref[0], dxh_ref[0], gx_ref[0] = main, halo, grads

    @pl.when(pair == pairs - 1)
    def _():
        whole = []
        for c in range(chunks):
            rows = part(c)
            ds = d_score[c].astype(BF)
            d_keys = d_bc[rows, :STATE] + nn(ds, bc_ref[0, rows, STATE:])
            d_reads = d_bc[rows, STATE:] + tn(ds, bc_ref[0, rows, :STATE])
            whole.append(jnp.concatenate([d_keys, d_reads], axis=1))
        main, halo, grads = conv_back(
            jnp.concatenate(whole, axis=0), extended(bh_ref[0], bm_ref[0]), tb_ref[...], same
        )
        dbm_ref[0], dbh_ref[0], gb_ref[0] = main, halo, grads


def tile(rows):
    return pl.BlockSpec((1, rows, 128), lambda q, p: (q, 0, p))


def per_seq(rows, width):
    return pl.BlockSpec((1, rows, width), lambda q, p: (q, 0, 0))


def lanes(rows):
    return pl.BlockSpec((rows, 128), lambda q, p: (0, p))


def shared(rows, width):
    return pl.BlockSpec((rows, width), lambda q, p: (0, 0))


def shape(*dims, dtype=F32):
    return jax.ShapeDtypeStruct(dims, dtype)


def params():
    return pltpu.CompilerParams(
        dimension_semantics=("arbitrary", "arbitrary"), vmem_limit_bytes=40 * 2**20
    )


def cost(flops, size):
    return pl.CostEstimate(flops=int(flops), bytes_accessed=int(size), transcendentals=0)


def on_device(
    tokens, segment_ids, in_proj, conv_weight, conv_bias, out_proj, norm_gain, gate_gain,
    a_log, dt_bias, skip_d, cotangent,
):
    n_x = lax.axis_size("x")
    groups = 2 * n_x
    positions = lax.axis_size("a") * lax.axis_size("b")
    me, place = group_of(0, 0), lax.axis_index("a") * lax.axis_size("b") + lax.axis_index("b")
    index = me * positions + place
    rows, width = tokens.shape
    heads = HEADS // groups
    cols = heads * HEADDIM
    pairs = heads // 2
    chunks = rows // GROUP
    state2 = 2 * STATE

    tok = jnp.stack(gather_group(tokens))
    halo_tok = jnp.stack(gather_group(along(tokens[rows - HALO :], 1)))
    own_halo = jnp.where(place == 0, -1, along(segment_ids[rows - HALO :], 1))
    ids = jnp.stack(gather_group(jnp.concatenate([own_halo, segment_ids])))
    cot = jnp.stack(gather_group(cotangent))

    small = jnp.concatenate([norm_gain, gate_gain, conv_bias, conv_weight.reshape(-1)])
    n_norm, n_gate, n_conv = norm_gain.shape[0], gate_gain.shape[0], conv_bias.shape[0]
    small = jnp.pad(small, (0, -small.shape[0] % 128))
    slots = jnp.stack(gather_group(small))
    by_group = jnp.zeros((groups,) + small.shape, BF)
    for at, (sx, sc) in enumerate(peers()):
        by_group = lax.dynamic_update_slice_in_dim(by_group, slots[at : at + 1], group_of(-sx, sc), 0)
    every = gather_blocks(by_group[:, None]).reshape(groups * positions, -1).astype(F32)
    cuts = [n_norm, n_norm + n_gate, n_norm + n_gate + n_conv]
    gain_in = every[:, : cuts[0]].reshape(-1)
    gain_out = every[:, cuts[0] : cuts[1]].reshape(-1)
    bias_all = every[:, cuts[1] : cuts[2]].reshape(-1)
    taps_all = every[:, cuts[2] : cuts[2] + CONV * n_conv].reshape(-1, CONV, n_conv)
    taps_all = taps_all.transpose(1, 0, 2).reshape(CONV, XBC)
    conv_all = jnp.concatenate([taps_all, bias_all[None], jnp.zeros((3, XBC), F32)], axis=0)
    taps_x = lax.dynamic_slice_in_dim(conv_all, me * cols, cols, 1)
    taps_b = conv_all[:, INNER:]
    gain_g = jnp.broadcast_to(lax.dynamic_slice_in_dim(gain_out, me * cols, cols, 0), (8, cols))
    a_g = lax.dynamic_slice_in_dim(a_log, me * heads, heads, 0)
    bias_g = lax.dynamic_slice_in_dim(dt_bias, me * heads, heads, 0)
    skip_g = lax.dynamic_slice_in_dim(skip_d, me * heads, heads, 0)

    def columns_of(group):
        return (
            jnp.concatenate(
                [
                    lax.dynamic_slice_in_dim(in_proj, INNER + group * cols, cols, 1),
                    in_proj[:, 2 * INNER : INNER + XBC],
                    jnp.pad(
                        lax.dynamic_slice_in_dim(in_proj, INNER + XBC + group * heads, heads, 1),
                        ((0, 0), (0, 128 - heads)),
                    ),
                ],
                axis=1,
            ),
            lax.dynamic_slice_in_dim(in_proj, group * cols, cols, 1),
        )

    first = jnp.zeros((groups, in_proj.shape[0], cols + state2 + 128), BF)
    second = jnp.zeros((groups, in_proj.shape[0], cols), BF)
    for sx, sc in peers():
        one, two = columns_of(group_of(sx, sc))
        if (sx, sc) != (0, 0):
            one, two = to_peer(one, sx, sc), to_peer(two, sx, sc)
        first = lax.dynamic_update_slice_in_dim(first, one[None], group_of(-sx, sc), 0)
        second = lax.dynamic_update_slice_in_dim(second, two[None], group_of(-sx, sc), 0)
    w_first = gather_blocks(first).reshape(width, -1)
    w_gate = gather_blocks(second).reshape(width, -1)
    w_out = gather_blocks(out_proj[None]).reshape(cols, width)
    w_xbc = w_first[:, : cols + state2]
    w_dt = w_first[:, cols + state2 :]

    def normed_of(values):
        v = values.astype(F32)
        scale = lax.rsqrt(jnp.mean(v * v, axis=-1, keepdims=True) + EPSILON)
        return (v * scale * gain_in).astype(BF)

    normed = normed_of(tok).reshape(groups * rows, width)
    normed_halo = normed_of(halo_tok).reshape(groups * HALO, width)

    def project(values, weight, dtype):
        return jnp.dot(values, weight, preferred_element_type=F32).astype(dtype)

    w_x, w_bc = w_xbc[:, :cols], w_xbc[:, cols:]
    x_main = project(normed, w_x, BF).reshape(groups, rows, cols)
    b_main = project(normed, w_bc, BF).reshape(groups, rows, state2)
    raw_halo = project(normed_halo, w_xbc, BF).reshape(groups, HALO, cols + state2)
    x_halo, b_halo = raw_halo[:, :, :cols], raw_halo[:, :, cols:]
    dt_raw = project(normed, w_dt, F32).reshape(groups, rows, 128)[:, :, :heads]

    seg, prev = ids[:, HALO:], ids[:, HALO - 1]
    step_dt = jax.nn.softplus(dt_raw + bias_g)
    rate = jnp.exp(a_g)
    decay_log = -rate * step_dt
    triangle = jnp.tril(jnp.ones((GROUP, GROUP), F32))
    cum = jnp.einsum(
        "ij,qcjh->qcih", triangle, decay_log.reshape(groups, chunks, GROUP, heads), precision=PRECISE
    )
    total = cum[:, :, -1]
    seg_c = seg.reshape(groups, chunks, GROUP)
    last = seg_c[:, :, -1]
    earlier = jnp.concatenate([prev[:, None], last[:, :-1]], axis=1)
    carry = jnp.where((seg_c == earlier[:, :, None])[..., None], jnp.exp(cum), 0.0)
    endn = jnp.where((seg_c == last[:, :, None])[..., None], jnp.exp(total[:, :, None] - cum), 0.0)
    retain = jnp.where((last == earlier)[..., None], jnp.exp(total), 0.0)
    reach_c, end_c = [], []
    run = jnp.ones((groups, heads), F32)
    for c in range(chunks):
        reach_c.append(carry[:, c] * run[:, None])
        run = run * retain[:, c]
    device_decay = run
    run = jnp.ones((groups, heads), F32)
    for c in range(chunks - 1, -1, -1):
        end_c.insert(0, endn[:, c] * run[:, None])
        run = run * retain[:, c]
    reach = jnp.concatenate(reach_c, axis=1)
    last_w = jnp.concatenate(end_c, axis=1) * step_dt

    def wide(v):
        return jnp.pad(v.reshape(groups, rows, heads), ((0, 0), (0, 0), (0, 16 - heads)))

    same = jnp.stack(
        [ids[:, HALO - k : HALO - k + rows] == seg for k in range(1, CONV)], axis=-1
    ).astype(F32)
    col_table = jnp.concatenate(
        [wide(v) for v in (cum, step_dt, reach, carry, endn, last_w)]
        + [same, jnp.zeros((groups, rows, 1), F32), seg.astype(F32)[..., None], jnp.zeros((groups, rows, 27), F32)],
        axis=-1,
    )
    row_table = jnp.concatenate(
        [
            jnp.pad(cum.reshape(groups, rows, heads).transpose(0, 2, 1), ((0, 0), (0, 16 - heads), (0, 0))),
            seg.astype(F32)[:, None],
            jnp.zeros((groups, 7, rows), F32),
        ],
        axis=1,
    )
    lane_table = jnp.concatenate(
        [
            jnp.broadcast_to(jnp.repeat(skip_g, HEADDIM), (groups, 1, cols)),
            jnp.repeat(retain, HEADDIM, axis=-1),
            jnp.zeros((groups, 7 - chunks, cols), F32),
        ],
        axis=1,
    )

    grid = (groups, pairs)
    big = groups * rows * cols
    values_x, bc, own_state = pl.pallas_call(
        conv_kernel,
        grid=grid,
        in_specs=[
            tile(HALO), tile(rows), per_seq(HALO, state2), per_seq(rows, state2),
            lanes(8), shared(8, state2), per_seq(rows, 128),
        ],
        out_specs=[tile(rows), per_seq(rows, state2), tile(STATE)],
        out_shape=[
            shape(groups, rows, cols), shape(groups, rows, state2, dtype=BF), shape(groups, STATE, cols),
        ],
        compiler_params=params(),
        cost_estimate=cost(2 * big * STATE, 8 * big),
        name="conv_and_state",
    )(x_halo, x_main, b_halo, b_main, taps_x, taps_b, col_table)

    hops = -(-(LONGEST - 1) // rows)

    def entering(own, decay, sign):
        total_in, weight = None, jnp.ones_like(decay)
        sent = own.astype(BF)
        for hop in range(1, hops + 1):
            got = along(sent, sign * hop).astype(F32)
            term = got if hop == 1 else jnp.repeat(weight, HEADDIM, axis=-1)[:, None] * got
            total_in = term if total_in is None else total_in + term
            if hop < hops:
                weight = weight * along(decay, sign * hop)
        return total_in

    incoming = entering(own_state, device_decay, 1)

    mixed_local = pl.pallas_call(
        forward_kernel,
        grid=grid,
        in_specs=[tile(rows), per_seq(rows, state2), per_seq(rows, 128), per_seq(24, rows), tile(8)],
        out_specs=tile(rows),
        out_shape=shape(groups, rows, cols),
        scratch_shapes=[pltpu.VMEM((chunks, GROUP, GROUP), F32)] * 2,
        compiler_params=params(),
        cost_estimate=cost(8 * big * GROUP, 8 * big),
        name="mix_within_block",
    )(values_x, bc, col_table, row_table, lane_table)

    gate_z = project(normed, w_gate, F32).reshape(groups, rows, cols)
    d_normed = jnp.einsum("qtd,cd->qtc", cot, w_out, preferred_element_type=F32)

    mixed_y, sums = pl.pallas_call(
        gate_kernel,
        grid=grid,
        in_specs=[
            tile(rows), per_seq(rows, state2), tile(STATE), tile(rows), tile(rows), lanes(8), per_seq(rows, 128),
        ],
        out_specs=[tile(rows), per_seq(rows, 128)],
        out_shape=[shape(groups, rows, cols), shape(groups, rows, 128)],
        compiler_params=params(),
        cost_estimate=cost(2 * big * STATE, 16 * big),
        name="gate",
    )(mixed_local, bc, incoming, gate_z, d_normed, gain_g, col_table)
    sums = sum_over_group(sums[:, :, :2])
    sums = jnp.pad(sums, ((0, 0), (0, 0), (0, 126)))

    normed_out, d_y, d_gate, pull, gate_sums = pl.pallas_call(
        gate_back_kernel,
        grid=grid,
        in_specs=[
            tile(rows), tile(rows), tile(rows), lanes(8), per_seq(rows, 128), per_seq(rows, state2), per_seq(rows, 128),
        ],
        out_specs=[tile(rows), tile(rows), tile(rows), tile(STATE), tile(8)],
        out_shape=[
            shape(groups, rows, cols, dtype=BF), shape(groups, rows, cols),
            shape(groups, rows, cols, dtype=BF), shape(groups, STATE, cols), shape(groups, 8, cols),
        ],
        compiler_params=params(),
        cost_estimate=cost(2 * big * STATE, 20 * big),
        name="gate_back",
    )(mixed_y, gate_z, d_normed, gain_g, sums, bc, col_table)

    later = entering(pull, device_decay, -1)

    grad_out = jnp.einsum("qtc,qtd->cd", normed_out, cot, preferred_element_type=F32)
    grad_out_proj = sum_blocks(grad_out.reshape(1, positions, -1, width), None)[0]
    out_terms = jnp.einsum("qtc,cd->qtd", normed_out, w_out, preferred_element_type=F32)
    stream = tokens.astype(F32)
    output = (stream + sum_to_owner([out_terms[q] for q in range(groups)])).astype(BF)

    def grad_in(values, d_values):
        out = jnp.dot(values.T, d_values, preferred_element_type=F32)
        return sum_blocks(out.reshape(groups, positions, -1, d_values.shape[1]), None)

    d_gate_rows = d_gate.reshape(groups * rows, cols)
    grad_gate_cols = grad_in(normed, d_gate_rows)

    d_xm, d_xh, d_bm, d_bh, d_table, g_x, g_b, g_skip = pl.pallas_call(
        backward_kernel,
        grid=grid,
        in_specs=[
            tile(rows), per_seq(rows, state2), tile(rows), tile(STATE), tile(STATE),
            per_seq(rows, 128), per_seq(24, rows), tile(8),
            tile(HALO), tile(rows), per_seq(HALO, state2), per_seq(rows, state2), lanes(8), shared(8, state2),
        ],
        out_specs=[
            tile(rows), tile(HALO), per_seq(rows, state2), per_seq(HALO, state2), per_seq(rows, 128),
            tile(8), per_seq(8, state2), tile(8),
        ],
        out_shape=[
            shape(groups, rows, cols, dtype=BF), shape(groups, HALO, cols, dtype=BF),
            shape(groups, rows, state2, dtype=BF), shape(groups, HALO, state2, dtype=BF),
            shape(groups, rows, 128), shape(groups, 8, cols), shape(groups, 8, state2), shape(groups, 8, cols),
        ],
        scratch_shapes=[pltpu.VMEM((chunks, GROUP, GROUP), F32)] * 3 + [pltpu.VMEM((rows, state2), F32)],
        compiler_params=params(),
        cost_estimate=cost(20 * big * GROUP, 16 * big),
        name="mix_back",
    )(
        values_x, bc, d_y, incoming, later, col_table, row_table, lane_table,
        x_halo, x_main, b_halo, b_main, taps_x, taps_b,
    )

    spill = along(jnp.concatenate([d_xh, d_bh], axis=2), -1).astype(F32)

    def with_spill(main, more):
        tail = (main[:, rows - HALO :].astype(F32) + more).astype(BF)
        return lax.dynamic_update_slice_in_dim(main, tail, rows - HALO, 1)

    d_xm = with_spill(d_xm, spill[:, :, :cols])
    d_bm = with_spill(d_bm, spill[:, :, cols:])
    d_log, d_step = d_table[:, :, :heads], d_table[:, :, 16 : 16 + heads]
    d_dt = (d_step - rate * d_log) * jax.nn.sigmoid(dt_raw + bias_g)
    grad_bias_g = jnp.sum(d_dt, axis=(0, 1))
    grad_a_g = -jnp.sum(rate * step_dt * d_log, axis=(0, 1))
    grad_skip_g = jnp.sum(g_skip[:, 0].reshape(groups, heads, HEADDIM), axis=(0, 2))
    d_dt_b = jnp.pad(d_dt, ((0, 0), (0, 0), (0, 128 - heads))).astype(BF)
    d_first = jnp.concatenate([d_xm, d_bm, d_dt_b], axis=2).reshape(groups * rows, -1)

    grad_first_cols = grad_in(normed, d_first)
    d_normed_in = jnp.dot(d_first, w_first.T, preferred_element_type=F32)
    d_normed_in = d_normed_in + jnp.dot(d_gate_rows, w_gate.T, preferred_element_type=F32)
    d_normed_in = d_normed_in.reshape(groups, rows, width)

    values = tok.astype(F32)
    scale = lax.rsqrt(jnp.mean(values * values, axis=-1, keepdims=True) + EPSILON)
    grad_norm = jnp.sum(d_normed_in * (values * scale), axis=(0, 1))
    own = sum_to_owner([d_normed_in[q] for q in range(groups)])
    inner = own * gain_in
    r = lax.rsqrt(jnp.mean(stream * stream, axis=-1, keepdims=True) + EPSILON)
    d_stream = r * (inner - stream * (r * r * jnp.mean(inner * stream, axis=-1, keepdims=True)))
    grad_tokens = cotangent.astype(F32) + d_stream

    grad_in_proj = jnp.zeros((in_proj.shape[0], in_proj.shape[1]), F32)
    bc_total = None
    for sx, sc in peers():
        one = lax.dynamic_index_in_dim(grad_first_cols, group_of(sx, sc), 0, False)
        two = lax.dynamic_index_in_dim(grad_gate_cols, group_of(sx, sc), 0, False)
        if (sx, sc) != (0, 0):
            one = to_peer(one.astype(BF), sx, sc).astype(F32)
            two = to_peer(two.astype(BF), sx, sc).astype(F32)
        source = group_of(-sx, sc)
        grad_in_proj = lax.dynamic_update_slice_in_dim(grad_in_proj, two, source * cols, 1)
        grad_in_proj = lax.dynamic_update_slice_in_dim(grad_in_proj, one[:, :cols], INNER + source * cols, 1)
        grad_in_proj = lax.dynamic_update_slice_in_dim(
            grad_in_proj, one[:, cols + state2 : cols + state2 + heads], INNER + XBC + source * heads, 1
        )
        shared_cols = one[:, cols : cols + state2]
        bc_total = shared_cols if bc_total is None else bc_total + shared_cols
    grad_in_proj = lax.dynamic_update_slice(grad_in_proj, bc_total, (0, 2 * INNER))

    def placed(v):
        out = jnp.zeros((groups,) + v.shape, F32)
        return lax.dynamic_update_slice_in_dim(out, v[None], me, 0)

    g_x, g_b = jnp.sum(g_x, axis=0)[: CONV + 1], jnp.sum(g_b, axis=0)[: CONV + 1]
    pieces = [
        placed(g_x), g_b, placed(jnp.sum(gate_sums[:, 0], axis=0)),
        placed(jnp.stack([grad_a_g, grad_bias_g, grad_skip_g])), grad_norm,
    ]
    flat = jnp.concatenate([p.reshape(-1) for p in pieces])
    count = flat.shape[0]
    flat = jnp.pad(flat, (0, -count % 1024)).reshape(-1, 128)
    flat = sum_everywhere(flat).reshape(-1)
    sizes, at, back = [p.size for p in pieces], 0, []
    for p, size in zip(pieces, sizes):
        back.append(flat[at : at + size].reshape(p.shape))
        at += size
    conv_x, conv_b, gate_all, head_all, norm_all = back
    conv_sum = jnp.concatenate([conv_x.transpose(1, 0, 2).reshape(CONV + 1, INNER), conv_b], axis=1)
    conv_own = lax.dynamic_slice_in_dim(conv_sum, index * n_conv, n_conv, 1)
    grad_gate = lax.dynamic_slice_in_dim(gate_all.reshape(-1), index * n_gate, n_gate, 0)
    grad_norm = lax.dynamic_slice_in_dim(norm_all, index * n_norm, n_norm, 0)
    head_all = head_all.transpose(1, 0, 2).reshape(3, HEADS)
    return (
        output, grad_tokens, grad_in_proj, conv_own[:CONV], conv_own[CONV], grad_out_proj,
        grad_norm, grad_gate, head_all[0], head_all[1], head_all[2],
    )


def solution(mesh):
    n_dp, n_seq = mesh.shape["dp"], mesh.shape["seq"]
    slow = 4 if n_seq % 4 == 0 else 1
    finer = Mesh(
        mesh.devices.reshape(n_dp // 2, 2, slow, n_seq // slow), ("x", "core", "a", "b")
    )
    every = ("x", "core", "a", "b")
    rows, flat, second, copied = P(every, None), P(every), P(None, every), P()
    in_specs = (rows, flat, rows, second, flat, rows, flat, flat, copied, copied, copied, rows)
    out_specs = (rows, rows, rows, second, flat, rows, flat, flat, copied, copied, copied)
    return jax.shard_map(
        on_device, mesh=finer, in_specs=in_specs, out_specs=out_specs, check_vma=False
    )
```

```python
import jax
import jax.numpy as jnp
from jax import lax
from jax.experimental import pallas as pl
from jax.experimental.pallas import tpu as pltpu
from jax.sharding import Mesh
from jax.sharding import PartitionSpec as P

INNER = 3072
HEADDIM = 64
STATE = 128
CONV = 4
GROUP = 256
HEADS = 48
XBC = 3328
LONGEST = 1024
HALO = 16
PAIRS = 3
WIDE = PAIRS * 128
LAST = WIDE + 3 * 128

EPSILON = 1e-05
BF = jnp.bfloat16
F32 = jnp.float32
NEVER = -1e30

CUM, DT, CARRY, ENDN, SAME, SEG = 0, 16, 32, 48, 64, 67
SEG_ROW = 16


def shift(v, axis, step):
    n = lax.axis_size(axis)
    return lax.ppermute(v, axis, [(i, (i + step) % n) for i in range(n)])


def along(v, step):
    n = lax.axis_size("a") * lax.axis_size("b")
    route = [(i, i + step) for i in range(n) if 0 <= i + step < n]
    return lax.ppermute(v, ("a", "b"), route)


def exchange(v, axes):
    return lax.all_to_all(v, axes, 0, 0, tiled=True)


def group_of(sx, sc):
    x, c, n = lax.axis_index("x"), lax.axis_index("core"), lax.axis_size("x")
    return lax.rem(x + sx + n, n) * 2 + (c + sc) % 2


def position_of(sa, sb):
    na, nb = lax.axis_size("a"), lax.axis_size("b")
    a, b = lax.axis_index("a"), lax.axis_index("b")
    return lax.rem(a + sa + na, na) * nb + lax.rem(b + sb + nb, nb)


def after(v, *others):
    def nothing(*refs):
        pass

    anywhere = pl.BlockSpec(memory_space=pl.ANY)
    return pl.pallas_call(
        nothing,
        in_specs=[anywhere] * (1 + len(others)),
        out_specs=anywhere,
        out_shape=jax.ShapeDtypeStruct(v.shape, v.dtype),
        input_output_aliases={0: 0},
        name="in_order",
    )(v, *others)


def gather_over_x(v):
    return [v] + [shift(v, "x", sx) for sx in range(1, lax.axis_size("x"))]


def gather_over_cores(along_x, *others):
    slots = []
    for sx, here in enumerate(along_x):
        here = after(here, *others) if sx else here
        slots += [here, shift(here, "core", 1)]
    return slots


def sum_over_cores(kept, sent):
    both = kept + shift(sent.astype(BF), "core", 1).astype(F32)
    return both[0], [both[sx].astype(BF) for sx in range(1, lax.axis_size("x"))]


def sum_to_owner(own, others):
    total = own
    for sx in range(1, lax.axis_size("x")):
        total = total + shift(others[sx - 1], "x", -sx).astype(F32)
    return total


def sum_over_group(v):
    n = lax.axis_size("x")
    v = v.reshape((n, 2) + v.shape[1:])
    v = v + shift(v, "core", 1)[:, ::-1]
    total = v
    for step in range(1, n):
        total = total + jnp.roll(shift(v, "x", step), step, axis=0)
    return total.reshape((n * 2,) + v.shape[2:])


def gather_over_a(block):
    return exchange(jnp.broadcast_to(block[None], (lax.axis_size("a"),) + block.shape), "a")


def gather_over_b(v):
    return [v] + [shift(v, "b", sb) for sb in range(1, lax.axis_size("b"))]


def sum_over_b(parts, *others):
    total = (after(parts[0], *others) if others else parts[0]).astype(F32)
    for rb in range(1, lax.axis_size("b")):
        total = total + shift(parts[rb], "b", rb).astype(F32)
    return total.astype(BF)


def sum_over_a(parts):
    return jnp.sum(exchange(parts, "a").astype(F32), axis=0)


def sum_over(v, axes, marks=()):
    marks = list(marks)
    for axis in axes:
        step, n = 1, lax.axis_size(axis)
        while step < n:
            moved = lax.ppermute(v, axis, [(i, i ^ step) for i in range(n)])
            v = (after(v, marks.pop(0)) if marks else v) + moved
            step *= 2
    return v


def nn(a, b):
    return lax.dot_general(a, b, (((1,), (0,)), ((), ())), preferred_element_type=F32)


def nt(a, b):
    return lax.dot_general(a, b, (((1,), (1,)), ((), ())), preferred_element_type=F32)


def tn(a, b):
    return lax.dot_general(a, b, (((0,), (0,)), ((), ())), preferred_element_type=F32)


def low_half(rows):
    return lax.broadcasted_iota(jnp.int32, (rows, 128), 1) < HEADDIM


def spread(table, kind, pair):
    at = kind + 2 * pair
    return jnp.where(low_half(table.shape[0]), table[:, at : at + 1], table[:, at + 1 : at + 2])


def lanes_of(pair):
    return slice(pair * 128, (pair + 1) * 128)


def rows_of(chunk):
    return slice(chunk * GROUP, (chunk + 1) * GROUP)


def end_of(chunk):
    return slice((chunk + 1) * GROUP - 1, (chunk + 1) * GROUP)


def from_start(carry, chunks):
    out, run = [carry[rows_of(0)]], carry[end_of(0)]
    for c in range(1, chunks):
        out.append(carry[rows_of(c)] * run)
        run = run * carry[end_of(c)]
    return jnp.concatenate(out, axis=0)


def to_block_end(endn, carry, chunks):
    out, run = [endn[rows_of(chunks - 1)]], carry[end_of(chunks - 1)]
    for c in range(chunks - 2, -1, -1):
        out.insert(0, endn[rows_of(c)] * run)
        run = run * carry[end_of(c)]
    return jnp.concatenate(out, axis=0)


def convolved(ext, taps, same):
    rows = ext.shape[0] - HALO
    pre = taps[CONV : CONV + 1] + taps[CONV - 1 : CONV] * ext[HALO:]
    for k in range(1, CONV):
        pre = pre + same[k - 1] * (taps[CONV - 1 - k : CONV - k] * ext[HALO - k : HALO - k + rows])
    return pre


def extended(v):
    rows = v.shape[0] - HALO
    v = v.astype(BF).astype(F32)
    return jnp.concatenate([v[rows:], v[:rows]], axis=0)


def same_columns(table):
    return [table[:, SAME + k : SAME + k + 1] for k in range(CONV - 1)]


def pack_kernel(weight_ref, first_ref, cols, heads):
    state2 = 2 * STATE
    rows = weight_ref.shape[0]
    steps = weight_ref[:, INNER + XBC :].astype(F32)
    steps = jnp.concatenate([steps, jnp.zeros((rows, 128 - steps.shape[1]), F32)], axis=1)
    lane = lax.broadcasted_iota(jnp.int32, (rows, 128), 1)
    for r in range(first_ref.shape[0]):
        at, early = r * cols, cols - WIDE
        tail = INNER + at + early
        first_ref[r, :, :WIDE] = weight_ref[:, tail : tail + WIDE]
        first_ref[r, :, WIDE : WIDE + state2] = weight_ref[:, 2 * INNER : INNER + XBC]
        mine = pltpu.roll(steps, (128 - r * heads) % 128, 1)
        first_ref[r, :, WIDE + state2 : LAST] = jnp.where(lane < heads, mine, 0.0).astype(BF)
        if early:
            first_ref[r, :, LAST : LAST + early] = weight_ref[:, INNER + at : INNER + at + early]
        first_ref[r, :, LAST + early :] = weight_ref[:, at : at + cols]


def unpack_kernel(last_ref, early_ref, weight_ref, out_ref, gain_ref, cols, heads):
    state2 = 2 * STATE
    shared, steps = None, None
    lane = lax.broadcasted_iota(jnp.int32, (out_ref.shape[0], 128), 1)
    for r in range(last_ref.shape[0]):
        at, early = r * cols, cols - WIDE
        tail = INNER + at + early
        out_ref[:, at : at + cols] = early_ref[r, :, :cols].astype(F32)
        out_ref[:, tail : tail + WIDE] = last_ref[r, :, :WIDE].astype(F32)
        if early:
            out_ref[:, INNER + at : tail] = early_ref[r, :, cols:].astype(F32)
        both = last_ref[r, :, WIDE : WIDE + state2].astype(F32)
        shared = both if shared is None else shared + both
        step = jnp.where(lane < heads, last_ref[r, :, WIDE + state2 :].astype(F32), 0.0)
        step = pltpu.roll(step, r * heads, 1) if r else step
        steps = step if steps is None else steps + step
    out_ref[:, 2 * INNER : INNER + XBC] = shared
    out_ref[:, INNER + XBC :] = steps[:, : out_ref.shape[1] - INNER - XBC]
    products = out_ref[...] * weight_ref[...].astype(F32)
    gain_ref[...] = jnp.broadcast_to(jnp.sum(products, axis=1, keepdims=True), gain_ref.shape)


def place_kernel(at_ref, *refs, moves, n_in):
    for source, row, lane, target, to, more, to_lane, count, wide in moves:
        if more is not None:
            to = pl.multiple_of(to + at_ref[more] * count, 16)
        piece = refs[source][row : row + count, lane : lane + wide]
        refs[n_in + target][pl.ds(to, count), to_lane : to_lane + wide] = piece


def norm_kernel(*refs):
    gain_ref, out_ref = refs[-2], refs[-1]
    for r in range(len(refs) - 2):
        v = refs[r][...].astype(F32)
        scale = lax.rsqrt(jnp.mean(v * v, axis=-1, keepdims=True) + EPSILON)
        out_ref[r] = (v * scale * gain_ref[0:1, :]).astype(BF)


def norm_back_kernel(tokens_ref, cot_ref, *refs):
    gain_ref, out_ref = refs[-2], refs[-1]
    total = refs[0][...]
    for ref in refs[1:-2]:
        total = total + ref[...].astype(F32)
    inner = total * gain_ref[0:1, :]
    v = tokens_ref[...].astype(F32)
    r = lax.rsqrt(jnp.mean(v * v, axis=-1, keepdims=True) + EPSILON)
    pull = r * r * jnp.mean(inner * v, axis=-1, keepdims=True)
    out_ref[...] = cot_ref[...].astype(F32) + r * (inner - v * pull)


def table_kernel(dt_ref, seg_ref, par_ref, ct_ref, rt_ref, heads):
    rows = dt_ref.shape[1]
    chunks = rows // GROUP
    lane = lax.broadcasted_iota(jnp.int32, (rows, 128), 1)
    v = dt_ref[0] + par_ref[0:1, :]
    step = jnp.where(lane < heads, jnp.maximum(v, 0.0) + jnp.log1p(jnp.exp(-jnp.abs(v))), 0.0)
    decay = -par_ref[1:2, :] * step
    aux = jnp.concatenate([seg_ref[0], jnp.zeros((120, rows), F32)], axis=0).T
    seg, entering = aux[:, 3:4], aux[:, 4:5]
    cums, carries, ends = [], [], []
    for c in range(chunks):
        cum = decay[rows_of(c)]
        step_rows = 1
        while step_rows < GROUP:
            cum = cum + jnp.concatenate(
                [jnp.zeros((step_rows, 128), F32), cum[: GROUP - step_rows]], axis=0
            )
            step_rows *= 2
        here = seg[rows_of(c)]
        held = entering[rows_of(0)] > 0.5 if c == 0 else here == seg[end_of(c - 1)]
        cums.append(cum)
        carries.append(jnp.where(held, jnp.exp(cum), 0.0))
        ends.append(jnp.where(here == seg[end_of(c)], jnp.exp(cum[GROUP - 1 :] - cum), 0.0))
    kept = lane < heads
    cum = jnp.concatenate(cums, axis=0)
    carry = jnp.where(kept, jnp.concatenate(carries, axis=0), 0.0)
    endn = jnp.where(kept, jnp.concatenate(ends, axis=0), 0.0)
    whole = cum + pltpu.roll(step, DT, 1) + pltpu.roll(carry, CARRY, 1) + pltpu.roll(endn, ENDN, 1)
    aux = pltpu.roll(jnp.where(lane < 4, aux, 0.0), SAME, 1)
    for t in range(ct_ref.shape[1]):
        mine = whole if t == 0 else pltpu.roll(whole, 128 - 2 * PAIRS * t, 1)
        ct_ref[0, t] = jnp.where((lane >= SAME) & (lane < SAME + 4), aux, mine)
    rt_ref[0, :SEG_ROW] = cum.T[:SEG_ROW]
    rt_ref[0, SEG_ROW:] = jnp.broadcast_to(seg_ref[0, 3:4, :], (8, rows))


def conv_kernel(xm_ref, bm_ref, cm_ref, tx_ref, tb_ref, ct_ref, x_ref, bc_ref, own_ref):
    table = ct_ref[0, 0]
    chunks = table.shape[0] // GROUP
    same = same_columns(table)

    @pl.when(pl.program_id(1) == 0)
    def _():
        for i, main in enumerate((bm_ref, cm_ref)):
            pre = convolved(extended(main[0]), tb_ref[:, lanes_of(i)], same)
            bc_ref[0, :, lanes_of(i)] = (pre * jax.nn.sigmoid(pre)).astype(BF)

    weighted = []
    for j in range(PAIRS):
        at = lanes_of(j)
        pre = convolved(extended(xm_ref[0, :, at]), tx_ref[:, at], same)
        x = pre * jax.nn.sigmoid(pre)
        x_ref[0, :, at] = x
        left = to_block_end(spread(table, ENDN, j), spread(table, CARRY, j), chunks)
        weighted.append((left * spread(table, DT, j) * x).astype(BF))
    own_ref[0] = tn(bc_ref[0, :, :STATE], jnp.concatenate(weighted, axis=1))


def causal(table, segrow, chunk, transposed):
    seg_c = table[rows_of(chunk), SEG : SEG + 1]
    seg_r = segrow[:, rows_of(chunk)]
    down = lax.broadcasted_iota(jnp.int32, (GROUP, GROUP), 0)
    right = lax.broadcasted_iota(jnp.int32, (GROUP, GROUP), 1)
    order = (down <= right) if transposed else (down >= right)
    return jnp.where((seg_c == seg_r) & order, 0.0, NEVER)


def halves_of(v, half):
    return [jnp.where(half, v, 0.0).astype(BF), jnp.where(half, 0.0, v).astype(BF)]


def mix_kernel(x_ref, bc_ref, ct_ref, rt_ref, skip_ref, y_ref, score, mask):
    table = ct_ref[0, 0]
    chunks = x_ref.shape[1] // GROUP
    base = pl.program_id(1) * (2 * PAIRS)

    @pl.when(pl.program_id(1) == 0)
    def _():
        for c in range(chunks):
            score[c] = nt(bc_ref[0, rows_of(c), STATE:], bc_ref[0, rows_of(c), :STATE])
            mask[c] = causal(table, rt_ref[0, SEG_ROW : SEG_ROW + 1, :], c, False)

    for j in range(PAIRS):
        at = lanes_of(j)
        x = x_ref[0, :, at]
        xd = x * spread(table, DT, j)
        parts = halves_of(xd, low_half(xd.shape[0]))
        carry = spread(table, CARRY, j)
        ending = (spread(table, ENDN, j) * xd).astype(BF)
        cum_rows = [rt_ref[0, pl.ds(base + 2 * j + e, 1), :] for e in range(2)]
        state = None
        for c in range(chunks):
            rows = rows_of(c)
            y = skip_ref[0:1, at] * x[rows]
            for e in range(2):
                h = 2 * j + e
                row = cum_rows[e][:, rows]
                mixing = score[c] * jnp.exp(table[rows, CUM + h : CUM + h + 1] - row + mask[c])
                y = y + nn(mixing.astype(BF), parts[e][rows])
            if c:
                y = y + carry[rows] * nn(bc_ref[0, rows, STATE:], state.astype(BF))
            y_ref[0, rows, at] = y
            if c + 1 < chunks:
                added = tn(bc_ref[0, rows, :STATE], ending[rows])
                state = added if c == 0 else carry[end_of(c)] * state + added


def gate_kernel(yl_ref, bc_ref, inc_ref, z_ref, dn_ref, gain_ref, ct_ref, y_ref, sums_ref, held):
    table = ct_ref[0, 0]
    chunks = table.shape[0] // GROUP
    from_state = nn(bc_ref[0, :, STATE:], inc_ref[0].astype(BF))
    squares, pulled = None, None
    for j in range(PAIRS):
        at = lanes_of(j)
        y = yl_ref[0, :, at] + from_start(spread(table, CARRY, j), chunks) * from_state[:, at]
        y_ref[0, :, at] = y
        z = z_ref[0, :, at]
        gated = y * (z * jax.nn.sigmoid(z))
        square, pull = gated * gated, dn_ref[0, :, at] * gain_ref[0:1, at] * gated
        squares = square if j == 0 else squares + square
        pulled = pull if j == 0 else pulled + pull
    lane = lax.broadcasted_iota(jnp.int32, squares.shape, 1)
    squares = jnp.sum(squares, axis=1, keepdims=True)
    pulled = jnp.sum(pulled, axis=1, keepdims=True)
    both = jnp.where(lane == 0, squares, jnp.where(lane == 1, pulled, 0.0))
    first = pl.program_id(1) == 0

    @pl.when(first)
    def _():
        held[...] = both

    @pl.when(jnp.logical_not(first))
    def _():
        held[...] += both

    @pl.when(pl.program_id(1) == pl.num_programs(1) - 1)
    def _():
        sums_ref[0] = held[...].T[:8]


def gate_back_kernel(
    y_ref, z_ref, dn_ref, gain_ref, sums_ref, bc_ref, ct_ref, out_ref, dy_ref, dz_ref, pull_ref, gg_ref
):
    table = ct_ref[0, 0]
    chunks = table.shape[0] // GROUP
    sums = jnp.concatenate([sums_ref[0], jnp.zeros((120, table.shape[0]), F32)], axis=0).T
    r = lax.rsqrt(sums[:, 0:1] * (1.0 / INNER) + EPSILON)
    along_unit = r * (1.0 / INNER) * sums[:, 1:2]
    pulled = []
    for j in range(PAIRS):
        at = lanes_of(j)
        gain = gain_ref[0:1, at]
        y, z, dn = y_ref[0, :, at], z_ref[0, :, at], dn_ref[0, :, at]
        sig = jax.nn.sigmoid(z)
        silu = z * sig
        unit = y * silu * r
        out_ref[0, :, at] = (unit * gain).astype(BF)
        dg = r * (dn * gain - unit * along_unit)
        dy = dg * silu
        dy_ref[0, :, at] = dy
        dz_ref[0, : y.shape[0], at] = (dg * y * (sig * (1.0 + z * (1.0 - sig)))).astype(BF)
        dz_ref[0, y.shape[0] :, at] = jnp.zeros((HALO, 128), BF)
        pulled.append((from_start(spread(table, CARRY, j), chunks) * dy).astype(BF))
        grad = jnp.sum(dn * unit, axis=0, keepdims=True)
        gg_ref[0, :, at] = jnp.broadcast_to(grad, (8, 128))
    pull_ref[0] = tn(bc_ref[0, :, STATE:], jnp.concatenate(pulled, axis=1))


def conv_back(d_conv, ext, taps, same):
    rows, width = d_conv.shape
    pre = convolved(ext, taps, same)
    sig = jax.nn.sigmoid(pre)
    d_pre = d_conv * (sig * (1.0 + pre * (1.0 - sig)))
    d_ext = jnp.concatenate(
        [jnp.zeros((HALO, width), F32), taps[CONV - 1 : CONV] * d_pre], axis=0
    )
    grads = [None] * 8
    grads[CONV - 1] = jnp.sum(d_pre * ext[HALO:], axis=0, keepdims=True)
    grads[CONV] = jnp.sum(d_pre, axis=0, keepdims=True)
    for k in range(1, CONV):
        kept = same[k - 1] * d_pre
        grads[CONV - 1 - k] = jnp.sum(kept * ext[HALO - k : HALO - k + rows], axis=0, keepdims=True)
        d_ext = d_ext + taps[CONV - 1 - k : CONV - k] * jnp.concatenate(
            [jnp.zeros((HALO - k, width), F32), kept, jnp.zeros((k, width), F32)], axis=0
        )
    grads = [g if g is not None else jnp.zeros((1, width), F32) for g in grads]
    d_rows = jnp.concatenate([d_ext[HALO:], d_ext[:HALO]], axis=0).astype(BF)
    return d_rows, jnp.concatenate(grads, axis=0)


def mix_back_kernel(*refs, base, first, last):
    x_ref, bc_ref, dy_ref, inc_ref, adj_ref, ct_ref, rt_ref, skip_ref, xm_ref, tx_ref = refs[:10]
    at_ref = 10
    if not first:
        before_ref = refs[at_ref]
        at_ref += 1
    if last:
        bm_ref, cm_ref, dt_ref, tb_ref, par_ref = refs[at_ref : at_ref + 5]
    if last:
        d_ref, gx_ref, gs_ref, gb_ref, gh_ref = refs[-6:-1]
    else:
        d_ref, gx_ref, gs_ref, part_ref = refs[-5:-1]
    d_x = refs[-1]

    table = ct_ref[0, 0]
    chunks = x_ref.shape[1] // GROUP
    down = lax.broadcasted_iota(jnp.int32, (GROUP, GROUP), 0)
    right = lax.broadcasted_iota(jnp.int32, (GROUP, GROUP), 1)
    before = (right < down).astype(BF)
    upto = (right >= down).astype(BF)
    same = same_columns(table)
    lane = lax.broadcasted_iota(jnp.int32, (GROUP, 128), 1)
    half = low_half(GROUP)

    def lane_wise(kind, c):
        return jnp.concatenate([spread(table[rows_of(c)], kind, j) for j in range(PAIRS)], axis=1)

    carries = [lane_wise(CARRY, c) for c in range(chunks)]
    pulled = [carries[c] * dy_ref[0, rows_of(c), :] for c in range(chunks)]
    xds = [x_ref[0, rows_of(c), :] * lane_wise(DT, c) for c in range(chunks)]
    endns = [lane_wise(ENDN, c) for c in range(chunks)]
    endings = [endns[c] * xds[c] for c in range(chunks)]
    states, adjoints = [inc_ref[0]], [adj_ref[0]]
    for c in range(chunks - 1):
        added = tn(bc_ref[0, rows_of(c), :STATE], endings[c].astype(BF))
        states.append(carries[c][GROUP - 1 :] * states[-1] + added)
    for c in range(chunks - 1, 0, -1):
        added = tn(bc_ref[0, rows_of(c), STATE:], pulled[c].astype(BF))
        adjoints.insert(0, carries[c][GROUP - 1 :] * adjoints[0] + added)

    d_keys, d_reads, all_logs, all_steps = [], [], [], []
    for c in range(chunks):
        rows = rows_of(c)
        keys, reads = bc_ref[0, rows, :STATE], bc_ref[0, rows, STATE:]
        state_b, adj_b = states[c].astype(BF), adjoints[c].astype(BF)
        from_state = pulled[c] * nn(reads, state_b)
        to_end = nn(keys, adj_b)
        across = nn(upto, from_state.astype(BF)) + nn(before, (endings[c] * to_end).astype(BF))
        across = across + carries[c][GROUP - 1 :] * jnp.sum(
            states[c] * adjoints[c], axis=0, keepdims=True
        )
        d_k, d_r = nt(endings[c].astype(BF), adj_b), nt(pulled[c].astype(BF), state_b)
        score = nt(keys, reads)
        mask = causal(table, rt_ref[0, SEG_ROW : SEG_ROW + 1, :], c, True)
        d_scores = None
        logs, steps = jnp.zeros((GROUP, 128), F32), jnp.zeros((GROUP, 128), F32)
        for j in range(PAIRS):
            at = lanes_of(j)
            dy = dy_ref[0, rows, at]
            dyb = dy.astype(BF)
            parts = halves_of(xds[c][:, at], half)
            d_xd = []
            crossings = []
            for e in range(2):
                h = 2 * j + e
                row = rt_ref[0, base + h : base + h + 1, rows]
                decay = jnp.exp(row - table[rows, CUM + h : CUM + h + 1] + mask)
                weighted = decay * nt(parts[e], dyb)
                d_scores = weighted if d_scores is None else d_scores + weighted
                d_xd.append(nn((score * decay).astype(BF), dyb))
                crossing = nn(before, (score * weighted).astype(BF))
                crossings.append(
                    jnp.sum(jnp.where(right >= down, crossing, 0.0), axis=1, keepdims=True)
                )
            u = jnp.where(half, d_xd[0], d_xd[1]) + endns[c][:, at] * to_end[:, at]
            x = x_ref[0, rows, at]
            d_x[rows, at] = spread(table[rows], DT, j) * u + skip_ref[0:1, at] * dy
            d_step = x * u
            for e in range(2):
                keep = half if e == 0 else jnp.logical_not(half)
                log_e = crossings[e] + jnp.sum(
                    jnp.where(keep, across[:, at], 0.0), axis=1, keepdims=True
                )
                step_e = jnp.sum(jnp.where(keep, d_step, 0.0), axis=1, keepdims=True)
                place = lane == base + 2 * j + e
                logs = jnp.where(place, log_e, logs)
                steps = jnp.where(place, step_e, steps)
        all_logs.append(logs)
        all_steps.append(steps)
        ds = d_scores.astype(BF)
        d_keys.append(d_k + nn(ds, reads))
        d_reads.append(d_r + tn(ds, keys))

    for j in range(PAIRS):
        at = lanes_of(j)
        grad = jnp.sum(dy_ref[0, :, at] * x_ref[0, :, at], axis=0, keepdims=True)
        gs_ref[0, :, at] = jnp.broadcast_to(grad, (8, 128))
        d_rows, grads = conv_back(d_x[:, at], extended(xm_ref[0, :, at]), tx_ref[:, at], same)
        d_ref[0, :, at], gx_ref[0, :, at] = d_rows, grads

    state2 = 2 * STATE
    for i, d_rows in enumerate((d_keys, d_reads)):
        at = lanes_of(i)
        whole = jnp.concatenate(d_rows, axis=0)
        if not first:
            whole = whole + before_ref[0, :, at]
        if last:
            main_ref = (bm_ref, cm_ref)[i]
            d_rows, grads = conv_back(whole, extended(main_ref[0]), tb_ref[:, at], same)
            d_ref[0, :, lanes_of(PAIRS + i)], gb_ref[0, :, at] = d_rows, grads
        else:
            part_ref[0, :, at] = whole
    logs, steps = jnp.concatenate(all_logs, axis=0), jnp.concatenate(all_steps, axis=0)
    if not first:
        logs = logs + before_ref[0, :, state2 : state2 + 128]
        steps = steps + before_ref[0, :, state2 + 128 :]
    if last:
        rows = logs.shape[0]
        v = dt_ref[0, :rows] + par_ref[0:1, :]
        step_dt = jnp.maximum(v, 0.0) + jnp.log1p(jnp.exp(-jnp.abs(v)))
        d_dt = (steps - par_ref[1:2, :] * logs) * jax.nn.sigmoid(v)
        d_ref[0, :rows, lanes_of(PAIRS + 2)] = d_dt.astype(BF)
        d_ref[0, rows:, lanes_of(PAIRS + 2)] = jnp.zeros((HALO, 128), BF)
        by_bias = jnp.sum(d_dt, axis=0, keepdims=True)
        by_log = -jnp.sum(par_ref[1:2, :] * step_dt * logs, axis=0, keepdims=True)
        gh_ref[0] = jnp.concatenate([by_log, by_bias, jnp.zeros((6, 128), F32)], axis=0)
    else:
        part_ref[0, :, state2 : state2 + 128] = logs
        part_ref[0, :, state2 + 128 :] = steps


def split_kernel(at_ref, v_ref, out_ref):
    out_ref[0] = v_ref[:, 0].astype(BF)


def split_both_kernel(at_ref, v_ref, w_ref, out_ref):
    groups, rows, cols = v_ref.shape[0], v_ref.shape[2], v_ref.shape[3]
    many = w_ref.shape[2]
    for g in range(groups):
        out_ref[0, g * rows : (g + 1) * rows, :cols] = v_ref[g, 0].astype(BF)
    for half in range(2):
        here = w_ref[0, 0, :, half * cols : (half + 1) * cols].astype(BF)
        out_ref[0, half * many : (half + 1) * many, cols:] = here


def shape(*dims, dtype=F32):
    return jax.ShapeDtypeStruct(dims, dtype)


def params(n=2, limit=48):
    return pltpu.CompilerParams(
        dimension_semantics=("arbitrary",) * n, vmem_limit_bytes=limit * 2**20
    )


def cost(flops, size):
    return pl.CostEstimate(flops=int(flops), bytes_accessed=int(size), transcendentals=0)


def on_device(
    tokens, segment_ids, in_proj, conv_weight, conv_bias, out_proj, norm_gain, gate_gain,
    a_log, dt_bias, skip_d, cotangent,
):
    n_x = lax.axis_size("x")
    na, nb = lax.axis_size("a"), lax.axis_size("b")
    groups, positions = 2 * n_x, na * nb
    me, place = group_of(0, 0), position_of(0, 0)
    index = me * positions + place
    rows, width = tokens.shape
    long = rows + HALO
    heads = HEADS // groups
    cols = heads * HEADDIM
    n_steps = heads // (2 * PAIRS)
    state2 = 2 * STATE
    early = cols - WIDE
    first_cols, all_cols = LAST + early, LAST + cols + early
    in_rows, out_rows = in_proj.shape[0], out_proj.shape[0]
    aligned = in_rows % 16 == 0 and width == 2 * cols and 2 * out_rows == groups * in_rows
    anywhere = pl.BlockSpec(memory_space=pl.ANY)

    small = jnp.concatenate([norm_gain, gate_gain, conv_bias, conv_weight.reshape(-1)])
    n_norm, n_gate, n_conv = norm_gain.shape[0], gate_gain.shape[0], conv_bias.shape[0]
    small = jnp.pad(small, (0, -small.shape[0] % 128))
    every = jnp.zeros((groups * positions, small.shape[0]), BF)
    every = lax.dynamic_update_slice_in_dim(every, small[None], index, 0)

    packed = pl.pallas_call(
        lambda *refs: pack_kernel(*refs, cols=cols, heads=heads),
        grid=(1,),
        in_specs=[pl.BlockSpec(in_proj.shape, lambda i: (0, 0))],
        out_specs=pl.BlockSpec((groups, in_rows, all_cols), lambda i: (0, 0, 0)),
        out_shape=shape(groups, in_rows, all_cols, dtype=BF),
        compiler_params=params(1),
        name="pack_weights",
    )(in_proj)
    held = exchange(packed, ("x", "core"))
    every = sum_over(every, ("a", "b", "x", "core"), [packed, packed, packed, held])
    block = held[:, :, :first_cols].reshape(-1, first_cols)
    first_over_a = [block] + [shift(block, "a", sa) for sa in range(1, na)]
    first_blocks = [v for here in first_over_a for v in gather_over_b(here)]

    ids_row = jnp.pad(segment_ids.astype(BF)[None], ((0, 15), (0, width - rows)))
    before = along(jnp.concatenate([tokens[rows - HALO :], ids_row], axis=0), 1)
    token_rows = jnp.concatenate([tokens, before[:HALO], ids_row[:8], before[HALO : HALO + 8]], axis=0)
    token_rows = gather_over_x(after(token_rows, every, held))
    slots = gather_over_cores(token_rows, *first_blocks)

    every = every.astype(F32)
    cuts = [n_norm, n_norm + n_gate, n_norm + n_gate + n_conv]
    gain_in = every[:, : cuts[0]].reshape(1, -1)
    gain_out = every[:, cuts[0] : cuts[1]].reshape(-1)
    bias_all = every[:, cuts[1] : cuts[2]].reshape(-1)
    taps_all = every[:, cuts[2] : cuts[2] + CONV * n_conv].reshape(-1, CONV, n_conv)
    taps_all = taps_all.transpose(1, 0, 2).reshape(CONV, XBC)
    conv_all = jnp.concatenate([taps_all, bias_all[None], jnp.zeros((3, XBC), F32)], axis=0)
    taps_x = lax.dynamic_slice_in_dim(conv_all, me * cols, cols, 1)
    taps_b = conv_all[:, INNER:]
    gain_g = jnp.broadcast_to(lax.dynamic_slice_in_dim(gain_out, me * cols, cols, 0), (8, cols))
    a_g = lax.dynamic_slice_in_dim(a_log, me * heads, heads, 0)
    bias_g = lax.dynamic_slice_in_dim(dt_bias, me * heads, heads, 0)
    skip_g = lax.dynamic_slice_in_dim(skip_d, me * heads, heads, 0)
    head_rows = jnp.pad(jnp.stack([bias_g, jnp.exp(a_g)]), ((0, 6), (0, 128 - heads)))
    skip_l = jnp.broadcast_to(jnp.repeat(skip_g, HEADDIM), (8, cols))

    tall = long // 3
    normed = pl.pallas_call(
        norm_kernel,
        grid=(long // tall,),
        in_specs=[pl.BlockSpec((tall, width), lambda i: (i, 0))] * groups
        + [pl.BlockSpec((8, width), lambda i: (0, 0))],
        out_specs=pl.BlockSpec((groups, tall, width), lambda i: (0, i, 0)),
        out_shape=shape(groups, long, width, dtype=BF),
        compiler_params=params(1),
        cost_estimate=cost(10 * groups * rows * width, 4 * groups * rows * width),
        name="input_norm",
    )(*slots, jnp.broadcast_to(gain_in, (8, width)))
    ids = jnp.concatenate([s[long : long + 1, :rows] for s in slots], axis=0)
    halo_ids = jnp.concatenate([s[long + 8 : long + 9, rows - HALO : rows] for s in slots], axis=0)
    ids = jnp.concatenate([jnp.where(place == 0, jnp.asarray(-1, BF), halo_ids), ids], axis=1).astype(F32)
    seg = ids[:, HALO:]
    seg_rows = jnp.stack(
        [(ids[:, HALO - k : HALO - k + rows] == seg).astype(F32) for k in range(1, CONV)]
        + [seg, (seg == ids[:, HALO - 1 : HALO]).astype(F32)]
        + [jnp.zeros_like(seg)] * 3,
        axis=1,
    )

    b_behind = jnp.stack([lax.rem(lax.axis_index("b") - sb + nb, nb) for sb in range(nb)])
    behind = jnp.stack([position_of(-sa, -sb) for sa in range(na) for sb in range(nb)])

    def place_rows(blocks, moves, outs, at, *others):
        return pl.pallas_call(
            lambda *refs: place_kernel(*refs, moves=moves, n_in=len(blocks) + len(others)),
            grid_spec=pltpu.PrefetchScalarGridSpec(
                num_scalar_prefetch=1,
                grid=(1,),
                in_specs=[pl.BlockSpec(v.shape, lambda i, s: (0, 0)) for v in blocks]
                + [anywhere] * len(others),
                out_specs=[pl.BlockSpec(v.shape, lambda i, s: (0, 0)) for v in outs],
            ),
            out_shape=outs,
            compiler_params=params(1, 56),
            name="place_weights",
        )(at, *blocks, *others)

    def in_moves(source, target, own_lane, lane, wide, held_by, many):
        return [
            (
                source + sb, a * many + i * in_rows, own_lane,
                target, ((held_by + i) * positions + a * nb) * in_rows, sb, lane, in_rows, wide,
            )
            for sb in range(nb) for a in range(na) for i in range(min(groups, many // in_rows))
        ]

    def whole_rows(blocks, many, parts):
        out = jnp.zeros((parts, na, nb, many) + blocks[0].shape[-1:], BF)
        for sb in range(nb):
            v = blocks[sb].reshape(na, parts, many, -1).transpose(1, 0, 2, 3)[:, :, None]
            out = lax.dynamic_update_slice_in_dim(out, v, b_behind[sb], 2)
        return out.reshape(parts * positions * many, -1)

    def flat2(v):
        return v.reshape(-1, v.shape[-1])

    if aligned:
        moves = [
            (k, g * in_rows, 0, 0, g * positions * in_rows, k, 0, in_rows, first_cols)
            for k in range(positions) for g in range(groups)
        ]
        (w_first,) = place_rows(first_blocks, moves, [shape(width, first_cols, dtype=BF)], behind, normed)
    else:
        w_first = jnp.zeros((groups, positions, in_rows, first_cols), BF)
        for k in range(positions):
            v = first_blocks[k].reshape(groups, 1, in_rows, first_cols)
            w_first = lax.dynamic_update_slice_in_dim(w_first, v, behind[k], 1)
        w_first = w_first.reshape(width, first_cols)

    cot_rows = gather_over_x(after(cotangent, w_first))
    gate_block = held[:, :, first_cols:].reshape(-1, cols)
    if aligned:
        out_block = jnp.concatenate([out_proj[:, :cols], out_proj[:, cols:]], axis=0)
        gate_over_a = gather_over_a(after(gate_block, w_first))
    else:
        gate_over_a, out_over_a = gather_over_a(gate_block), gather_over_a(out_proj)

    normed_rows = normed.reshape(groups * long, width)
    proj = jnp.dot(normed_rows, w_first, preferred_element_type=F32).reshape(groups, long, first_cols)
    keys_at = WIDE // 128
    if aligned:
        gate_blocks = gather_over_b(after(gate_over_a, proj))

    def step_tile(t):
        return jnp.where(t == n_steps - 1, 0, LAST // WIDE + t)

    def tile(count):
        return pl.BlockSpec((1, count, WIDE), lambda q, t: (q, 0, t))

    def narrow(at):
        return pl.BlockSpec((1, long, 128), lambda q, t: (q, 0, at))

    def per_seq(count, wide):
        return pl.BlockSpec((1, count, wide), lambda q, t: (q, 0, 0))

    def lanes(count):
        return pl.BlockSpec((count, WIDE), lambda q, t: (0, t))

    by_step = pl.BlockSpec((1, 1, rows, 128), lambda q, t: (q, t, 0, 0))
    all_taps = pl.BlockSpec((8, state2), lambda q, t: (0, 0))

    col_table, row_table = pl.pallas_call(
        lambda *refs: table_kernel(*refs, heads=heads),
        grid=(groups,),
        in_specs=[
            pl.BlockSpec((1, rows, 128), lambda q: (q, 0, keys_at + 2)),
            pl.BlockSpec((1, 8, rows), lambda q: (q, 0, 0)),
            pl.BlockSpec((8, 128), lambda q: (0, 0)),
        ],
        out_specs=[
            pl.BlockSpec((1, n_steps, rows, 128), lambda q: (q, 0, 0, 0)),
            pl.BlockSpec((1, SEG_ROW + 8, rows), lambda q: (q, 0, 0)),
        ],
        out_shape=[shape(groups, n_steps, rows, 128), shape(groups, SEG_ROW + 8, rows)],
        compiler_params=params(1),
        cost_estimate=cost(100 * groups * rows * 128, 16 * groups * rows * 128),
        name="token_table",
    )(proj, seg_rows, head_rows)

    if aligned:
        out_block = after(out_block, w_first)
        out_over_a = jnp.stack([out_block] + [shift(out_block, "a", sa) for sa in range(1, na)])
    grid = (groups, n_steps)
    big = groups * rows * cols
    values_x, bc, own_state = pl.pallas_call(
        lambda *refs: conv_kernel(*refs[:6], *refs[-3:]),
        grid=grid,
        in_specs=[
            pl.BlockSpec((1, long, WIDE), lambda q, t: (q, 0, step_tile(t))),
            narrow(keys_at), narrow(keys_at + 1), lanes(8), all_taps, by_step,
        ],
        out_specs=[tile(rows), per_seq(rows, state2), tile(STATE)],
        out_shape=[
            shape(groups, rows, cols), shape(groups, rows, state2, dtype=BF), shape(groups, STATE, cols),
        ],
        compiler_params=params(),
        cost_estimate=cost(20 * big * STATE, 8 * big),
        name="conv_and_state",
    )(proj, proj, proj, taps_x, taps_b, col_table)

    if aligned:
        out_blocks = gather_over_b(after(out_over_a, values_x))
    else:
        gate_blocks, out_blocks = gather_over_b(gate_over_a), gather_over_b(out_over_a)

    hops = -(-(LONGEST - 1) // rows)
    kept = col_table[:, :, GROUP - 1, CARRY : CARRY + 2 * PAIRS]
    for c in range(1, rows // GROUP):
        kept = kept * col_table[:, :, (c + 1) * GROUP - 1, CARRY : CARRY + 2 * PAIRS]
    device_decay = jnp.repeat(kept.reshape(groups, heads), HEADDIM, axis=-1)[:, None]

    def entering(own, sign):
        sent = jnp.concatenate(
            [own, jnp.broadcast_to(device_decay, (groups, 16, cols))], axis=1
        ).astype(BF)
        total_in, weight = None, None
        for hop in range(1, hops + 1):
            got = along(sent, sign * hop).astype(F32)
            state, decay = got[:, :STATE], got[:, STATE : STATE + 1]
            total_in = state if hop == 1 else total_in + weight * state
            weight = decay if hop == 1 else weight * decay
        return total_in

    incoming = entering(own_state, 1)

    mixed_local = pl.pallas_call(
        mix_kernel,
        grid=grid,
        in_specs=[tile(rows), per_seq(rows, state2), by_step, per_seq(SEG_ROW + 8, rows), lanes(8)],
        out_specs=tile(rows),
        out_shape=shape(groups, rows, cols),
        scratch_shapes=[pltpu.VMEM((rows // GROUP, GROUP, GROUP), F32)] * 2,
        compiler_params=params(),
        cost_estimate=cost(80 * big * GROUP, 8 * big),
        name="mix_within_block",
    )(values_x, bc, col_table, row_table, skip_l)

    if aligned:
        many = groups * in_rows
        moves = in_moves(0, 0, 0, LAST, cols, 0, many)
        moves.append((nb, 0, 0, 0, 0, None, 0, width, LAST))
        moves.append((nb, 0, LAST, 0, 0, None, LAST + cols, width, early))
        blocks = [flat2(v) for v in gate_blocks] + [w_first]
        (w_all,) = place_rows(blocks, moves, [shape(width, all_cols, dtype=BF)], b_behind, mixed_local)
        moves = [
            (sb, sa * many + half * out_rows, 0, 0, 0, sa * nb + sb, half * cols, out_rows, cols)
            for sb in range(nb) for sa in range(na) for half in range(2)
        ]
        blocks = [flat2(v) for v in out_blocks]
        (w_out,) = place_rows(blocks, moves, [shape(cols, width, dtype=BF)], behind)
    else:
        w_out = whole_rows(out_blocks, out_rows, 1)
        w_gate = whole_rows(gate_blocks, in_rows, groups)
        w_all = jnp.concatenate([w_first[:, :LAST], w_gate, w_first[:, LAST:]], axis=1)

    cot = jnp.stack(gather_over_cores(cot_rows, mixed_local))
    gate_z = jnp.dot(normed_rows, w_all[:, LAST : LAST + cols], preferred_element_type=F32)
    gate_z = gate_z.reshape(groups, long, cols)
    d_normed = jnp.einsum("qtd,cd->qtc", cot, w_out, preferred_element_type=F32)

    mixed_y, sums = pl.pallas_call(
        gate_kernel,
        grid=grid,
        in_specs=[
            tile(rows), per_seq(rows, state2), tile(STATE), tile(rows), tile(rows), lanes(8), by_step,
        ],
        out_specs=[tile(rows), per_seq(8, rows)],
        out_shape=[shape(groups, rows, cols), shape(groups, 8, rows)],
        scratch_shapes=[pltpu.VMEM((rows, 128), F32)],
        compiler_params=params(),
        cost_estimate=cost(2 * big * STATE, 16 * big),
        name="gate",
    )(mixed_local, bc, incoming, gate_z, d_normed, gain_g, col_table)
    sums = sum_over_group(sums)

    gate_tile = LAST // WIDE
    normed_out, d_y, d_all, pull, gate_sums = pl.pallas_call(
        gate_back_kernel,
        grid=grid,
        in_specs=[
            tile(rows), tile(rows), tile(rows), lanes(8), per_seq(8, rows), per_seq(rows, state2), by_step,
        ],
        out_specs=[
            tile(rows), tile(rows),
            pl.BlockSpec((1, long, WIDE), lambda q, t: (q, 0, gate_tile + t)), tile(STATE), tile(8),
        ],
        out_shape=[
            shape(groups, rows, cols, dtype=BF), shape(groups, rows, cols),
            shape(groups, long, all_cols, dtype=BF), shape(groups, STATE, cols), shape(groups, 8, cols),
        ],
        compiler_params=params(),
        cost_estimate=cost(2 * big * STATE, 20 * big),
        name="gate_back",
    )(mixed_y, gate_z, d_normed, gain_g, sums, bc, col_table)

    later = entering(pull, -1)

    ahead = jnp.stack([a * nb + lax.rem(lax.axis_index("b") + rb, nb) for rb in range(nb) for a in range(na)])

    def split(grad, many):
        shaped = grad.reshape(-1, positions, many, grad.shape[1])
        g, _, r, c = shaped.shape
        out = pl.pallas_call(
            split_kernel,
            grid_spec=pltpu.PrefetchScalarGridSpec(
                num_scalar_prefetch=1,
                grid=(positions,),
                in_specs=[pl.BlockSpec((g, 1, r, c), lambda k, at: (0, at[k], 0, 0))],
                out_specs=pl.BlockSpec((1, g, r, c), lambda k, at: (k, 0, 0, 0)),
            ),
            out_shape=shape(positions, g, r, c, dtype=BF),
            compiler_params=params(1),
            cost_estimate=cost(grad.size, 6 * grad.size),
            name="split_gradient",
        )(ahead, shaped)
        return out.reshape(nb, na, g, r, c)

    def split_both(grad, other):
        many = groups * in_rows
        return pl.pallas_call(
            split_both_kernel,
            grid_spec=pltpu.PrefetchScalarGridSpec(
                num_scalar_prefetch=1,
                grid=(positions,),
                in_specs=[
                    pl.BlockSpec((groups, 1, in_rows, cols), lambda k, at: (0, at[k], 0, 0)),
                    pl.BlockSpec((1, 1, out_rows, width), lambda k, at: (0, at[k], 0, 0)),
                ],
                out_specs=pl.BlockSpec((1, many, width), lambda k, at: (k, 0, 0)),
            ),
            out_shape=shape(positions, many, width, dtype=BF),
            compiler_params=params(1),
            cost_estimate=cost(2 * grad.size, 12 * grad.size),
            name="split_gradients",
        )(
            ahead, grad.reshape(groups, positions, in_rows, cols), other.reshape(1, positions, out_rows, width)
        ).reshape(nb, na, many, width)

    def grad_of(d_values, low, high):
        d_rows = d_values[:, :, low:high].reshape(groups * long, high - low)
        return jnp.dot(normed_rows.T, d_rows, preferred_element_type=F32)

    grad_out = jnp.einsum("qtc,qtd->cd", normed_out, cot, preferred_element_type=F32)
    grad_gate_cols = grad_of(d_all, LAST, LAST + cols)
    if aligned:
        weights_split = [split_both(grad_gate_cols, grad_out)]
    else:
        weights_split = [split(grad_gate_cols, in_rows), split(grad_out, out_rows)]
    by_core = normed_out.reshape(n_x, 2, rows, cols)

    def outward(values):
        return jnp.einsum("qtc,cd->qtd", values, w_out, preferred_element_type=F32)

    out_sent = outward(by_core[:, 1])
    out_kept = outward(by_core[:, 0])

    d_parts, g_x, g_skip = None, [], []
    waits = list(weights_split)
    split_early = []
    for t in range(n_steps):
        first, last = t == 0, t == n_steps - 1

        def block(*dims, at=(0, 0)):
            return pl.BlockSpec((1,) + dims, lambda q, at=at: (q,) + at)

        def flat(*dims, at=(0, 0)):
            return pl.BlockSpec(dims, lambda q, at=at: at)

        tile_at = 0 if last else LAST // WIDE + t
        operands = [
            (values_x, block(rows, WIDE, at=(0, t))), (bc, block(rows, state2)),
            (d_y, block(rows, WIDE, at=(0, t))), (incoming, block(STATE, WIDE, at=(0, t))),
            (later, block(STATE, WIDE, at=(0, t))),
            (col_table, block(1, rows, 128, at=(t, 0, 0))), (row_table, block(SEG_ROW + 8, rows)),
            (skip_l, flat(8, WIDE, at=(0, t))), (proj, block(long, WIDE, at=(0, tile_at))),
            (taps_x, flat(8, WIDE, at=(0, t))),
        ]
        if not first:
            operands.append((d_parts, block(rows, 2 * state2)))
        if last:
            operands += [
                (proj, block(long, 128, at=(0, keys_at + i))) for i in range(3)
            ] + [(taps_b, flat(8, state2)), (head_rows, flat(8, 128))]
        used = len(operands)
        operands += [(d_all, anywhere)] + [(v, anywhere) for v in waits]
        d_tile = 0 if last else (LAST + cols) // WIDE + t
        made = [
            (block(long, LAST if last else WIDE, at=(0, d_tile)), d_all.shape, BF),
            (block(8, WIDE), (groups, 8, WIDE), F32), (block(8, WIDE), (groups, 8, WIDE), F32),
        ]
        if last:
            made += [
                (block(8, state2), (groups, 8, state2), F32), (block(8, 128), (groups, 8, 128), F32),
            ]
        else:
            made += [(block(rows, 2 * state2), (groups, rows, 2 * state2), F32)]

        def body(*refs, t=t, first=first, last=last, used=used, n_out=len(made)):
            mix_back_kernel(
                *refs[:used], *refs[-n_out - 1 :], base=2 * PAIRS * t, first=first, last=last
            )

        outs = pl.pallas_call(
            body,
            grid=(groups,),
            in_specs=[spec for _, spec in operands],
            out_specs=[spec for spec, _, _ in made],
            out_shape=[jax.ShapeDtypeStruct(s, d) for _, s, d in made],
            scratch_shapes=[pltpu.VMEM((rows, WIDE), F32)],
            input_output_aliases={used: 0},
            compiler_params=params(1),
            cost_estimate=cost(100 * big * GROUP, 16 * big),
            name="mix_back",
        )(*[v for v, _ in operands])
        d_all = outs[0]
        g_x.append(outs[1])
        g_skip.append(outs[2])
        if last:
            g_b, g_head = outs[3:]
        else:
            d_parts = outs[3]
            low = LAST + cols + t * WIDE
            split_early.append(split(grad_of(d_all, low, low + WIDE), in_rows))
            if first:
                weight_sums = [sum_over_b(v) for v in weights_split]
                out_own, out_others = sum_over_cores(out_kept, out_sent)
            waits = [split_early[-1]] + weight_sums * first + out_others * first
    if n_steps == 1:
        weight_sums = [sum_over_b(v) for v in weights_split]
        out_own, out_others = sum_over_cores(out_kept, out_sent)

    weight_totals = [sum_over_a(v) for v in weight_sums]
    stream = tokens.astype(F32)
    output = (stream + sum_to_owner(out_own, out_others)).astype(BF)
    early_sums = [sum_over_b(v, d_all) for v in split_early]

    if aligned:
        gate_part = weight_totals[0][:, :cols].reshape(groups, in_rows, cols)
        both = weight_totals[0][:, cols:]
        grad_out_proj = jnp.concatenate([both[:out_rows], both[out_rows:]], axis=1)
    else:
        gate_part, grad_out_proj = weight_totals[0], weight_totals[1][0]

    def to_owners(v):
        return exchange(v.astype(BF), ("x", "core"))

    d_all = after(d_all, output, *weight_totals)
    spill = along(d_all[:, rows:], -1)
    grad_last = grad_of(d_all, 0, LAST)
    split_last = split(grad_last, in_rows)
    last_sum = sum_over_b(split_last)
    early_part = [sum_over_a(after(v, *weight_totals)) for v in early_sums]
    d_sent = after(d_all, split_last, spill, *early_part)
    end = d_sent[:, rows - HALO : rows] + spill
    d_sent = lax.dynamic_update_slice_in_dim(d_sent, end, rows - HALO, 1)
    early_part = to_owners(jnp.concatenate([gate_part] + early_part, axis=2))

    def inward(d_values, core, kind):
        d_by = d_values.reshape(n_x, 2, long, all_cols)[:, core]
        return jnp.einsum("qtc,dc->qtd", d_by, w_all, preferred_element_type=F32).astype(kind)

    in_sent = inward(d_sent, 1, BF)
    in_kept = inward(d_sent, 0, F32)
    in_own, in_both = sum_over_cores(in_kept, after(in_sent, last_sum, early_part))
    in_others = [shift(v, "x", -sx - 1) for sx, v in enumerate(in_both)]

    def by_rows(wide=width):
        return pl.BlockSpec((128, wide), lambda i: (i, 0))

    grad_tokens = pl.pallas_call(
        norm_back_kernel,
        grid=(rows // 128,),
        in_specs=[by_rows()] * (3 + len(in_others)) + [pl.BlockSpec((8, width), lambda i: (0, 0))],
        out_specs=by_rows(),
        out_shape=shape(rows, width),
        compiler_params=params(1),
        name="input_norm_back",
    )(tokens, cotangent, in_own, *in_others, jnp.broadcast_to(gain_in, (8, width)))

    pieces = [to_owners(sum_over_a(after(last_sum, in_kept, *in_both))), early_part]
    grad_in_proj, gain_products = pl.pallas_call(
        lambda *refs: unpack_kernel(*refs, cols=cols, heads=heads),
        grid=(1,),
        in_specs=[pl.BlockSpec(p.shape, lambda i: (0, 0, 0)) for p in pieces]
        + [pl.BlockSpec(in_proj.shape, lambda i: (0, 0))],
        out_specs=[
            pl.BlockSpec(in_proj.shape, lambda i: (0, 0)), pl.BlockSpec((in_rows, 128), lambda i: (0, 0)),
        ],
        out_shape=[shape(*in_proj.shape), shape(in_rows, 128)],
        compiler_params=params(1),
        name="unpack_gradient",
    )(*pieces, in_proj)
    grad_norm = gain_products[:, 0] / norm_gain.astype(F32)

    def placed(v):
        out = jnp.zeros((groups,) + v.shape, F32)
        return lax.dynamic_update_slice_in_dim(out, v[None], me, 0)

    g_x = jnp.sum(jnp.concatenate(g_x, axis=2), axis=0)[: CONV + 1]
    g_b = jnp.sum(g_b, axis=0)[: CONV + 1]
    g_skip = jnp.sum(jnp.concatenate([g[:, 0] for g in g_skip], axis=1), axis=0)
    grad_skip_g = jnp.sum(g_skip.reshape(1, heads, HEADDIM), axis=2)
    g_head = jnp.sum(g_head, axis=0)[:2, :heads]
    pieces = [
        placed(g_x), g_b, placed(jnp.sum(gate_sums[:, 0], axis=0)),
        placed(jnp.concatenate([g_head, grad_skip_g], axis=0)),
    ]
    flat = jnp.concatenate([p.reshape(-1) for p in pieces])
    count = flat.shape[0]
    flat = jnp.pad(flat, (0, -count % 1024)).reshape(-1, 128)
    marks = [grad_last, split_last, in_sent, in_kept, in_own]
    flat = sum_over(flat, ("x", "a", "b", "core"), marks).reshape(-1)
    at, back = 0, []
    for p in pieces:
        back.append(flat[at : at + p.size].reshape(p.shape))
        at += p.size
    conv_x, conv_b, gate_all, head_all = back
    conv_sum = jnp.concatenate([conv_x.transpose(1, 0, 2).reshape(CONV + 1, INNER), conv_b], axis=1)
    conv_own = lax.dynamic_slice_in_dim(conv_sum, index * n_conv, n_conv, 1)
    grad_gate = lax.dynamic_slice_in_dim(gate_all.reshape(-1), index * n_gate, n_gate, 0)
    head_all = head_all.transpose(1, 0, 2).reshape(3, HEADS)
    return (
        output, grad_tokens, grad_in_proj, conv_own[:CONV], conv_own[CONV], grad_out_proj,
        grad_norm, grad_gate, head_all[0], head_all[1], head_all[2],
    )


def solution(mesh):
    n_dp, n_seq = mesh.shape["dp"], mesh.shape["seq"]
    slow = 4 if n_seq % 4 == 0 else 1
    finer = Mesh(
        mesh.devices.reshape(n_dp // 2, 2, slow, n_seq // slow), ("x", "core", "a", "b")
    )
    every = ("x", "core", "a", "b")
    rows, flat, second, copied = P(every, None), P(every), P(None, every), P()
    in_specs = (rows, flat, rows, second, flat, rows, flat, flat, copied, copied, copied, rows)
    out_specs = (rows, rows, rows, second, flat, rows, flat, flat, copied, copied, copied)
    return jax.shard_map(
        on_device, mesh=finer, in_specs=in_specs, out_specs=out_specs, check_vma=False
    )
```

```python
import jax
import jax.numpy as jnp
from jax import lax
from jax.experimental import pallas as pl
from jax.experimental.pallas import tpu as pltpu
from jax.sharding import Mesh
from jax.sharding import PartitionSpec as P

INNER = 3072
HEADDIM = 64
STATE = 128
CONV = 4
GROUP = 256
HEADS = 48
XBC = 3328
LONGEST = 1024
HALO = 16
TILE = 128
PAIRS = 3
WIDE = PAIRS * 128
LAST = WIDE + 3 * 128

EPSILON = 1e-05
BF = jnp.bfloat16
F32 = jnp.float32
NEVER = -1e30

CUM, DT, CARRY, ENDN, SAME, SEG = 0, 16, 32, 48, 64, 67
SEG_ROW = 16


def shift(v, axis, step):
    n = lax.axis_size(axis)
    return lax.ppermute(v, axis, [(i, (i + step) % n) for i in range(n)])


def along(v, step):
    n = lax.axis_size("a") * lax.axis_size("b")
    route = [(i, i + step) for i in range(n) if 0 <= i + step < n]
    return lax.ppermute(v, ("a", "b"), route)


def exchange(v, axes):
    return lax.all_to_all(v, axes, 0, 0, tiled=True)


def group_of(sx, sc):
    x, c, n = lax.axis_index("x"), lax.axis_index("core"), lax.axis_size("x")
    return lax.rem(x + sx + n, n) * 2 + (c + sc) % 2


def position_of(sa, sb):
    na, nb = lax.axis_size("a"), lax.axis_size("b")
    a, b = lax.axis_index("a"), lax.axis_index("b")
    return lax.rem(a + sa + na, na) * nb + lax.rem(b + sb + nb, nb)


def after(v, *others):
    def nothing(*refs):
        pass

    anywhere = pl.BlockSpec(memory_space=pl.ANY)
    return pl.pallas_call(
        nothing,
        in_specs=[anywhere] * (1 + len(others)),
        out_specs=anywhere,
        out_shape=jax.ShapeDtypeStruct(v.shape, v.dtype),
        input_output_aliases={0: 0},
        name="in_order",
    )(v, *others)


def gather_over_x(v):
    return [v] + [shift(v, "x", sx) for sx in range(1, lax.axis_size("x"))]


def gather_over_cores(along_x, *others):
    slots = []
    for sx, here in enumerate(along_x):
        here = after(here, *others) if sx else here
        slots += [here, shift(here, "core", 1)]
    return slots


def sum_over_cores(kept, sent):
    both = kept + shift(sent.astype(BF), "core", 1).astype(F32)
    return both[0], [both[sx].astype(BF) for sx in range(1, lax.axis_size("x"))]


def sum_to_owner(own, others):
    total = own
    for sx in range(1, lax.axis_size("x")):
        total = total + shift(others[sx - 1], "x", -sx).astype(F32)
    return total


def sum_over_group(v):
    n = lax.axis_size("x")
    v = v.reshape((n, 2) + v.shape[1:])
    v = v + shift(v, "core", 1)[:, ::-1]
    total = v
    for step in range(1, n):
        total = total + jnp.roll(shift(v, "x", step), step, axis=0)
    return total.reshape((n * 2,) + v.shape[2:])


def gather_over_a(block):
    return exchange(jnp.broadcast_to(block[None], (lax.axis_size("a"),) + block.shape), "a")


def gather_over_b(v):
    return [v] + [shift(v, "b", sb) for sb in range(1, lax.axis_size("b"))]


def sum_over_b(parts, *others):
    total = (after(parts[0], *others) if others else parts[0]).astype(F32)
    for rb in range(1, lax.axis_size("b")):
        total = total + shift(parts[rb], "b", rb).astype(F32)
    return total.astype(BF)


def sum_over_a(parts):
    return jnp.sum(exchange(parts, "a").astype(F32), axis=0)


def sum_over(v, axes, marks=()):
    marks = list(marks)
    for axis in axes:
        step, n = 1, lax.axis_size(axis)
        while step < n:
            moved = lax.ppermute(v, axis, [(i, i ^ step) for i in range(n)])
            v = (after(v, marks.pop(0)) if marks else v) + moved
            step *= 2
    return v


def nn(a, b):
    return lax.dot_general(a, b, (((1,), (0,)), ((), ())), preferred_element_type=F32)


def nt(a, b):
    return lax.dot_general(a, b, (((1,), (1,)), ((), ())), preferred_element_type=F32)


def tn(a, b):
    return lax.dot_general(a, b, (((0,), (0,)), ((), ())), preferred_element_type=F32)


def low_half(rows):
    return lax.broadcasted_iota(jnp.int32, (rows, 128), 1) < HEADDIM


def spread(table, kind, pair):
    at = kind + 2 * pair
    return jnp.where(low_half(table.shape[0]), table[:, at : at + 1], table[:, at + 1 : at + 2])


def lane_wise(table, kind):
    high = table.astype(BF)
    low = (table - high.astype(F32)).astype(BF)
    head_of = lax.broadcasted_iota(jnp.int32, (128, WIDE), 1) // HEADDIM + kind
    pick = (head_of == lax.broadcasted_iota(jnp.int32, (128, WIDE), 0)).astype(BF)
    return nn(jnp.concatenate([high, low], axis=1), jnp.concatenate([pick, pick], axis=0))


def lanes_of(pair):
    return slice(pair * 128, (pair + 1) * 128)


def rows_of(chunk):
    return slice(chunk * GROUP, (chunk + 1) * GROUP)


def end_of(chunk):
    return slice((chunk + 1) * GROUP - 1, (chunk + 1) * GROUP)


def from_start(carry, chunks):
    out, run = [carry[rows_of(0)]], carry[end_of(0)]
    for c in range(1, chunks):
        out.append(carry[rows_of(c)] * run)
        run = run * carry[end_of(c)]
    return jnp.concatenate(out, axis=0)


def to_block_end(endn, table, chunks):
    out, run = [endn[rows_of(chunks - 1)]], None
    for c in range(chunks - 2, -1, -1):
        keep = lane_wise(table[(c + 2) * GROUP - 8 : (c + 2) * GROUP], CARRY)[7:]
        run = keep if run is None else run * keep
        out.insert(0, endn[rows_of(c)] * run)
    return jnp.concatenate(out, axis=0)


def earlier_rows(v, k):
    return pltpu.roll(v, k, 0)[: v.shape[0] - HALO]


def convolved(v, taps, same):
    rows = v.shape[0] - HALO
    pre = taps[CONV : CONV + 1] + taps[CONV - 1 : CONV] * v[:rows]
    for k in range(1, CONV):
        pre = pre + same[k - 1] * (taps[CONV - 1 - k : CONV - k] * earlier_rows(v, k))
    return pre


def rounded(v):
    return v.astype(BF).astype(F32)


def same_columns(table):
    rows = table.shape[0]
    return [
        jnp.broadcast_to(table[:, SAME + k : SAME + k + 1], (rows, 128)) for k in range(CONV - 1)
    ]


def pack_kernel(weight_ref, first_ref, cols, heads):
    state2 = 2 * STATE
    rows = weight_ref.shape[0]
    steps = weight_ref[:, INNER + XBC :].astype(F32)
    steps = jnp.concatenate([steps, jnp.zeros((rows, 128 - steps.shape[1]), F32)], axis=1)
    lane = lax.broadcasted_iota(jnp.int32, (rows, 128), 1)
    for r in range(first_ref.shape[0]):
        at, early = r * cols, cols - WIDE
        tail = INNER + at + early
        first_ref[r, :, :WIDE] = weight_ref[:, tail : tail + WIDE]
        first_ref[r, :, WIDE : WIDE + state2] = weight_ref[:, 2 * INNER : INNER + XBC]
        mine = pltpu.roll(steps, (128 - r * heads) % 128, 1)
        first_ref[r, :, WIDE + state2 : LAST] = jnp.where(lane < heads, mine, 0.0).astype(BF)
        if early:
            first_ref[r, :, LAST : LAST + early] = weight_ref[:, INNER + at : INNER + at + early]
        first_ref[r, :, LAST + early :] = weight_ref[:, at : at + cols]


def unpack_kernel(last_ref, early_ref, weight_ref, out_ref, gain_ref, cols, heads):
    state2 = 2 * STATE
    shared, steps = None, None
    lane = lax.broadcasted_iota(jnp.int32, (out_ref.shape[0], 128), 1)
    for r in range(last_ref.shape[0]):
        at, early = r * cols, cols - WIDE
        tail = INNER + at + early
        out_ref[:, at : at + cols] = early_ref[r, :, :cols].astype(F32)
        out_ref[:, tail : tail + WIDE] = last_ref[r, :, :WIDE].astype(F32)
        if early:
            out_ref[:, INNER + at : tail] = early_ref[r, :, cols:].astype(F32)
        both = last_ref[r, :, WIDE : WIDE + state2].astype(F32)
        shared = both if shared is None else shared + both
        step = jnp.where(lane < heads, last_ref[r, :, WIDE + state2 :].astype(F32), 0.0)
        step = pltpu.roll(step, r * heads, 1) if r else step
        steps = step if steps is None else steps + step
    out_ref[:, 2 * INNER : INNER + XBC] = shared
    out_ref[:, INNER + XBC :] = steps[:, : out_ref.shape[1] - INNER - XBC]
    products = out_ref[...] * weight_ref[...].astype(F32)
    gain_ref[...] = jnp.broadcast_to(jnp.sum(products, axis=1, keepdims=True), gain_ref.shape)


def place_kernel(at_ref, *refs, moves, n_in):
    for source, row, lane, target, to, more, to_lane, count, wide in moves:
        if more is not None:
            to = pl.multiple_of(to + at_ref[more] * count, 16)
        piece = refs[source][row : row + count, lane : lane + wide]
        refs[n_in + target][pl.ds(to, count), to_lane : to_lane + wide] = piece


def norm_kernel(*refs):
    gain_ref, out_ref = refs[-2], refs[-1]
    for r in range(len(refs) - 2):
        v = refs[r][...].astype(F32)
        scale = lax.rsqrt(jnp.mean(v * v, axis=-1, keepdims=True) + EPSILON)
        out_ref[r] = (v * scale * gain_ref[0:1, :]).astype(BF)


def norm_back_kernel(tokens_ref, cot_ref, *refs):
    gain_ref, out_ref = refs[-2], refs[-1]
    total = refs[0][...]
    for ref in refs[1:-2]:
        total = total + ref[...].astype(F32)
    inner = total * gain_ref[0:1, :]
    v = tokens_ref[...].astype(F32)
    r = lax.rsqrt(jnp.mean(v * v, axis=-1, keepdims=True) + EPSILON)
    pull = r * r * jnp.mean(inner * v, axis=-1, keepdims=True)
    out_ref[...] = cot_ref[...].astype(F32) + r * (inner - v * pull)


def table_kernel(dt_ref, seg_ref, par_ref, ct_ref, rt_ref, heads):
    rows = dt_ref.shape[1]
    chunks = rows // GROUP
    lane = lax.broadcasted_iota(jnp.int32, (rows, 128), 1)
    v = dt_ref[0] + par_ref[0:1, :]
    step = jnp.where(lane < heads, jnp.maximum(v, 0.0) + jnp.log1p(jnp.exp(-jnp.abs(v))), 0.0)
    decay = -par_ref[1:2, :] * step
    aux = jnp.concatenate([seg_ref[0], jnp.zeros((120, rows), F32)], axis=0).T
    seg, entering = aux[:, 3:4], aux[:, 4:5]
    cums, carries, ends = [], [], []
    for c in range(chunks):
        cum = decay[rows_of(c)]
        step_rows = 1
        while step_rows < GROUP:
            cum = cum + jnp.concatenate(
                [jnp.zeros((step_rows, 128), F32), cum[: GROUP - step_rows]], axis=0
            )
            step_rows *= 2
        here = seg[rows_of(c)]
        held = entering[rows_of(0)] > 0.5 if c == 0 else here == seg[end_of(c - 1)]
        cums.append(cum)
        carries.append(jnp.where(held, jnp.exp(cum), 0.0))
        ends.append(jnp.where(here == seg[end_of(c)], jnp.exp(cum[GROUP - 1 :] - cum), 0.0))
    kept = lane < heads
    cum = jnp.concatenate(cums, axis=0)
    carry = jnp.where(kept, jnp.concatenate(carries, axis=0), 0.0)
    endn = jnp.where(kept, jnp.concatenate(ends, axis=0), 0.0)
    whole = cum + pltpu.roll(step, DT, 1) + pltpu.roll(carry, CARRY, 1) + pltpu.roll(endn, ENDN, 1)
    aux = pltpu.roll(jnp.where(lane < 4, aux, 0.0), SAME, 1)
    for t in range(ct_ref.shape[1]):
        mine = whole if t == 0 else pltpu.roll(whole, 128 - 2 * PAIRS * t, 1)
        ct_ref[0, t] = jnp.where((lane >= SAME) & (lane < SAME + 4), aux, mine)
    rt_ref[0, :SEG_ROW] = cum.T[:SEG_ROW]
    rt_ref[0, SEG_ROW:] = jnp.broadcast_to(seg_ref[0, 3:4, :], (8, rows))


def conv_kernel(xm_ref, bm_ref, cm_ref, tx_ref, tb_ref, ct_ref, x_ref, bc_ref, own_ref):
    table = ct_ref[0, 0]
    chunks = table.shape[0] // GROUP
    same = same_columns(table)

    @pl.when(pl.program_id(1) == 0)
    def _():
        for i, main in enumerate((bm_ref, cm_ref)):
            pre = convolved(rounded(main[0]), tb_ref[:, lanes_of(i)], same)
            bc_ref[0, :, lanes_of(i)] = (pre * jax.nn.sigmoid(pre)).astype(BF)

    weighted = []
    left = to_block_end(lane_wise(table, ENDN), table, chunks) * lane_wise(table, DT)
    for j in range(PAIRS):
        at = lanes_of(j)
        pre = convolved(rounded(xm_ref[0, :, at]), tx_ref[:, at], same)
        x = pre * jax.nn.sigmoid(pre)
        x_ref[0, :, at] = x
        weighted.append((left[:, at] * x).astype(BF))
    own_ref[0] = tn(bc_ref[0, :, :STATE], jnp.concatenate(weighted, axis=1))


def causal(table, segrow, chunk, transposed):
    seg_c = table[rows_of(chunk), SEG : SEG + 1]
    seg_r = segrow[:, rows_of(chunk)]
    down = lax.broadcasted_iota(jnp.int32, (GROUP, GROUP), 0)
    right = lax.broadcasted_iota(jnp.int32, (GROUP, GROUP), 1)
    order = (down <= right) if transposed else (down >= right)
    return jnp.where((seg_c == seg_r) & order, 0.0, NEVER)


def halves_of(v, half):
    return [jnp.where(half, v, 0.0).astype(BF), jnp.where(half, 0.0, v).astype(BF)]


def mix_kernel(x_ref, bc_ref, ct_ref, rt_ref, skip_ref, y_ref, score, mask):
    table = ct_ref[0, 0]
    chunks = x_ref.shape[1] // GROUP
    base = pl.program_id(1) * (2 * PAIRS)

    @pl.when(pl.program_id(1) == 0)
    def _():
        for c in range(chunks):
            score[c] = nt(bc_ref[0, rows_of(c), STATE:], bc_ref[0, rows_of(c), :STATE])
            mask[c] = causal(table, rt_ref[0, SEG_ROW : SEG_ROW + 1, :], c, False)

    dts, endns = lane_wise(table, DT), lane_wise(table, ENDN)
    carries = [lane_wise(table[rows_of(c)], CARRY) for c in range(1, chunks)]
    states = None
    for c in range(chunks):
        rows = rows_of(c)
        x = x_ref[0, rows, :]
        xd = x * dts[rows]
        xdb = xd.astype(BF)
        y_in = skip_ref[0:1, :] * x
        if c:
            y_in = y_in + carries[c - 1] * nn(bc_ref[0, rows, STATE:], states.astype(BF))
        if c + 1 < chunks:
            added = tn(bc_ref[0, rows, :STATE], (endns[rows] * xd).astype(BF))
            states = added if c == 0 else carries[c - 1][GROUP - 1 :] * states + added
        for j in range(PAIRS):
            at = lanes_of(j)
            cum_rows = [rt_ref[0, pl.ds(base + 2 * j + e, 1), :] for e in range(2)]
            for top in range(0, GROUP, TILE):
                here, live = slice(top, top + TILE), slice(0, top + TILE)
                tile_rows = slice(c * GROUP + top, c * GROUP + top + TILE)
                scores, masks = score[c, here, live], mask[c, here, live]
                mixing = []
                for e in range(2):
                    h = 2 * j + e
                    row = cum_rows[e][:, c * GROUP : c * GROUP + top + TILE]
                    decay = jnp.exp(table[tile_rows, CUM + h : CUM + h + 1] - row + masks)
                    mixing.append((scores * decay).astype(BF))
                y = nn(jnp.concatenate(mixing, axis=0), xdb[live, at])
                y_ref[0, tile_rows, at] = y_in[here, at] + jnp.where(low_half(TILE), y[:TILE], y[TILE:])


def gate_kernel(yl_ref, bc_ref, inc_ref, z_ref, dn_ref, gain_ref, ct_ref, y_ref, sums_ref, held):
    table = ct_ref[0, 0]
    chunks = table.shape[0] // GROUP
    from_state = nn(bc_ref[0, :, STATE:], inc_ref[0].astype(BF))
    squares, pulled = None, None
    reach = from_start(lane_wise(table, CARRY), chunks)
    for j in range(PAIRS):
        at = lanes_of(j)
        y = yl_ref[0, :, at] + reach[:, at] * from_state[:, at]
        y_ref[0, :, at] = y
        z = z_ref[0, :, at]
        gated = y * (z * jax.nn.sigmoid(z))
        square, pull = gated * gated, dn_ref[0, :, at] * gain_ref[0:1, at] * gated
        squares = square if j == 0 else squares + square
        pulled = pull if j == 0 else pulled + pull
    lane = lax.broadcasted_iota(jnp.int32, squares.shape, 1)
    squares = jnp.sum(squares, axis=1, keepdims=True)
    pulled = jnp.sum(pulled, axis=1, keepdims=True)
    both = jnp.where(lane == 0, squares, jnp.where(lane == 1, pulled, 0.0))
    first = pl.program_id(1) == 0

    @pl.when(first)
    def _():
        held[...] = both

    @pl.when(jnp.logical_not(first))
    def _():
        held[...] += both

    @pl.when(pl.program_id(1) == pl.num_programs(1) - 1)
    def _():
        sums_ref[0] = held[...].T[:8]


def gate_back_kernel(
    y_ref, z_ref, dn_ref, gain_ref, sums_ref, bc_ref, ct_ref, out_ref, dy_ref, dz_ref, pull_ref, gg_ref
):
    table = ct_ref[0, 0]
    chunks = table.shape[0] // GROUP
    sums = jnp.concatenate([sums_ref[0], jnp.zeros((120, table.shape[0]), F32)], axis=0).T
    r = lax.rsqrt(sums[:, 0:1] * (1.0 / INNER) + EPSILON)
    along_unit = r * (1.0 / INNER) * sums[:, 1:2]
    pulled = []
    reach = from_start(lane_wise(table, CARRY), chunks)
    for j in range(PAIRS):
        at = lanes_of(j)
        gain = gain_ref[0:1, at]
        y, z, dn = y_ref[0, :, at], z_ref[0, :, at], dn_ref[0, :, at]
        sig = jax.nn.sigmoid(z)
        silu = z * sig
        unit = y * silu * r
        out_ref[0, :, at] = (unit * gain).astype(BF)
        dg = r * (dn * gain - unit * along_unit)
        dy = dg * silu
        dy_ref[0, :, at] = dy
        dz_ref[0, : y.shape[0], at] = (dg * y * (sig * (1.0 + z * (1.0 - sig)))).astype(BF)
        dz_ref[0, y.shape[0] :, at] = jnp.zeros((HALO, 128), BF)
        pulled.append((reach[:, at] * dy).astype(BF))
        grad = jnp.sum(dn * unit, axis=0, keepdims=True)
        gg_ref[0, :, at] = jnp.broadcast_to(grad, (8, 128))
    pull_ref[0] = tn(bc_ref[0, :, STATE:], jnp.concatenate(pulled, axis=1))


def conv_back(d_conv, v, taps, same):
    rows, width = d_conv.shape
    pre = convolved(v, taps, same)
    sig = jax.nn.sigmoid(pre)
    d_pre = d_conv * (sig * (1.0 + pre * (1.0 - sig)))
    none = jnp.zeros((HALO, width), F32)
    d_v = jnp.concatenate([taps[CONV - 1 : CONV] * d_pre, none], axis=0)
    grads = [jnp.zeros((1, width), F32)] * 8
    grads[CONV - 1] = jnp.sum(d_pre * v[:rows], axis=0, keepdims=True)
    grads[CONV] = jnp.sum(d_pre, axis=0, keepdims=True)
    for k in range(1, CONV):
        kept = same[k - 1] * d_pre
        grads[CONV - 1 - k] = jnp.sum(kept * earlier_rows(v, k), axis=0, keepdims=True)
        moved = pltpu.roll(jnp.concatenate([kept, none], axis=0), rows + HALO - k, 0)
        d_v = d_v + taps[CONV - 1 - k : CONV - k] * moved
    return d_v.astype(BF), jnp.concatenate(grads, axis=0)


def mix_back_kernel(*refs, base, first, last):
    x_ref, bc_ref, dy_ref, inc_ref, adj_ref, ct_ref, rt_ref, skip_ref, xm_ref, tx_ref = refs[:10]
    at_ref = 10
    if not first:
        before_ref = refs[at_ref]
        at_ref += 1
    if last:
        bm_ref, cm_ref, dt_ref, tb_ref, par_ref = refs[at_ref : at_ref + 5]
    if last:
        d_ref, gx_ref, gs_ref, gb_ref, gh_ref = refs[-11:-6]
    else:
        d_ref, gx_ref, gs_ref, part_ref = refs[-10:-6]
    d_x, score_ref, mask_ref, d_score_ref, d_step_ref, cross_ref = refs[-6:]

    table = ct_ref[0, 0]
    chunks = x_ref.shape[1] // GROUP
    cross_ref[2 * PAIRS :] = jnp.zeros((8 - 2 * PAIRS, cross_ref.shape[1]), F32)
    down = lax.broadcasted_iota(jnp.int32, (GROUP, GROUP), 0)
    right = lax.broadcasted_iota(jnp.int32, (GROUP, GROUP), 1)
    before = (right < down).astype(BF)
    upto = (right >= down).astype(BF)
    upto_t, crossed = (down >= right).astype(BF), down < right
    same = same_columns(table)
    half = low_half(GROUP)
    head_of = lax.broadcasted_iota(jnp.int32, (WIDE, 128), 0) // HEADDIM + base
    pick = (head_of == lax.broadcasted_iota(jnp.int32, (WIDE, 128), 1)).astype(BF)

    carries = [lane_wise(table[rows_of(c)], CARRY) for c in range(chunks)]
    pulled = [carries[c] * dy_ref[0, rows_of(c), :] for c in range(chunks)]
    dts = [lane_wise(table[rows_of(c)], DT) for c in range(chunks)]
    xds = [x_ref[0, rows_of(c), :] * dts[c] for c in range(chunks)]
    endns = [lane_wise(table[rows_of(c)], ENDN) for c in range(chunks)]
    endings = [endns[c] * xds[c] for c in range(chunks)]
    states, adjoints = [inc_ref[0]], [adj_ref[0]]
    for c in range(chunks - 1):
        added = tn(bc_ref[0, rows_of(c), :STATE], endings[c].astype(BF))
        states.append(carries[c][GROUP - 1 :] * states[-1] + added)
    for c in range(chunks - 1, 0, -1):
        added = tn(bc_ref[0, rows_of(c), STATE:], pulled[c].astype(BF))
        adjoints.insert(0, carries[c][GROUP - 1 :] * adjoints[0] + added)

    d_keys, d_reads, all_logs, all_steps = [], [], [], []
    for c in range(chunks):
        rows = rows_of(c)
        keys, reads = bc_ref[0, rows, :STATE], bc_ref[0, rows, STATE:]
        state_b, adj_b = states[c].astype(BF), adjoints[c].astype(BF)
        from_state = pulled[c] * nn(reads, state_b)
        to_end = nn(keys, adj_b)
        whole = carries[c][GROUP - 1 :] * jnp.sum(states[c] * adjoints[c], axis=0, keepdims=True)
        logs = nn(upto, nn(from_state.astype(BF), pick).astype(BF))
        logs = logs + nn(before, nn((endings[c] * to_end).astype(BF), pick).astype(BF))
        logs = logs + nn(jnp.broadcast_to(whole, (8, WIDE)).astype(BF), pick)[:1]
        d_k, d_r = nt(endings[c].astype(BF), adj_b), nt(pulled[c].astype(BF), state_b)
        score = nt(keys, reads)
        mask = causal(table, rt_ref[0, SEG_ROW : SEG_ROW + 1, :], c, True)
        score_ref[...], mask_ref[...] = score, mask
        for j in range(PAIRS):
            at = lanes_of(j)
            dy = dy_ref[0, rows, at]
            dyb = dy.astype(BF)
            parts = halves_of(xds[c][:, at], half)
            crossings = [None, None]
            for top in range(0, GROUP, TILE):
                here, live = slice(top, top + TILE), slice(top // 128 * 128, GROUP)
                tile_rows = slice(c * GROUP + top, c * GROUP + top + TILE)
                scores = score_ref[here, live]
                weighted = nt(jnp.concatenate([parts[0][here], parts[1][here]], axis=0), dyb[live])
                decays = []
                for e in range(2):
                    h = 2 * j + e
                    row = rt_ref[0, base + h : base + h + 1, rows][:, live]
                    decays.append(jnp.exp(row - table[tile_rows, CUM + h : CUM + h + 1] + mask_ref[here, live]))
                weighted = [decays[0] * weighted[:TILE], decays[1] * weighted[TILE:]]
                d_scores = weighted[0] + weighted[1]
                mixing = jnp.concatenate([(scores * v).astype(BF) for v in decays], axis=0)
                d_xd = nn(mixing, dyb[live])
                d_xd = [d_xd[:TILE], d_xd[TILE:]]
                after_t = nn(jnp.concatenate([(scores * v).astype(BF) for v in weighted], axis=0), upto_t[live])
                for e in range(2):
                    mine = jnp.where(crossed[here], after_t[e * TILE : (e + 1) * TILE], 0.0)
                    crossing = jnp.sum(mine, axis=0, keepdims=True)
                    crossings[e] = crossing if top == 0 else crossings[e] + crossing
                if j == 0:
                    d_score_ref[here, live] = d_scores
                else:
                    d_score_ref[here, live] += d_scores
                u = jnp.where(half[:TILE], d_xd[0], d_xd[1]) + endns[c][here, at] * to_end[here, at]
                x = x_ref[0, tile_rows, at]
                d_x[tile_rows, at] = dts[c][here, at] * u + skip_ref[0:1, at] * dy[here]
                d_step_ref[here, at] = (x * u).astype(BF)
            for e in range(2):
                cross_ref[2 * j + e : 2 * j + e + 1, rows] = crossings[e]
        all_logs.append(logs)
        all_steps.append(nn(d_step_ref[...], pick))
        if GROUP > 128:
            d_score_ref[128:, :128] = jnp.zeros((GROUP - 128, 128), F32)
        ds = d_score_ref[...].astype(BF)
        d_keys.append(d_k + nn(ds, reads))
        d_reads.append(d_r + tn(ds, keys))
    turned = jnp.concatenate([cross_ref[...], jnp.zeros((120, cross_ref.shape[1]), F32)], axis=0).T
    turned = pltpu.roll(turned, base, 1) if base else turned
    all_logs = [v + turned[rows_of(c)] for c, v in enumerate(all_logs)]

    for j in range(PAIRS):
        at = lanes_of(j)
        grad = jnp.sum(dy_ref[0, :, at] * x_ref[0, :, at], axis=0, keepdims=True)
        gs_ref[0, :, at] = jnp.broadcast_to(grad, (8, 128))
        d_rows, grads = conv_back(d_x[:, at], rounded(xm_ref[0, :, at]), tx_ref[:, at], same)
        d_ref[0, :, at], gx_ref[0, :, at] = d_rows, grads

    state2 = 2 * STATE
    for i, d_rows in enumerate((d_keys, d_reads)):
        at = lanes_of(i)
        whole = jnp.concatenate(d_rows, axis=0)
        if not first:
            whole = whole + before_ref[0, :, at]
        if last:
            main_ref = (bm_ref, cm_ref)[i]
            d_rows, grads = conv_back(whole, rounded(main_ref[0]), tb_ref[:, at], same)
            d_ref[0, :, lanes_of(PAIRS + i)], gb_ref[0, :, at] = d_rows, grads
        else:
            part_ref[0, :, at] = whole
    logs, steps = jnp.concatenate(all_logs, axis=0), jnp.concatenate(all_steps, axis=0)
    if not first:
        logs = logs + before_ref[0, :, state2 : state2 + 128]
        steps = steps + before_ref[0, :, state2 + 128 :]
    if last:
        rows = logs.shape[0]
        v = dt_ref[0, :rows] + par_ref[0:1, :]
        step_dt = jnp.maximum(v, 0.0) + jnp.log1p(jnp.exp(-jnp.abs(v)))
        d_dt = (steps - par_ref[1:2, :] * logs) * jax.nn.sigmoid(v)
        d_ref[0, :rows, lanes_of(PAIRS + 2)] = d_dt.astype(BF)
        d_ref[0, rows:, lanes_of(PAIRS + 2)] = jnp.zeros((HALO, 128), BF)
        by_bias = jnp.sum(d_dt, axis=0, keepdims=True)
        by_log = -jnp.sum(par_ref[1:2, :] * step_dt * logs, axis=0, keepdims=True)
        gh_ref[0] = jnp.concatenate([by_log, by_bias, jnp.zeros((6, 128), F32)], axis=0)
    else:
        part_ref[0, :, state2 : state2 + 128] = logs
        part_ref[0, :, state2 + 128 :] = steps


def split_kernel(at_ref, v_ref, out_ref):
    out_ref[0] = v_ref[:, 0].astype(BF)


def split_both_kernel(at_ref, v_ref, w_ref, out_ref):
    groups, rows, cols = v_ref.shape[0], v_ref.shape[2], v_ref.shape[3]
    many = w_ref.shape[2]
    for g in range(groups):
        out_ref[0, g * rows : (g + 1) * rows, :cols] = v_ref[g, 0].astype(BF)
    for half in range(2):
        here = w_ref[0, 0, :, half * cols : (half + 1) * cols].astype(BF)
        out_ref[0, half * many : (half + 1) * many, cols:] = here


def shape(*dims, dtype=F32):
    return jax.ShapeDtypeStruct(dims, dtype)


def params(n=2, limit=48):
    return pltpu.CompilerParams(
        dimension_semantics=("arbitrary",) * n, vmem_limit_bytes=limit * 2**20
    )


def cost(flops, size, part=1):
    return pl.CostEstimate(flops=int(flops) // part, bytes_accessed=int(size) // part, transcendentals=0)


def on_device(
    tokens, segment_ids, in_proj, conv_weight, conv_bias, out_proj, norm_gain, gate_gain,
    a_log, dt_bias, skip_d, cotangent,
):
    n_x = lax.axis_size("x")
    na, nb = lax.axis_size("a"), lax.axis_size("b")
    groups, positions = 2 * n_x, na * nb
    me, place = group_of(0, 0), position_of(0, 0)
    index = me * positions + place
    rows, width = tokens.shape
    long = rows + HALO
    heads = HEADS // groups
    cols = heads * HEADDIM
    n_steps = heads // (2 * PAIRS)
    state2 = 2 * STATE
    early = cols - WIDE
    first_cols, all_cols = LAST + early, LAST + cols + early
    in_rows, out_rows = in_proj.shape[0], out_proj.shape[0]
    aligned = in_rows % 16 == 0 and width == 2 * cols and 2 * out_rows == groups * in_rows
    anywhere = pl.BlockSpec(memory_space=pl.ANY)

    small = jnp.concatenate([norm_gain, gate_gain, conv_bias, conv_weight.reshape(-1)])
    n_norm, n_gate, n_conv = norm_gain.shape[0], gate_gain.shape[0], conv_bias.shape[0]
    small = jnp.pad(small, (0, -small.shape[0] % 128))
    every = jnp.zeros((groups * positions, small.shape[0]), BF)
    every = lax.dynamic_update_slice_in_dim(every, small[None], index, 0)

    packed = pl.pallas_call(
        lambda *refs: pack_kernel(*refs, cols=cols, heads=heads),
        grid=(1,),
        in_specs=[pl.BlockSpec(in_proj.shape, lambda i: (0, 0))],
        out_specs=pl.BlockSpec((groups, in_rows, all_cols), lambda i: (0, 0, 0)),
        out_shape=shape(groups, in_rows, all_cols, dtype=BF),
        compiler_params=params(1),
        name="pack_weights",
    )(in_proj)
    held = exchange(packed, ("x", "core"))
    every = sum_over(every, ("a", "b", "x", "core"), [packed, packed, packed, held])
    block = held[:, :, :first_cols].reshape(-1, first_cols)
    first_over_a = [block] + [shift(block, "a", sa) for sa in range(1, na)]
    first_blocks = [v for here in first_over_a for v in gather_over_b(here)]

    ids_row = jnp.pad(segment_ids.astype(BF)[None], ((0, 15), (0, width - rows)))
    before = along(jnp.concatenate([tokens[rows - HALO :], ids_row], axis=0), 1)
    token_rows = jnp.concatenate([tokens, before[:HALO], ids_row[:8], before[HALO : HALO + 8]], axis=0)
    token_rows = gather_over_x(after(token_rows, every, held))
    slots = gather_over_cores(token_rows, *first_blocks)

    every = every.astype(F32)
    cuts = [n_norm, n_norm + n_gate, n_norm + n_gate + n_conv]
    gain_in = every[:, : cuts[0]].reshape(1, -1)
    gain_out = every[:, cuts[0] : cuts[1]].reshape(-1)
    bias_all = every[:, cuts[1] : cuts[2]].reshape(-1)
    taps_all = every[:, cuts[2] : cuts[2] + CONV * n_conv].reshape(-1, CONV, n_conv)
    taps_all = taps_all.transpose(1, 0, 2).reshape(CONV, XBC)
    conv_all = jnp.concatenate([taps_all, bias_all[None], jnp.zeros((3, XBC), F32)], axis=0)
    taps_x = lax.dynamic_slice_in_dim(conv_all, me * cols, cols, 1)
    taps_b = conv_all[:, INNER:]
    gain_g = jnp.broadcast_to(lax.dynamic_slice_in_dim(gain_out, me * cols, cols, 0), (8, cols))
    a_g = lax.dynamic_slice_in_dim(a_log, me * heads, heads, 0)
    bias_g = lax.dynamic_slice_in_dim(dt_bias, me * heads, heads, 0)
    skip_g = lax.dynamic_slice_in_dim(skip_d, me * heads, heads, 0)
    head_rows = jnp.pad(jnp.stack([bias_g, jnp.exp(a_g)]), ((0, 6), (0, 128 - heads)))
    skip_l = jnp.broadcast_to(jnp.repeat(skip_g, HEADDIM), (8, cols))

    tall = long // 3
    normed = pl.pallas_call(
        norm_kernel,
        grid=(long // tall,),
        in_specs=[pl.BlockSpec((tall, width), lambda i: (i, 0))] * groups
        + [pl.BlockSpec((8, width), lambda i: (0, 0))],
        out_specs=pl.BlockSpec((groups, tall, width), lambda i: (0, i, 0)),
        out_shape=shape(groups, long, width, dtype=BF),
        compiler_params=params(1),
        cost_estimate=cost(10 * groups * rows * width, 4 * groups * rows * width, 16),
        name="input_norm",
    )(*slots, jnp.broadcast_to(gain_in, (8, width)))
    ids = jnp.concatenate([s[long : long + 1, :rows] for s in slots], axis=0)
    halo_ids = jnp.concatenate([s[long + 8 : long + 9, rows - HALO : rows] for s in slots], axis=0)
    ids = jnp.concatenate([jnp.where(place == 0, jnp.asarray(-1, BF), halo_ids), ids], axis=1).astype(F32)
    seg = ids[:, HALO:]
    seg_rows = jnp.stack(
        [(ids[:, HALO - k : HALO - k + rows] == seg).astype(F32) for k in range(1, CONV)]
        + [seg, (seg == ids[:, HALO - 1 : HALO]).astype(F32)]
        + [jnp.zeros_like(seg)] * 3,
        axis=1,
    )

    b_behind = jnp.stack([lax.rem(lax.axis_index("b") - sb + nb, nb) for sb in range(nb)])
    behind = jnp.stack([position_of(-sa, -sb) for sa in range(na) for sb in range(nb)])

    def place_rows(blocks, moves, outs, at, *others):
        return pl.pallas_call(
            lambda *refs: place_kernel(*refs, moves=moves, n_in=len(blocks) + len(others)),
            grid_spec=pltpu.PrefetchScalarGridSpec(
                num_scalar_prefetch=1,
                grid=(1,),
                in_specs=[pl.BlockSpec(v.shape, lambda i, s: (0, 0)) for v in blocks]
                + [anywhere] * len(others),
                out_specs=[pl.BlockSpec(v.shape, lambda i, s: (0, 0)) for v in outs],
            ),
            out_shape=outs,
            compiler_params=params(1, 56),
            name="place_weights",
        )(at, *blocks, *others)

    def in_moves(source, target, own_lane, lane, wide, held_by, many):
        return [
            (
                source + sb, a * many + i * in_rows, own_lane,
                target, ((held_by + i) * positions + a * nb) * in_rows, sb, lane, in_rows, wide,
            )
            for sb in range(nb) for a in range(na) for i in range(min(groups, many // in_rows))
        ]

    def whole_rows(blocks, many, parts):
        out = jnp.zeros((parts, na, nb, many) + blocks[0].shape[-1:], BF)
        for sb in range(nb):
            v = blocks[sb].reshape(na, parts, many, -1).transpose(1, 0, 2, 3)[:, :, None]
            out = lax.dynamic_update_slice_in_dim(out, v, b_behind[sb], 2)
        return out.reshape(parts * positions * many, -1)

    def flat2(v):
        return v.reshape(-1, v.shape[-1])

    if aligned:
        moves = [
            (k, g * in_rows, 0, 0, g * positions * in_rows, k, 0, in_rows, first_cols)
            for k in range(positions) for g in range(groups)
        ]
        (w_first,) = place_rows(first_blocks, moves, [shape(width, first_cols, dtype=BF)], behind, normed)
    else:
        w_first = jnp.zeros((groups, positions, in_rows, first_cols), BF)
        for k in range(positions):
            v = first_blocks[k].reshape(groups, 1, in_rows, first_cols)
            w_first = lax.dynamic_update_slice_in_dim(w_first, v, behind[k], 1)
        w_first = w_first.reshape(width, first_cols)

    cot_rows = gather_over_x(after(cotangent, w_first))
    gate_block = held[:, :, first_cols:].reshape(-1, cols)
    if aligned:
        out_block = jnp.concatenate([out_proj[:, :cols], out_proj[:, cols:]], axis=0)
        gate_over_a = gather_over_a(after(gate_block, w_first))
    else:
        gate_over_a, out_over_a = gather_over_a(gate_block), gather_over_a(out_proj)

    normed_rows = normed.reshape(groups * long, width)
    proj = jnp.dot(normed_rows, w_first, preferred_element_type=F32).reshape(groups, long, first_cols)
    keys_at = WIDE // 128
    if aligned:
        gate_blocks = gather_over_b(gate_over_a)

    def step_tile(t):
        return jnp.where(t == n_steps - 1, 0, LAST // WIDE + t)

    def tile(count):
        return pl.BlockSpec((1, count, WIDE), lambda q, t: (q, 0, t))

    def narrow(at):
        return pl.BlockSpec((1, long, 128), lambda q, t: (q, 0, at))

    def per_seq(count, wide):
        return pl.BlockSpec((1, count, wide), lambda q, t: (q, 0, 0))

    def lanes(count):
        return pl.BlockSpec((count, WIDE), lambda q, t: (0, t))

    by_step = pl.BlockSpec((1, 1, rows, 128), lambda q, t: (q, t, 0, 0))
    all_taps = pl.BlockSpec((8, state2), lambda q, t: (0, 0))

    col_table, row_table = pl.pallas_call(
        lambda *refs: table_kernel(*refs, heads=heads),
        grid=(groups,),
        in_specs=[
            pl.BlockSpec((1, rows, 128), lambda q: (q, 0, keys_at + 2)),
            pl.BlockSpec((1, 8, rows), lambda q: (q, 0, 0)),
            pl.BlockSpec((8, 128), lambda q: (0, 0)),
        ],
        out_specs=[
            pl.BlockSpec((1, n_steps, rows, 128), lambda q: (q, 0, 0, 0)),
            pl.BlockSpec((1, SEG_ROW + 8, rows), lambda q: (q, 0, 0)),
        ],
        out_shape=[shape(groups, n_steps, rows, 128), shape(groups, SEG_ROW + 8, rows)],
        compiler_params=params(1),
        cost_estimate=cost(100 * groups * rows * 128, 16 * groups * rows * 128, 16),
        name="token_table",
    )(proj, seg_rows, head_rows)

    if aligned:
        out_block = after(out_block, w_first)
        out_over_a = jnp.stack([out_block] + [shift(out_block, "a", sa) for sa in range(1, na)])
    grid = (groups, n_steps)
    big = groups * rows * cols
    values_x, bc, own_state = pl.pallas_call(
        lambda *refs: conv_kernel(*refs[:6], *refs[-3:]),
        grid=grid,
        in_specs=[
            pl.BlockSpec((1, long, WIDE), lambda q, t: (q, 0, step_tile(t))),
            narrow(keys_at), narrow(keys_at + 1), lanes(8), all_taps, by_step,
        ],
        out_specs=[tile(rows), per_seq(rows, state2), tile(STATE)],
        out_shape=[
            shape(groups, rows, cols), shape(groups, rows, state2, dtype=BF), shape(groups, STATE, cols),
        ],
        compiler_params=params(),
        cost_estimate=cost(20 * big * STATE, 8 * big, 16),
        name="conv_and_state",
    )(proj, proj, proj, taps_x, taps_b, col_table)

    if aligned:
        out_blocks = gather_over_b(out_over_a)
    else:
        gate_blocks, out_blocks = gather_over_b(gate_over_a), gather_over_b(out_over_a)

    hops = -(-(LONGEST - 1) // rows)
    kept = col_table[:, :, GROUP - 1, CARRY : CARRY + 2 * PAIRS]
    for c in range(1, rows // GROUP):
        kept = kept * col_table[:, :, (c + 1) * GROUP - 1, CARRY : CARRY + 2 * PAIRS]
    device_decay = jnp.repeat(kept.reshape(groups, heads), HEADDIM, axis=-1)[:, None]

    def entering(own, sign):
        sent = jnp.concatenate(
            [own, jnp.broadcast_to(device_decay, (groups, 16, cols))], axis=1
        ).astype(BF)
        total_in, weight = None, None
        for hop in range(1, hops + 1):
            got = along(sent, sign * hop).astype(F32)
            state, decay = got[:, :STATE], got[:, STATE : STATE + 1]
            total_in = state if hop == 1 else total_in + weight * state
            weight = decay if hop == 1 else weight * decay
        return total_in

    incoming = entering(own_state, 1)

    mixed_local = pl.pallas_call(
        mix_kernel,
        grid=grid,
        in_specs=[tile(rows), per_seq(rows, state2), by_step, per_seq(SEG_ROW + 8, rows), lanes(8)],
        out_specs=tile(rows),
        out_shape=shape(groups, rows, cols),
        scratch_shapes=[pltpu.VMEM((rows // GROUP, GROUP, GROUP), F32)] * 2,
        compiler_params=params(),
        cost_estimate=cost(80 * big * GROUP, 8 * big, 16),
        name="mix_within_block",
    )(values_x, bc, col_table, row_table, skip_l)

    if aligned:
        many = groups * in_rows
        moves = in_moves(0, 0, 0, LAST, cols, 0, many)
        moves.append((nb, 0, 0, 0, 0, None, 0, width, LAST))
        moves.append((nb, 0, LAST, 0, 0, None, LAST + cols, width, early))
        blocks = [flat2(v) for v in gate_blocks] + [w_first]
        (w_all,) = place_rows(blocks, moves, [shape(width, all_cols, dtype=BF)], b_behind, mixed_local)
        moves = [
            (sb, sa * many + half * out_rows, 0, 0, 0, sa * nb + sb, half * cols, out_rows, cols)
            for sb in range(nb) for sa in range(na) for half in range(2)
        ]
        blocks = [flat2(v) for v in out_blocks]
        (w_out,) = place_rows(blocks, moves, [shape(cols, width, dtype=BF)], behind)
    else:
        w_out = whole_rows(out_blocks, out_rows, 1)
        w_gate = whole_rows(gate_blocks, in_rows, groups)
        w_all = jnp.concatenate([w_first[:, :LAST], w_gate, w_first[:, LAST:]], axis=1)

    cot = jnp.stack(gather_over_cores(cot_rows, mixed_local))
    gate_z = jnp.dot(normed_rows, w_all[:, LAST : LAST + cols], preferred_element_type=F32)
    gate_z = gate_z.reshape(groups, long, cols)
    d_normed = jnp.einsum("qtd,cd->qtc", cot, w_out, preferred_element_type=F32)

    mixed_y, sums = pl.pallas_call(
        gate_kernel,
        grid=grid,
        in_specs=[
            tile(rows), per_seq(rows, state2), tile(STATE), tile(rows), tile(rows), lanes(8), by_step,
        ],
        out_specs=[tile(rows), per_seq(8, rows)],
        out_shape=[shape(groups, rows, cols), shape(groups, 8, rows)],
        scratch_shapes=[pltpu.VMEM((rows, 128), F32)],
        compiler_params=params(),
        cost_estimate=cost(2 * big * STATE, 16 * big, 16),
        name="gate",
    )(mixed_local, bc, incoming, gate_z, d_normed, gain_g, col_table)
    sums = sum_over_group(sums)

    gate_tile = LAST // WIDE
    normed_out, d_y, d_all, pull, gate_sums = pl.pallas_call(
        gate_back_kernel,
        grid=grid,
        in_specs=[
            tile(rows), tile(rows), tile(rows), lanes(8), per_seq(8, rows), per_seq(rows, state2), by_step,
        ],
        out_specs=[
            tile(rows), tile(rows),
            pl.BlockSpec((1, long, WIDE), lambda q, t: (q, 0, gate_tile + t)), tile(STATE), tile(8),
        ],
        out_shape=[
            shape(groups, rows, cols, dtype=BF), shape(groups, rows, cols),
            shape(groups, long, all_cols, dtype=BF), shape(groups, STATE, cols), shape(groups, 8, cols),
        ],
        compiler_params=params(),
        cost_estimate=cost(2 * big * STATE, 20 * big),
        name="gate_back",
    )(mixed_y, gate_z, d_normed, gain_g, sums, bc, col_table)

    later = entering(pull, -1)

    ahead = jnp.stack([a * nb + lax.rem(lax.axis_index("b") + rb, nb) for rb in range(nb) for a in range(na)])

    def split(grad, many):
        shaped = grad.reshape(-1, positions, many, grad.shape[1])
        g, _, r, c = shaped.shape
        out = pl.pallas_call(
            split_kernel,
            grid_spec=pltpu.PrefetchScalarGridSpec(
                num_scalar_prefetch=1,
                grid=(positions,),
                in_specs=[pl.BlockSpec((g, 1, r, c), lambda k, at: (0, at[k], 0, 0))],
                out_specs=pl.BlockSpec((1, g, r, c), lambda k, at: (k, 0, 0, 0)),
            ),
            out_shape=shape(positions, g, r, c, dtype=BF),
            compiler_params=params(1),
            cost_estimate=cost(grad.size, 6 * grad.size),
            name="split_gradient",
        )(ahead, shaped)
        return out.reshape(nb, na, g, r, c)

    def split_both(grad, other):
        many = groups * in_rows
        return pl.pallas_call(
            split_both_kernel,
            grid_spec=pltpu.PrefetchScalarGridSpec(
                num_scalar_prefetch=1,
                grid=(positions,),
                in_specs=[
                    pl.BlockSpec((groups, 1, in_rows, cols), lambda k, at: (0, at[k], 0, 0)),
                    pl.BlockSpec((1, 1, out_rows, width), lambda k, at: (0, at[k], 0, 0)),
                ],
                out_specs=pl.BlockSpec((1, many, width), lambda k, at: (k, 0, 0)),
            ),
            out_shape=shape(positions, many, width, dtype=BF),
            compiler_params=params(1),
            cost_estimate=cost(2 * grad.size, 12 * grad.size),
            name="split_gradients",
        )(
            ahead, grad.reshape(groups, positions, in_rows, cols), other.reshape(1, positions, out_rows, width)
        ).reshape(nb, na, many, width)

    def grad_of(d_values, low, high):
        d_rows = d_values[:, :, low:high].reshape(groups * long, high - low)
        return jnp.dot(normed_rows.T, d_rows, preferred_element_type=F32)

    grad_out = jnp.einsum("qtc,qtd->cd", normed_out, cot, preferred_element_type=F32)
    grad_gate_cols = grad_of(d_all, LAST, LAST + cols)
    if aligned:
        weights_split = [split_both(grad_gate_cols, grad_out)]
    else:
        weights_split = [split(grad_gate_cols, in_rows), split(grad_out, out_rows)]
    by_core = normed_out.reshape(n_x, 2, rows, cols)
    w_out = after(w_out, weights_split[0])

    def outward(values):
        return jnp.einsum("qtc,cd->qtd", values, w_out, preferred_element_type=F32)

    out_sent = outward(by_core[:, 1])
    out_kept = outward(by_core[:, 0])

    d_parts, g_x, g_skip = None, [], []
    waits = list(weights_split)
    split_early = []
    for t in range(n_steps):
        first, last = t == 0, t == n_steps - 1

        def block(*dims, at=(0, 0)):
            return pl.BlockSpec((1,) + dims, lambda q, at=at: (q,) + at)

        def flat(*dims, at=(0, 0)):
            return pl.BlockSpec(dims, lambda q, at=at: at)

        tile_at = 0 if last else LAST // WIDE + t
        operands = [
            (values_x, block(rows, WIDE, at=(0, t))), (bc, block(rows, state2)),
            (d_y, block(rows, WIDE, at=(0, t))), (incoming, block(STATE, WIDE, at=(0, t))),
            (later, block(STATE, WIDE, at=(0, t))),
            (col_table, block(1, rows, 128, at=(t, 0, 0))), (row_table, block(SEG_ROW + 8, rows)),
            (skip_l, flat(8, WIDE, at=(0, t))), (proj, block(long, WIDE, at=(0, tile_at))),
            (taps_x, flat(8, WIDE, at=(0, t))),
        ]
        if not first:
            operands.append((d_parts, block(rows, 2 * state2)))
        if last:
            operands += [
                (proj, block(long, 128, at=(0, keys_at + i))) for i in range(3)
            ] + [(taps_b, flat(8, state2)), (head_rows, flat(8, 128))]
        used = len(operands)
        operands += [(d_all, anywhere)] + [(v, anywhere) for v in waits]
        d_tile = 0 if last else (LAST + cols) // WIDE + t
        made = [
            (block(long, LAST if last else WIDE, at=(0, d_tile)), d_all.shape, BF),
            (block(8, WIDE), (groups, 8, WIDE), F32), (block(8, WIDE), (groups, 8, WIDE), F32),
        ]
        if last:
            made += [
                (block(8, state2), (groups, 8, state2), F32), (block(8, 128), (groups, 8, 128), F32),
            ]
        else:
            made += [(block(rows, 2 * state2), (groups, rows, 2 * state2), F32)]

        def body(*refs, t=t, first=first, last=last, used=used, n_out=len(made)):
            mix_back_kernel(
                *refs[:used], *refs[-n_out - 6 :], base=2 * PAIRS * t, first=first, last=last
            )

        outs = pl.pallas_call(
            body,
            grid=(groups,),
            in_specs=[spec for _, spec in operands],
            out_specs=[spec for spec, _, _ in made],
            out_shape=[jax.ShapeDtypeStruct(s, d) for _, s, d in made],
            scratch_shapes=[pltpu.VMEM((rows, WIDE), F32)]
            + [pltpu.VMEM((GROUP, GROUP), F32)] * 3
            + [pltpu.VMEM((GROUP, WIDE), BF), pltpu.VMEM((8, rows), F32)],
            input_output_aliases={used: 0},
            compiler_params=params(1),
            cost_estimate=cost(100 * big * GROUP, 16 * big),
            name="mix_back",
        )(*[v for v, _ in operands])
        d_all = outs[0]
        g_x.append(outs[1])
        g_skip.append(outs[2])
        if last:
            g_b, g_head = outs[3:]
        else:
            d_parts = outs[3]
            low = LAST + cols + t * WIDE
            split_early.append(split(grad_of(d_all, low, low + WIDE), in_rows))
            if first:
                weight_sums = [sum_over_b(v) for v in weights_split]
                out_own, out_others = sum_over_cores(out_kept, out_sent)
            waits = [split_early[-1]] + weight_sums * first + out_others * first
    if n_steps == 1:
        weight_sums = [sum_over_b(v) for v in weights_split]
        out_own, out_others = sum_over_cores(out_kept, out_sent)

    weight_totals = [sum_over_a(v) for v in weight_sums]
    stream = tokens.astype(F32)
    output = (stream + sum_to_owner(out_own, out_others)).astype(BF)
    early_sums = [sum_over_b(v, d_all) for v in split_early]

    if aligned:
        gate_part = weight_totals[0][:, :cols].reshape(groups, in_rows, cols)
        both = weight_totals[0][:, cols:]
        grad_out_proj = jnp.concatenate([both[:out_rows], both[out_rows:]], axis=1)
    else:
        gate_part, grad_out_proj = weight_totals[0], weight_totals[1][0]

    def to_owners(v):
        return exchange(v.astype(BF), ("x", "core"))

    d_all = after(d_all, output, *weight_totals)
    spill = along(d_all[:, rows:], -1)
    grad_last = grad_of(d_all, 0, LAST)
    split_last = split(grad_last, in_rows)
    last_sum = sum_over_b(split_last)
    early_part = [sum_over_a(after(v, *weight_totals)) for v in early_sums]
    d_sent = after(d_all, split_last, spill, *early_part)
    end = d_sent[:, rows - HALO : rows] + spill
    d_sent = lax.dynamic_update_slice_in_dim(d_sent, end, rows - HALO, 1)
    early_part = to_owners(jnp.concatenate([gate_part] + early_part, axis=2))

    def inward(d_values, core, kind):
        d_by = d_values.reshape(n_x, 2, long, all_cols)[:, core]
        return jnp.einsum("qtc,dc->qtd", d_by, w_all, preferred_element_type=F32).astype(kind)

    in_sent = inward(d_sent, 1, BF)
    in_kept = inward(d_sent, 0, F32)
    in_own, in_both = sum_over_cores(in_kept, after(in_sent, last_sum, early_part))
    in_others = [shift(v, "x", -sx - 1) for sx, v in enumerate(in_both)]

    def by_rows(wide=width):
        return pl.BlockSpec((128, wide), lambda i: (i, 0))

    grad_tokens = pl.pallas_call(
        norm_back_kernel,
        grid=(rows // 128,),
        in_specs=[by_rows()] * (3 + len(in_others)) + [pl.BlockSpec((8, width), lambda i: (0, 0))],
        out_specs=by_rows(),
        out_shape=shape(rows, width),
        compiler_params=params(1),
        name="input_norm_back",
    )(tokens, cotangent, in_own, *in_others, jnp.broadcast_to(gain_in, (8, width)))

    pieces = [to_owners(sum_over_a(after(last_sum, in_kept, *in_both))), early_part]
    grad_in_proj, gain_products = pl.pallas_call(
        lambda *refs: unpack_kernel(*refs, cols=cols, heads=heads),
        grid=(1,),
        in_specs=[pl.BlockSpec(p.shape, lambda i: (0, 0, 0)) for p in pieces]
        + [pl.BlockSpec(in_proj.shape, lambda i: (0, 0))],
        out_specs=[
            pl.BlockSpec(in_proj.shape, lambda i: (0, 0)), pl.BlockSpec((in_rows, 128), lambda i: (0, 0)),
        ],
        out_shape=[shape(*in_proj.shape), shape(in_rows, 128)],
        compiler_params=params(1),
        name="unpack_gradient",
    )(*pieces, in_proj)
    grad_norm = gain_products[:, 0] / norm_gain.astype(F32)

    def placed(v):
        out = jnp.zeros((groups,) + v.shape, F32)
        return lax.dynamic_update_slice_in_dim(out, v[None], me, 0)

    g_x = jnp.sum(jnp.concatenate(g_x, axis=2), axis=0)[: CONV + 1]
    g_b = jnp.sum(g_b, axis=0)[: CONV + 1]
    g_skip = jnp.sum(jnp.concatenate([g[:, 0] for g in g_skip], axis=1), axis=0)
    grad_skip_g = jnp.sum(g_skip.reshape(1, heads, HEADDIM), axis=2)
    g_head = jnp.sum(g_head, axis=0)[:2, :heads]
    pieces = [
        placed(g_x), g_b, placed(jnp.sum(gate_sums[:, 0], axis=0)),
        placed(jnp.concatenate([g_head, grad_skip_g], axis=0)),
    ]
    flat = jnp.concatenate([p.reshape(-1) for p in pieces])
    count = flat.shape[0]
    flat = jnp.pad(flat, (0, -count % 1024)).reshape(-1, 128)
    marks = [grad_last, split_last, in_sent, in_kept, in_own]
    flat = sum_over(flat, ("x", "a", "b", "core"), marks).reshape(-1)
    at, back = 0, []
    for p in pieces:
        back.append(flat[at : at + p.size].reshape(p.shape))
        at += p.size
    conv_x, conv_b, gate_all, head_all = back
    conv_sum = jnp.concatenate([conv_x.transpose(1, 0, 2).reshape(CONV + 1, INNER), conv_b], axis=1)
    conv_own = lax.dynamic_slice_in_dim(conv_sum, index * n_conv, n_conv, 1)
    grad_gate = lax.dynamic_slice_in_dim(gate_all.reshape(-1), index * n_gate, n_gate, 0)
    head_all = head_all.transpose(1, 0, 2).reshape(3, HEADS)
    return (
        output, grad_tokens, grad_in_proj, conv_own[:CONV], conv_own[CONV], grad_out_proj,
        grad_norm, grad_gate, head_all[0], head_all[1], head_all[2],
    )


def solution(mesh):
    n_dp, n_seq = mesh.shape["dp"], mesh.shape["seq"]
    slow = 4 if n_seq % 4 == 0 else 1
    finer = Mesh(
        mesh.devices.reshape(n_dp // 2, 2, slow, n_seq // slow), ("x", "core", "a", "b")
    )
    every = ("x", "core", "a", "b")
    rows, flat, second, copied = P(every, None), P(every), P(None, every), P()
    in_specs = (rows, flat, rows, second, flat, rows, flat, flat, copied, copied, copied, rows)
    out_specs = (rows, rows, rows, second, flat, rows, flat, flat, copied, copied, copied)
    return jax.shard_map(
        on_device, mesh=finer, in_specs=in_specs, out_specs=out_specs, check_vma=False
    )
```

```python
import jax
import jax.numpy as jnp
from jax import lax
from jax.experimental import pallas as pl
from jax.experimental.pallas import tpu as pltpu
from jax.sharding import Mesh
from jax.sharding import PartitionSpec as P

INNER = 3072
HEADDIM = 64
STATE = 128
CONV = 4
GROUP = 256
HEADS = 48
XBC = 3328
LONGEST = 1024
HALO = 16
TILE = 128
PAIRS = 3
WIDE = PAIRS * 128
LAST = WIDE + 3 * 128

EPSILON = 1e-05
BF = jnp.bfloat16
F32 = jnp.float32
NEVER = -1e30

CUM, DT, CARRY, ENDN, SAME, SEG = 0, 16, 32, 48, 64, 67
SEG_ROW = 16


def shift(v, axis, step):
    n = lax.axis_size(axis)
    return lax.ppermute(v, axis, [(i, (i + step) % n) for i in range(n)])


def along(v, step):
    n = lax.axis_size("a") * lax.axis_size("b")
    route = [(i, i + step) for i in range(n) if 0 <= i + step < n]
    return lax.ppermute(v, ("a", "b"), route)


def exchange(v, axes):
    return lax.all_to_all(v, axes, 0, 0, tiled=True)


def group_of(sx, sc):
    x, c, n = lax.axis_index("x"), lax.axis_index("core"), lax.axis_size("x")
    return lax.rem(x + sx + n, n) * 2 + (c + sc) % 2


def position_of(sa, sb):
    na, nb = lax.axis_size("a"), lax.axis_size("b")
    a, b = lax.axis_index("a"), lax.axis_index("b")
    return lax.rem(a + sa + na, na) * nb + lax.rem(b + sb + nb, nb)


def after(v, *others):
    def nothing(*refs):
        pass

    anywhere = pl.BlockSpec(memory_space=pl.ANY)
    return pl.pallas_call(
        nothing,
        in_specs=[anywhere] * (1 + len(others)),
        out_specs=anywhere,
        out_shape=jax.ShapeDtypeStruct(v.shape, v.dtype),
        input_output_aliases={0: 0},
        name="in_order",
    )(v, *others)


def gather_over_x(v):
    return [v] + [shift(v, "x", sx) for sx in range(1, lax.axis_size("x"))]


def gather_over_cores(along_x, *others):
    slots = []
    for sx, here in enumerate(along_x):
        here = after(here, *others) if sx else here
        slots += [here, shift(here, "core", 1)]
    return slots


def sum_over_cores(kept, sent):
    both = kept + shift(sent.astype(BF), "core", 1).astype(F32)
    return both[0], [both[sx].astype(BF) for sx in range(1, lax.axis_size("x"))]


def sum_to_owner(own, others):
    total = own
    for sx in range(1, lax.axis_size("x")):
        total = total + shift(others[sx - 1], "x", -sx).astype(F32)
    return total


def sum_over_group(v):
    n = lax.axis_size("x")
    v = v.reshape((n, 2) + v.shape[1:])
    v = v + shift(v, "core", 1)[:, ::-1]
    total = v
    for step in range(1, n):
        total = total + jnp.roll(shift(v, "x", step), step, axis=0)
    return total.reshape((n * 2,) + v.shape[2:])


def gather_over_a(block):
    return exchange(jnp.broadcast_to(block[None], (lax.axis_size("a"),) + block.shape), "a")


def gather_over_b(v):
    return [v] + [shift(v, "b", sb) for sb in range(1, lax.axis_size("b"))]


def sum_over_b(parts, *others):
    total = (after(parts[0], *others) if others else parts[0]).astype(F32)
    for rb in range(1, lax.axis_size("b")):
        total = total + shift(parts[rb], "b", rb).astype(F32)
    return total.astype(BF)


def sum_over_a(parts):
    return jnp.sum(exchange(parts, "a").astype(F32), axis=0)


def sum_over(v, axes, marks=()):
    marks = list(marks)
    for axis in axes:
        step, n = 1, lax.axis_size(axis)
        while step < n:
            moved = lax.ppermute(v, axis, [(i, i ^ step) for i in range(n)])
            v = (after(v, marks.pop(0)) if marks else v) + moved
            step *= 2
    return v


def nn(a, b):
    return lax.dot_general(a, b, (((1,), (0,)), ((), ())), preferred_element_type=F32)


def nt(a, b):
    return lax.dot_general(a, b, (((1,), (1,)), ((), ())), preferred_element_type=F32)


def tn(a, b):
    return lax.dot_general(a, b, (((0,), (0,)), ((), ())), preferred_element_type=F32)


def low_half(rows):
    return lax.broadcasted_iota(jnp.int32, (rows, 128), 1) < HEADDIM


def spread(table, kind, pair):
    at = kind + 2 * pair
    return jnp.where(low_half(table.shape[0]), table[:, at : at + 1], table[:, at + 1 : at + 2])


def lane_wise(table, kind):
    high = table.astype(BF)
    low = (table - high.astype(F32)).astype(BF)
    head_of = lax.broadcasted_iota(jnp.int32, (128, WIDE), 1) // HEADDIM + kind
    pick = (head_of == lax.broadcasted_iota(jnp.int32, (128, WIDE), 0)).astype(BF)
    return nn(jnp.concatenate([high, low], axis=1), jnp.concatenate([pick, pick], axis=0))


def lanes_of(pair):
    return slice(pair * 128, (pair + 1) * 128)


def rows_of(chunk):
    return slice(chunk * GROUP, (chunk + 1) * GROUP)


def end_of(chunk):
    return slice((chunk + 1) * GROUP - 1, (chunk + 1) * GROUP)


def from_start(carry, chunks):
    out, run = [carry[rows_of(0)]], carry[end_of(0)]
    for c in range(1, chunks):
        out.append(carry[rows_of(c)] * run)
        run = run * carry[end_of(c)]
    return jnp.concatenate(out, axis=0)


def to_block_end(endn, table, chunks):
    out, run = [endn[rows_of(chunks - 1)]], None
    for c in range(chunks - 2, -1, -1):
        keep = lane_wise(table[(c + 2) * GROUP - 8 : (c + 2) * GROUP], CARRY)[7:]
        run = keep if run is None else run * keep
        out.insert(0, endn[rows_of(c)] * run)
    return jnp.concatenate(out, axis=0)


def earlier_rows(v, k):
    return pltpu.roll(v, k, 0)[: v.shape[0] - HALO]


def convolved(v, taps, same):
    rows = v.shape[0] - HALO
    pre = taps[CONV : CONV + 1] + taps[CONV - 1 : CONV] * v[:rows]
    for k in range(1, CONV):
        pre = pre + same[k - 1] * (taps[CONV - 1 - k : CONV - k] * earlier_rows(v, k))
    return pre


def rounded(v):
    return v.astype(BF).astype(F32)


def same_columns(table):
    rows = table.shape[0]
    return [
        jnp.broadcast_to(table[:, SAME + k : SAME + k + 1], (rows, 128)) for k in range(CONV - 1)
    ]


def pack_kernel(weight_ref, first_ref, cols, heads):
    state2 = 2 * STATE
    rows = weight_ref.shape[0]
    steps = weight_ref[:, INNER + XBC :].astype(F32)
    steps = jnp.concatenate([steps, jnp.zeros((rows, 128 - steps.shape[1]), F32)], axis=1)
    lane = lax.broadcasted_iota(jnp.int32, (rows, 128), 1)
    for r in range(first_ref.shape[0]):
        at, early = r * cols, cols - WIDE
        tail = INNER + at + early
        first_ref[r, :, :WIDE] = weight_ref[:, tail : tail + WIDE]
        first_ref[r, :, WIDE : WIDE + state2] = weight_ref[:, 2 * INNER : INNER + XBC]
        mine = pltpu.roll(steps, (128 - r * heads) % 128, 1)
        first_ref[r, :, WIDE + state2 : LAST] = jnp.where(lane < heads, mine, 0.0).astype(BF)
        if early:
            first_ref[r, :, LAST : LAST + early] = weight_ref[:, INNER + at : INNER + at + early]
        first_ref[r, :, LAST + early :] = weight_ref[:, at : at + cols]


def unpack_kernel(last_ref, early_ref, weight_ref, out_ref, gain_ref, cols, heads):
    state2 = 2 * STATE
    shared, steps = None, None
    lane = lax.broadcasted_iota(jnp.int32, (out_ref.shape[0], 128), 1)
    for r in range(last_ref.shape[0]):
        at, early = r * cols, cols - WIDE
        tail = INNER + at + early
        out_ref[:, at : at + cols] = early_ref[r, :, :cols].astype(F32)
        out_ref[:, tail : tail + WIDE] = last_ref[r, :, :WIDE].astype(F32)
        if early:
            out_ref[:, INNER + at : tail] = early_ref[r, :, cols:].astype(F32)
        both = last_ref[r, :, WIDE : WIDE + state2].astype(F32)
        shared = both if shared is None else shared + both
        step = jnp.where(lane < heads, last_ref[r, :, WIDE + state2 :].astype(F32), 0.0)
        step = pltpu.roll(step, r * heads, 1) if r else step
        steps = step if steps is None else steps + step
    out_ref[:, 2 * INNER : INNER + XBC] = shared
    out_ref[:, INNER + XBC :] = steps[:, : out_ref.shape[1] - INNER - XBC]
    products = out_ref[...] * weight_ref[...].astype(F32)
    gain_ref[...] = jnp.broadcast_to(jnp.sum(products, axis=1, keepdims=True), gain_ref.shape)


def place_kernel(at_ref, *refs, moves, n_in):
    for source, row, lane, target, to, more, to_lane, count, wide in moves:
        if more is not None:
            to = pl.multiple_of(to + at_ref[more] * count, 16)
        piece = refs[source][row : row + count, lane : lane + wide]
        refs[n_in + target][pl.ds(to, count), to_lane : to_lane + wide] = piece


def norm_kernel(*refs):
    gain_ref, out_ref = refs[-2], refs[-1]
    for r in range(len(refs) - 2):
        v = refs[r][...].astype(F32)
        scale = lax.rsqrt(jnp.mean(v * v, axis=-1, keepdims=True) + EPSILON)
        out_ref[r] = (v * scale * gain_ref[0:1, :]).astype(BF)


def norm_back_kernel(tokens_ref, cot_ref, *refs):
    gain_ref, out_ref = refs[-2], refs[-1]
    total = refs[0][...]
    for ref in refs[1:-2]:
        total = total + ref[...].astype(F32)
    inner = total * gain_ref[0:1, :]
    v = tokens_ref[...].astype(F32)
    r = lax.rsqrt(jnp.mean(v * v, axis=-1, keepdims=True) + EPSILON)
    pull = r * r * jnp.mean(inner * v, axis=-1, keepdims=True)
    out_ref[...] = cot_ref[...].astype(F32) + r * (inner - v * pull)


def table_kernel(dt_ref, seg_ref, par_ref, ct_ref, rt_ref, heads):
    rows = dt_ref.shape[1]
    chunks = rows // GROUP
    lane = lax.broadcasted_iota(jnp.int32, (rows, 128), 1)
    v = dt_ref[0] + par_ref[0:1, :]
    step = jnp.where(lane < heads, jnp.maximum(v, 0.0) + jnp.log1p(jnp.exp(-jnp.abs(v))), 0.0)
    decay = -par_ref[1:2, :] * step
    aux = jnp.concatenate([seg_ref[0], jnp.zeros((120, rows), F32)], axis=0).T
    seg, entering = aux[:, 3:4], aux[:, 4:5]
    cums, carries, ends = [], [], []
    for c in range(chunks):
        cum = decay[rows_of(c)]
        step_rows = 1
        while step_rows < GROUP:
            cum = cum + jnp.concatenate(
                [jnp.zeros((step_rows, 128), F32), cum[: GROUP - step_rows]], axis=0
            )
            step_rows *= 2
        here = seg[rows_of(c)]
        held = entering[rows_of(0)] > 0.5 if c == 0 else here == seg[end_of(c - 1)]
        cums.append(cum)
        carries.append(jnp.where(held, jnp.exp(cum), 0.0))
        ends.append(jnp.where(here == seg[end_of(c)], jnp.exp(cum[GROUP - 1 :] - cum), 0.0))
    kept = lane < heads
    cum = jnp.concatenate(cums, axis=0)
    carry = jnp.where(kept, jnp.concatenate(carries, axis=0), 0.0)
    endn = jnp.where(kept, jnp.concatenate(ends, axis=0), 0.0)
    whole = cum + pltpu.roll(step, DT, 1) + pltpu.roll(carry, CARRY, 1) + pltpu.roll(endn, ENDN, 1)
    aux = pltpu.roll(jnp.where(lane < 4, aux, 0.0), SAME, 1)
    for t in range(ct_ref.shape[1]):
        mine = whole if t == 0 else pltpu.roll(whole, 128 - 2 * PAIRS * t, 1)
        ct_ref[0, t] = jnp.where((lane >= SAME) & (lane < SAME + 4), aux, mine)
    rt_ref[0, :SEG_ROW] = cum.T[:SEG_ROW]
    rt_ref[0, SEG_ROW:] = jnp.broadcast_to(seg_ref[0, 3:4, :], (8, rows))


def conv_kernel(xm_ref, bm_ref, cm_ref, tx_ref, tb_ref, ct_ref, x_ref, bc_ref, own_ref):
    table = ct_ref[0, 0]
    chunks = table.shape[0] // GROUP
    same = same_columns(table)

    @pl.when(pl.program_id(1) == 0)
    def _():
        for i, main in enumerate((bm_ref, cm_ref)):
            pre = convolved(rounded(main[0]), tb_ref[:, lanes_of(i)], same)
            bc_ref[0, :, lanes_of(i)] = (pre * jax.nn.sigmoid(pre)).astype(BF)

    weighted = []
    left = to_block_end(lane_wise(table, ENDN), table, chunks) * lane_wise(table, DT)
    for j in range(PAIRS):
        at = lanes_of(j)
        pre = convolved(rounded(xm_ref[0, :, at]), tx_ref[:, at], same)
        x = pre * jax.nn.sigmoid(pre)
        x_ref[0, :, at] = x
        weighted.append((left[:, at] * x).astype(BF))
    own_ref[0] = tn(bc_ref[0, :, :STATE], jnp.concatenate(weighted, axis=1))


def causal(table, segrow, chunk, transposed):
    seg_c = table[rows_of(chunk), SEG : SEG + 1]
    seg_r = segrow[:, rows_of(chunk)]
    down = lax.broadcasted_iota(jnp.int32, (GROUP, GROUP), 0)
    right = lax.broadcasted_iota(jnp.int32, (GROUP, GROUP), 1)
    order = (down <= right) if transposed else (down >= right)
    return jnp.where((seg_c == seg_r) & order, 0.0, NEVER)


def halves_of(v, half):
    return [jnp.where(half, v, 0.0).astype(BF), jnp.where(half, 0.0, v).astype(BF)]


def mix_kernel(x_ref, bc_ref, ct_ref, rt_ref, skip_ref, y_ref, score, mask):
    table = ct_ref[0, 0]
    chunks = x_ref.shape[1] // GROUP
    base = pl.program_id(1) * (2 * PAIRS)

    @pl.when(pl.program_id(1) == 0)
    def _():
        for c in range(chunks):
            score[c] = nt(bc_ref[0, rows_of(c), STATE:], bc_ref[0, rows_of(c), :STATE])
            mask[c] = causal(table, rt_ref[0, SEG_ROW : SEG_ROW + 1, :], c, False)

    dts, endns = lane_wise(table, DT), lane_wise(table, ENDN)
    carries = [lane_wise(table[rows_of(c)], CARRY) for c in range(1, chunks)]
    states = None
    for c in range(chunks):
        rows = rows_of(c)
        x = x_ref[0, rows, :]
        xd = x * dts[rows]
        xdb = xd.astype(BF)
        y_in = skip_ref[0:1, :] * x
        if c:
            y_in = y_in + carries[c - 1] * nn(bc_ref[0, rows, STATE:], states.astype(BF))
        if c + 1 < chunks:
            added = tn(bc_ref[0, rows, :STATE], (endns[rows] * xd).astype(BF))
            states = added if c == 0 else carries[c - 1][GROUP - 1 :] * states + added
        for j in range(PAIRS):
            at = lanes_of(j)
            cum_rows = [rt_ref[0, pl.ds(base + 2 * j + e, 1), :] for e in range(2)]
            for top in range(0, GROUP, TILE):
                here, live = slice(top, top + TILE), slice(0, top + TILE)
                tile_rows = slice(c * GROUP + top, c * GROUP + top + TILE)
                scores, masks = score[c, here, live], mask[c, here, live]
                mixing = []
                for e in range(2):
                    h = 2 * j + e
                    row = cum_rows[e][:, c * GROUP : c * GROUP + top + TILE]
                    decay = jnp.exp(table[tile_rows, CUM + h : CUM + h + 1] - row + masks)
                    mixing.append((scores * decay).astype(BF))
                y = nn(jnp.concatenate(mixing, axis=0), xdb[live, at])
                y_ref[0, tile_rows, at] = y_in[here, at] + jnp.where(low_half(TILE), y[:TILE], y[TILE:])


def gate_kernel(yl_ref, bc_ref, inc_ref, z_ref, dn_ref, gain_ref, ct_ref, y_ref, sums_ref, held):
    table = ct_ref[0, 0]
    chunks = table.shape[0] // GROUP
    from_state = nn(bc_ref[0, :, STATE:], inc_ref[0].astype(BF))
    squares, pulled = None, None
    reach = from_start(lane_wise(table, CARRY), chunks)
    for j in range(PAIRS):
        at = lanes_of(j)
        y = yl_ref[0, :, at] + reach[:, at] * from_state[:, at]
        y_ref[0, :, at] = y
        z = z_ref[0, :, at]
        gated = y * (z * jax.nn.sigmoid(z))
        square, pull = gated * gated, dn_ref[0, :, at] * gain_ref[0:1, at] * gated
        squares = square if j == 0 else squares + square
        pulled = pull if j == 0 else pulled + pull
    lane = lax.broadcasted_iota(jnp.int32, squares.shape, 1)
    squares = jnp.sum(squares, axis=1, keepdims=True)
    pulled = jnp.sum(pulled, axis=1, keepdims=True)
    both = jnp.where(lane == 0, squares, jnp.where(lane == 1, pulled, 0.0))
    first = pl.program_id(1) == 0

    @pl.when(first)
    def _():
        held[...] = both

    @pl.when(jnp.logical_not(first))
    def _():
        held[...] += both

    @pl.when(pl.program_id(1) == pl.num_programs(1) - 1)
    def _():
        sums_ref[0] = held[...].T[:8]


def gate_back_kernel(
    y_ref, z_ref, dn_ref, gain_ref, sums_ref, bc_ref, ct_ref, out_ref, dy_ref, dz_ref, pull_ref, gg_ref
):
    table = ct_ref[0, 0]
    chunks = table.shape[0] // GROUP
    sums = jnp.concatenate([sums_ref[0], jnp.zeros((120, table.shape[0]), F32)], axis=0).T
    r = lax.rsqrt(sums[:, 0:1] * (1.0 / INNER) + EPSILON)
    along_unit = r * (1.0 / INNER) * sums[:, 1:2]
    pulled = []
    reach = from_start(lane_wise(table, CARRY), chunks)
    for j in range(PAIRS):
        at = lanes_of(j)
        gain = gain_ref[0:1, at]
        y, z, dn = y_ref[0, :, at], z_ref[0, :, at], dn_ref[0, :, at]
        sig = jax.nn.sigmoid(z)
        silu = z * sig
        unit = y * silu * r
        out_ref[0, :, at] = (unit * gain).astype(BF)
        dg = r * (dn * gain - unit * along_unit)
        dy = dg * silu
        dy_ref[0, :, at] = dy
        dz_ref[0, : y.shape[0], at] = (dg * y * (sig * (1.0 + z * (1.0 - sig)))).astype(BF)
        dz_ref[0, y.shape[0] :, at] = jnp.zeros((HALO, 128), BF)
        pulled.append((reach[:, at] * dy).astype(BF))
        grad = jnp.sum(dn * unit, axis=0, keepdims=True)
        gg_ref[0, :, at] = jnp.broadcast_to(grad, (8, 128))
    pull_ref[0] = tn(bc_ref[0, :, STATE:], jnp.concatenate(pulled, axis=1))


def conv_back(d_conv, v, taps, same):
    rows, width = d_conv.shape
    pre = convolved(v, taps, same)
    sig = jax.nn.sigmoid(pre)
    d_pre = d_conv * (sig * (1.0 + pre * (1.0 - sig)))
    none = jnp.zeros((HALO, width), F32)
    d_v = jnp.concatenate([taps[CONV - 1 : CONV] * d_pre, none], axis=0)
    grads = [jnp.zeros((1, width), F32)] * 8
    grads[CONV - 1] = jnp.sum(d_pre * v[:rows], axis=0, keepdims=True)
    grads[CONV] = jnp.sum(d_pre, axis=0, keepdims=True)
    for k in range(1, CONV):
        kept = same[k - 1] * d_pre
        grads[CONV - 1 - k] = jnp.sum(kept * earlier_rows(v, k), axis=0, keepdims=True)
        moved = pltpu.roll(jnp.concatenate([kept, none], axis=0), rows + HALO - k, 0)
        d_v = d_v + taps[CONV - 1 - k : CONV - k] * moved
    return d_v.astype(BF), jnp.concatenate(grads, axis=0)


def mix_back_kernel(*refs, base, first, last):
    x_ref, bc_ref, dy_ref, inc_ref, adj_ref, ct_ref, rt_ref, skip_ref, xm_ref, tx_ref = refs[:10]
    at_ref = 10
    if not first:
        before_ref = refs[at_ref]
        at_ref += 1
    if last:
        bm_ref, cm_ref, dt_ref, tb_ref, par_ref = refs[at_ref : at_ref + 5]
    if last:
        d_ref, gx_ref, gs_ref, gb_ref, gh_ref = refs[-11:-6]
    else:
        d_ref, gx_ref, gs_ref, part_ref = refs[-10:-6]
    d_x, score_ref, mask_ref, d_score_ref, d_step_ref, cross_ref = refs[-6:]

    table = ct_ref[0, 0]
    chunks = x_ref.shape[1] // GROUP
    cross_ref[2 * PAIRS :] = jnp.zeros((8 - 2 * PAIRS, cross_ref.shape[1]), F32)
    down = lax.broadcasted_iota(jnp.int32, (GROUP, GROUP), 0)
    right = lax.broadcasted_iota(jnp.int32, (GROUP, GROUP), 1)
    before = (right < down).astype(BF)
    upto = (right >= down).astype(BF)
    upto_t, crossed = (down >= right).astype(BF), down < right
    same = same_columns(table)
    half = low_half(GROUP)
    head_of = lax.broadcasted_iota(jnp.int32, (WIDE, 128), 0) // HEADDIM + base
    pick = (head_of == lax.broadcasted_iota(jnp.int32, (WIDE, 128), 1)).astype(BF)

    carries = [lane_wise(table[rows_of(c)], CARRY) for c in range(chunks)]
    pulled = [carries[c] * dy_ref[0, rows_of(c), :] for c in range(chunks)]
    dts = [lane_wise(table[rows_of(c)], DT) for c in range(chunks)]
    xds = [x_ref[0, rows_of(c), :] * dts[c] for c in range(chunks)]
    endns = [lane_wise(table[rows_of(c)], ENDN) for c in range(chunks)]
    endings = [endns[c] * xds[c] for c in range(chunks)]
    states, adjoints = [inc_ref[0]], [adj_ref[0]]
    for c in range(chunks - 1):
        added = tn(bc_ref[0, rows_of(c), :STATE], endings[c].astype(BF))
        states.append(carries[c][GROUP - 1 :] * states[-1] + added)
    for c in range(chunks - 1, 0, -1):
        added = tn(bc_ref[0, rows_of(c), STATE:], pulled[c].astype(BF))
        adjoints.insert(0, carries[c][GROUP - 1 :] * adjoints[0] + added)

    d_keys, d_reads, all_logs, all_steps = [], [], [], []
    for c in range(chunks):
        rows = rows_of(c)
        keys, reads = bc_ref[0, rows, :STATE], bc_ref[0, rows, STATE:]
        state_b, adj_b = states[c].astype(BF), adjoints[c].astype(BF)
        from_state = pulled[c] * nn(reads, state_b)
        to_end = nn(keys, adj_b)
        whole = carries[c][GROUP - 1 :] * jnp.sum(states[c] * adjoints[c], axis=0, keepdims=True)
        logs = nn(upto, nn(from_state.astype(BF), pick).astype(BF))
        logs = logs + nn(before, nn((endings[c] * to_end).astype(BF), pick).astype(BF))
        logs = logs + nn(jnp.broadcast_to(whole, (8, WIDE)).astype(BF), pick)[:1]
        d_k, d_r = nt(endings[c].astype(BF), adj_b), nt(pulled[c].astype(BF), state_b)
        score = nt(keys, reads)
        mask = causal(table, rt_ref[0, SEG_ROW : SEG_ROW + 1, :], c, True)
        score_ref[...], mask_ref[...] = score, mask
        for j in range(PAIRS):
            at = lanes_of(j)
            dy = dy_ref[0, rows, at]
            dyb = dy.astype(BF)
            parts = halves_of(xds[c][:, at], half)
            crossings = [None, None]
            for top in range(0, GROUP, TILE):
                here, live = slice(top, top + TILE), slice(top // 128 * 128, GROUP)
                tile_rows = slice(c * GROUP + top, c * GROUP + top + TILE)
                scores = score_ref[here, live]
                weighted = nt(jnp.concatenate([parts[0][here], parts[1][here]], axis=0), dyb[live])
                decays = []
                for e in range(2):
                    h = 2 * j + e
                    row = rt_ref[0, base + h : base + h + 1, rows][:, live]
                    decays.append(jnp.exp(row - table[tile_rows, CUM + h : CUM + h + 1] + mask_ref[here, live]))
                weighted = [decays[0] * weighted[:TILE], decays[1] * weighted[TILE:]]
                d_scores = weighted[0] + weighted[1]
                mixing = jnp.concatenate([(scores * v).astype(BF) for v in decays], axis=0)
                d_xd = nn(mixing, dyb[live])
                d_xd = [d_xd[:TILE], d_xd[TILE:]]
                after_t = nn(jnp.concatenate([(scores * v).astype(BF) for v in weighted], axis=0), upto_t[live])
                for e in range(2):
                    mine = jnp.where(crossed[here], after_t[e * TILE : (e + 1) * TILE], 0.0)
                    crossing = jnp.sum(mine, axis=0, keepdims=True)
                    crossings[e] = crossing if top == 0 else crossings[e] + crossing
                if j == 0:
                    d_score_ref[here, live] = d_scores
                else:
                    d_score_ref[here, live] += d_scores
                u = jnp.where(half[:TILE], d_xd[0], d_xd[1]) + endns[c][here, at] * to_end[here, at]
                x = x_ref[0, tile_rows, at]
                d_x[tile_rows, at] = dts[c][here, at] * u + skip_ref[0:1, at] * dy[here]
                d_step_ref[here, at] = (x * u).astype(BF)
            for e in range(2):
                cross_ref[2 * j + e : 2 * j + e + 1, rows] = crossings[e]
        all_logs.append(logs)
        all_steps.append(nn(d_step_ref[...], pick))
        if GROUP > 128:
            d_score_ref[128:, :128] = jnp.zeros((GROUP - 128, 128), F32)
        ds = d_score_ref[...].astype(BF)
        d_keys.append(d_k + nn(ds, reads))
        d_reads.append(d_r + tn(ds, keys))
    turned = jnp.concatenate([cross_ref[...], jnp.zeros((120, cross_ref.shape[1]), F32)], axis=0).T
    turned = pltpu.roll(turned, base, 1) if base else turned
    all_logs = [v + turned[rows_of(c)] for c, v in enumerate(all_logs)]

    for j in range(PAIRS):
        at = lanes_of(j)
        grad = jnp.sum(dy_ref[0, :, at] * x_ref[0, :, at], axis=0, keepdims=True)
        gs_ref[0, :, at] = jnp.broadcast_to(grad, (8, 128))
        d_rows, grads = conv_back(d_x[:, at], rounded(xm_ref[0, :, at]), tx_ref[:, at], same)
        d_ref[0, :, at], gx_ref[0, :, at] = d_rows, grads

    state2 = 2 * STATE
    for i, d_rows in enumerate((d_keys, d_reads)):
        at = lanes_of(i)
        whole = jnp.concatenate(d_rows, axis=0)
        if not first:
            whole = whole + before_ref[0, :, at]
        if last:
            main_ref = (bm_ref, cm_ref)[i]
            d_rows, grads = conv_back(whole, rounded(main_ref[0]), tb_ref[:, at], same)
            d_ref[0, :, lanes_of(PAIRS + i)], gb_ref[0, :, at] = d_rows, grads
        else:
            part_ref[0, :, at] = whole
    logs, steps = jnp.concatenate(all_logs, axis=0), jnp.concatenate(all_steps, axis=0)
    if not first:
        logs = logs + before_ref[0, :, state2 : state2 + 128]
        steps = steps + before_ref[0, :, state2 + 128 :]
    if last:
        rows = logs.shape[0]
        v = dt_ref[0, :rows] + par_ref[0:1, :]
        step_dt = jnp.maximum(v, 0.0) + jnp.log1p(jnp.exp(-jnp.abs(v)))
        d_dt = (steps - par_ref[1:2, :] * logs) * jax.nn.sigmoid(v)
        d_ref[0, :rows, lanes_of(PAIRS + 2)] = d_dt.astype(BF)
        d_ref[0, rows:, lanes_of(PAIRS + 2)] = jnp.zeros((HALO, 128), BF)
        by_bias = jnp.sum(d_dt, axis=0, keepdims=True)
        by_log = -jnp.sum(par_ref[1:2, :] * step_dt * logs, axis=0, keepdims=True)
        gh_ref[0] = jnp.concatenate([by_log, by_bias, jnp.zeros((6, 128), F32)], axis=0)
    else:
        part_ref[0, :, state2 : state2 + 128] = logs
        part_ref[0, :, state2 + 128 :] = steps


def split_kernel(at_ref, v_ref, out_ref):
    out_ref[0] = v_ref[:, 0].astype(BF)


def split_both_kernel(at_ref, v_ref, w_ref, out_ref):
    groups, rows, cols = v_ref.shape[0], v_ref.shape[2], v_ref.shape[3]
    many = w_ref.shape[2]
    for g in range(groups):
        out_ref[0, g * rows : (g + 1) * rows, :cols] = v_ref[g, 0].astype(BF)
    for half in range(2):
        here = w_ref[0, 0, :, half * cols : (half + 1) * cols].astype(BF)
        out_ref[0, half * many : (half + 1) * many, cols:] = here


def shape(*dims, dtype=F32):
    return jax.ShapeDtypeStruct(dims, dtype)


def params(n=2, limit=48):
    return pltpu.CompilerParams(
        dimension_semantics=("arbitrary",) * n, vmem_limit_bytes=limit * 2**20
    )


def cost(flops, size, part=1):
    return pl.CostEstimate(flops=int(flops) // part, bytes_accessed=int(size) // part, transcendentals=0)


def on_device(
    tokens, segment_ids, in_proj, conv_weight, conv_bias, out_proj, norm_gain, gate_gain,
    a_log, dt_bias, skip_d, cotangent,
):
    n_x = lax.axis_size("x")
    na, nb = lax.axis_size("a"), lax.axis_size("b")
    groups, positions = 2 * n_x, na * nb
    me, place = group_of(0, 0), position_of(0, 0)
    index = me * positions + place
    rows, width = tokens.shape
    long = rows + HALO
    heads = HEADS // groups
    cols = heads * HEADDIM
    n_steps = heads // (2 * PAIRS)
    state2 = 2 * STATE
    early = cols - WIDE
    first_cols, all_cols = LAST + early, LAST + cols + early
    in_rows, out_rows = in_proj.shape[0], out_proj.shape[0]
    aligned = in_rows % 16 == 0 and width == 2 * cols and 2 * out_rows == groups * in_rows
    anywhere = pl.BlockSpec(memory_space=pl.ANY)

    small = jnp.concatenate([norm_gain, gate_gain, conv_bias, conv_weight.reshape(-1)])
    n_norm, n_gate, n_conv = norm_gain.shape[0], gate_gain.shape[0], conv_bias.shape[0]
    small = jnp.pad(small, (0, -small.shape[0] % 128))
    every = jnp.zeros((groups * positions, small.shape[0]), BF)
    every = lax.dynamic_update_slice_in_dim(every, small[None], index, 0)

    packed = pl.pallas_call(
        lambda *refs: pack_kernel(*refs, cols=cols, heads=heads),
        grid=(1,),
        in_specs=[pl.BlockSpec(in_proj.shape, lambda i: (0, 0))],
        out_specs=pl.BlockSpec((groups, in_rows, all_cols), lambda i: (0, 0, 0)),
        out_shape=shape(groups, in_rows, all_cols, dtype=BF),
        compiler_params=params(1),
        name="pack_weights",
    )(in_proj)
    held = exchange(packed, ("x", "core"))
    every = sum_over(every, ("a", "b", "x", "core"), [packed, packed, packed, held])
    block = held[:, :, :first_cols].reshape(-1, first_cols)
    first_over_a = [block] + [shift(block, "a", sa) for sa in range(1, na)]
    first_blocks = [v for here in first_over_a for v in gather_over_b(here)]

    ids_row = jnp.pad(segment_ids.astype(BF)[None], ((0, 15), (0, width - rows)))
    before = along(jnp.concatenate([tokens[rows - HALO :], ids_row], axis=0), 1)
    token_rows = jnp.concatenate([tokens, before[:HALO], ids_row[:8], before[HALO : HALO + 8]], axis=0)
    token_rows = gather_over_x(after(token_rows, every, held))
    slots = gather_over_cores(token_rows, *first_blocks)

    every = every.astype(F32)
    cuts = [n_norm, n_norm + n_gate, n_norm + n_gate + n_conv]
    gain_in = every[:, : cuts[0]].reshape(1, -1)
    gain_out = every[:, cuts[0] : cuts[1]].reshape(-1)
    bias_all = every[:, cuts[1] : cuts[2]].reshape(-1)
    taps_all = every[:, cuts[2] : cuts[2] + CONV * n_conv].reshape(-1, CONV, n_conv)
    taps_all = taps_all.transpose(1, 0, 2).reshape(CONV, XBC)
    conv_all = jnp.concatenate([taps_all, bias_all[None], jnp.zeros((3, XBC), F32)], axis=0)
    taps_x = lax.dynamic_slice_in_dim(conv_all, me * cols, cols, 1)
    taps_b = conv_all[:, INNER:]
    gain_g = jnp.broadcast_to(lax.dynamic_slice_in_dim(gain_out, me * cols, cols, 0), (8, cols))
    a_g = lax.dynamic_slice_in_dim(a_log, me * heads, heads, 0)
    bias_g = lax.dynamic_slice_in_dim(dt_bias, me * heads, heads, 0)
    skip_g = lax.dynamic_slice_in_dim(skip_d, me * heads, heads, 0)
    head_rows = jnp.pad(jnp.stack([bias_g, jnp.exp(a_g)]), ((0, 6), (0, 128 - heads)))
    skip_l = jnp.broadcast_to(jnp.repeat(skip_g, HEADDIM), (8, cols))

    tall = long // 3
    normed = pl.pallas_call(
        norm_kernel,
        grid=(long // tall,),
        in_specs=[pl.BlockSpec((tall, width), lambda i: (i, 0))] * groups
        + [pl.BlockSpec((8, width), lambda i: (0, 0))],
        out_specs=pl.BlockSpec((groups, tall, width), lambda i: (0, i, 0)),
        out_shape=shape(groups, long, width, dtype=BF),
        compiler_params=params(1),
        cost_estimate=cost(10 * groups * rows * width, 4 * groups * rows * width, 16),
        name="input_norm",
    )(*slots, jnp.broadcast_to(gain_in, (8, width)))
    ids = jnp.concatenate([s[long : long + 1, :rows] for s in slots], axis=0)
    halo_ids = jnp.concatenate([s[long + 8 : long + 9, rows - HALO : rows] for s in slots], axis=0)
    ids = jnp.concatenate([jnp.where(place == 0, jnp.asarray(-1, BF), halo_ids), ids], axis=1).astype(F32)
    seg = ids[:, HALO:]
    seg_rows = jnp.stack(
        [(ids[:, HALO - k : HALO - k + rows] == seg).astype(F32) for k in range(1, CONV)]
        + [seg, (seg == ids[:, HALO - 1 : HALO]).astype(F32)]
        + [jnp.zeros_like(seg)] * 3,
        axis=1,
    )

    b_behind = jnp.stack([lax.rem(lax.axis_index("b") - sb + nb, nb) for sb in range(nb)])
    behind = jnp.stack([position_of(-sa, -sb) for sa in range(na) for sb in range(nb)])

    def place_rows(blocks, moves, outs, at, *others):
        return pl.pallas_call(
            lambda *refs: place_kernel(*refs, moves=moves, n_in=len(blocks) + len(others)),
            grid_spec=pltpu.PrefetchScalarGridSpec(
                num_scalar_prefetch=1,
                grid=(1,),
                in_specs=[pl.BlockSpec(v.shape, lambda i, s: (0, 0)) for v in blocks]
                + [anywhere] * len(others),
                out_specs=[pl.BlockSpec(v.shape, lambda i, s: (0, 0)) for v in outs],
            ),
            out_shape=outs,
            compiler_params=params(1, 56),
            name="place_weights",
        )(at, *blocks, *others)

    def in_moves(source, target, own_lane, lane, wide, held_by, many):
        return [
            (
                source + sb, a * many + i * in_rows, own_lane,
                target, ((held_by + i) * positions + a * nb) * in_rows, sb, lane, in_rows, wide,
            )
            for sb in range(nb) for a in range(na) for i in range(min(groups, many // in_rows))
        ]

    def whole_rows(blocks, many, parts):
        out = jnp.zeros((parts, na, nb, many) + blocks[0].shape[-1:], BF)
        for sb in range(nb):
            v = blocks[sb].reshape(na, parts, many, -1).transpose(1, 0, 2, 3)[:, :, None]
            out = lax.dynamic_update_slice_in_dim(out, v, b_behind[sb], 2)
        return out.reshape(parts * positions * many, -1)

    def flat2(v):
        return v.reshape(-1, v.shape[-1])

    if aligned:
        moves = [
            (k, g * in_rows, 0, 0, g * positions * in_rows, k, 0, in_rows, first_cols)
            for k in range(positions) for g in range(groups)
        ]
        (w_first,) = place_rows(first_blocks, moves, [shape(width, first_cols, dtype=BF)], behind, normed)
    else:
        w_first = jnp.zeros((groups, positions, in_rows, first_cols), BF)
        for k in range(positions):
            v = first_blocks[k].reshape(groups, 1, in_rows, first_cols)
            w_first = lax.dynamic_update_slice_in_dim(w_first, v, behind[k], 1)
        w_first = w_first.reshape(width, first_cols)

    cot_rows = gather_over_x(after(cotangent, w_first))
    gate_block = held[:, :, first_cols:].reshape(-1, cols)
    if aligned:
        out_block = jnp.concatenate([out_proj[:, :cols], out_proj[:, cols:]], axis=0)
        gate_over_a = gather_over_a(after(gate_block, *first_blocks))
    else:
        gate_over_a, out_over_a = gather_over_a(gate_block), gather_over_a(out_proj)

    normed_rows = normed.reshape(groups * long, width)
    proj = jnp.dot(normed_rows, w_first, preferred_element_type=F32).reshape(groups, long, first_cols)
    keys_at = WIDE // 128

    def step_tile(t):
        return jnp.where(t == n_steps - 1, 0, LAST // WIDE + t)

    def tile(count):
        return pl.BlockSpec((1, count, WIDE), lambda q, t: (q, 0, t))

    def narrow(at):
        return pl.BlockSpec((1, long, 128), lambda q, t: (q, 0, at))

    def per_seq(count, wide):
        return pl.BlockSpec((1, count, wide), lambda q, t: (q, 0, 0))

    def lanes(count):
        return pl.BlockSpec((count, WIDE), lambda q, t: (0, t))

    by_step = pl.BlockSpec((1, 1, rows, 128), lambda q, t: (q, t, 0, 0))
    all_taps = pl.BlockSpec((8, state2), lambda q, t: (0, 0))

    col_table, row_table = pl.pallas_call(
        lambda *refs: table_kernel(*refs, heads=heads),
        grid=(groups,),
        in_specs=[
            pl.BlockSpec((1, rows, 128), lambda q: (q, 0, keys_at + 2)),
            pl.BlockSpec((1, 8, rows), lambda q: (q, 0, 0)),
            pl.BlockSpec((8, 128), lambda q: (0, 0)),
        ],
        out_specs=[
            pl.BlockSpec((1, n_steps, rows, 128), lambda q: (q, 0, 0, 0)),
            pl.BlockSpec((1, SEG_ROW + 8, rows), lambda q: (q, 0, 0)),
        ],
        out_shape=[shape(groups, n_steps, rows, 128), shape(groups, SEG_ROW + 8, rows)],
        compiler_params=params(1),
        cost_estimate=cost(100 * groups * rows * 128, 16 * groups * rows * 128, 16),
        name="token_table",
    )(proj, seg_rows, head_rows)

    if aligned:
        out_block = after(out_block, *first_blocks)
        out_over_a = [shift(out_block, "a", sa) for sa in range(1, na)]
        out_over_a = jnp.stack([out_block] + [after(v, col_table) for v in out_over_a])
    grid = (groups, n_steps)
    big = groups * rows * cols
    values_x, bc, own_state = pl.pallas_call(
        lambda *refs: conv_kernel(*refs[:6], *refs[-3:]),
        grid=grid,
        in_specs=[
            pl.BlockSpec((1, long, WIDE), lambda q, t: (q, 0, step_tile(t))),
            narrow(keys_at), narrow(keys_at + 1), lanes(8), all_taps, by_step,
        ],
        out_specs=[tile(rows), per_seq(rows, state2), tile(STATE)],
        out_shape=[
            shape(groups, rows, cols), shape(groups, rows, state2, dtype=BF), shape(groups, STATE, cols),
        ],
        compiler_params=params(),
        cost_estimate=cost(20 * big * STATE, 8 * big, 16),
        name="conv_and_state",
    )(proj, proj, proj, taps_x, taps_b, col_table)

    if aligned:
        out_blocks = gather_over_b(out_over_a)
        gate_blocks = gather_over_b(after(gate_over_a, col_table))
    else:
        gate_blocks, out_blocks = gather_over_b(gate_over_a), gather_over_b(out_over_a)

    hops = -(-(LONGEST - 1) // rows)
    kept = col_table[:, :, GROUP - 1, CARRY : CARRY + 2 * PAIRS]
    for c in range(1, rows // GROUP):
        kept = kept * col_table[:, :, (c + 1) * GROUP - 1, CARRY : CARRY + 2 * PAIRS]
    device_decay = jnp.repeat(kept.reshape(groups, heads), HEADDIM, axis=-1)[:, None]

    def entering(own, sign):
        sent = jnp.concatenate(
            [own, jnp.broadcast_to(device_decay, (groups, 16, cols))], axis=1
        ).astype(BF)
        total_in, weight = None, None
        for hop in range(1, hops + 1):
            got = along(sent, sign * hop).astype(F32)
            state, decay = got[:, :STATE], got[:, STATE : STATE + 1]
            total_in = state if hop == 1 else total_in + weight * state
            weight = decay if hop == 1 else weight * decay
        return total_in

    incoming = entering(own_state, 1)

    mixed_local = pl.pallas_call(
        lambda *refs: mix_kernel(*refs[:5], *refs[6:]),
        grid=grid,
        in_specs=[
            tile(rows), per_seq(rows, state2), by_step, per_seq(SEG_ROW + 8, rows), lanes(8), anywhere,
        ],
        out_specs=tile(rows),
        out_shape=shape(groups, rows, cols),
        scratch_shapes=[pltpu.VMEM((rows // GROUP, GROUP, GROUP), F32)] * 2,
        compiler_params=params(),
        cost_estimate=cost(80 * big * GROUP, 8 * big, 16),
        name="mix_within_block",
    )(values_x, bc, col_table, row_table, skip_l, out_blocks[-1])

    if aligned:
        many = groups * in_rows
        moves = in_moves(0, 0, 0, LAST, cols, 0, many)
        moves.append((nb, 0, 0, 0, 0, None, 0, width, LAST))
        moves.append((nb, 0, LAST, 0, 0, None, LAST + cols, width, early))
        blocks = [flat2(v) for v in gate_blocks] + [w_first]
        (w_all,) = place_rows(blocks, moves, [shape(width, all_cols, dtype=BF)], b_behind, mixed_local)
        moves = [
            (sb, sa * many + half * out_rows, 0, 0, 0, sa * nb + sb, half * cols, out_rows, cols)
            for sb in range(nb) for sa in range(na) for half in range(2)
        ]
        blocks = [flat2(v) for v in out_blocks]
        (w_out,) = place_rows(blocks, moves, [shape(cols, width, dtype=BF)], behind)
    else:
        w_out = whole_rows(out_blocks, out_rows, 1)
        w_gate = whole_rows(gate_blocks, in_rows, groups)
        w_all = jnp.concatenate([w_first[:, :LAST], w_gate, w_first[:, LAST:]], axis=1)

    cot = jnp.stack(gather_over_cores(cot_rows, mixed_local))
    gate_z = jnp.dot(normed_rows, w_all[:, LAST : LAST + cols], preferred_element_type=F32)
    gate_z = gate_z.reshape(groups, long, cols)
    d_normed = jnp.einsum("qtd,cd->qtc", cot, w_out, preferred_element_type=F32)

    mixed_y, sums = pl.pallas_call(
        gate_kernel,
        grid=grid,
        in_specs=[
            tile(rows), per_seq(rows, state2), tile(STATE), tile(rows), tile(rows), lanes(8), by_step,
        ],
        out_specs=[tile(rows), per_seq(8, rows)],
        out_shape=[shape(groups, rows, cols), shape(groups, 8, rows)],
        scratch_shapes=[pltpu.VMEM((rows, 128), F32)],
        compiler_params=params(),
        cost_estimate=cost(2 * big * STATE, 16 * big, 16),
        name="gate",
    )(mixed_local, bc, incoming, gate_z, d_normed, gain_g, col_table)
    sums = sum_over_group(sums)

    gate_tile = LAST // WIDE
    normed_out, d_y, d_all, pull, gate_sums = pl.pallas_call(
        gate_back_kernel,
        grid=grid,
        in_specs=[
            tile(rows), tile(rows), tile(rows), lanes(8), per_seq(8, rows), per_seq(rows, state2), by_step,
        ],
        out_specs=[
            tile(rows), tile(rows),
            pl.BlockSpec((1, long, WIDE), lambda q, t: (q, 0, gate_tile + t)), tile(STATE), tile(8),
        ],
        out_shape=[
            shape(groups, rows, cols, dtype=BF), shape(groups, rows, cols),
            shape(groups, long, all_cols, dtype=BF), shape(groups, STATE, cols), shape(groups, 8, cols),
        ],
        compiler_params=params(),
        cost_estimate=cost(2 * big * STATE, 20 * big),
        name="gate_back",
    )(mixed_y, gate_z, d_normed, gain_g, sums, bc, col_table)

    later = entering(pull, -1)

    ahead = jnp.stack([a * nb + lax.rem(lax.axis_index("b") + rb, nb) for rb in range(nb) for a in range(na)])

    def split(grad, many):
        shaped = grad.reshape(-1, positions, many, grad.shape[1])
        g, _, r, c = shaped.shape
        out = pl.pallas_call(
            split_kernel,
            grid_spec=pltpu.PrefetchScalarGridSpec(
                num_scalar_prefetch=1,
                grid=(positions,),
                in_specs=[pl.BlockSpec((g, 1, r, c), lambda k, at: (0, at[k], 0, 0))],
                out_specs=pl.BlockSpec((1, g, r, c), lambda k, at: (k, 0, 0, 0)),
            ),
            out_shape=shape(positions, g, r, c, dtype=BF),
            compiler_params=params(1),
            cost_estimate=cost(grad.size, 6 * grad.size),
            name="split_gradient",
        )(ahead, shaped)
        return out.reshape(nb, na, g, r, c)

    def split_both(grad, other):
        many = groups * in_rows
        return pl.pallas_call(
            split_both_kernel,
            grid_spec=pltpu.PrefetchScalarGridSpec(
                num_scalar_prefetch=1,
                grid=(positions,),
                in_specs=[
                    pl.BlockSpec((groups, 1, in_rows, cols), lambda k, at: (0, at[k], 0, 0)),
                    pl.BlockSpec((1, 1, out_rows, width), lambda k, at: (0, at[k], 0, 0)),
                ],
                out_specs=pl.BlockSpec((1, many, width), lambda k, at: (k, 0, 0)),
            ),
            out_shape=shape(positions, many, width, dtype=BF),
            compiler_params=params(1),
            cost_estimate=cost(2 * grad.size, 12 * grad.size),
            name="split_gradients",
        )(
            ahead, grad.reshape(groups, positions, in_rows, cols), other.reshape(1, positions, out_rows, width)
        ).reshape(nb, na, many, width)

    def grad_of(d_values, low, high):
        d_rows = d_values[:, :, low:high].reshape(groups * long, high - low)
        return jnp.dot(normed_rows.T, d_rows, preferred_element_type=F32)

    grad_out = jnp.einsum("qtc,qtd->cd", normed_out, cot, preferred_element_type=F32)
    grad_gate_cols = grad_of(d_all, LAST, LAST + cols)
    if aligned:
        weights_split = [split_both(grad_gate_cols, grad_out)]
    else:
        weights_split = [split(grad_gate_cols, in_rows), split(grad_out, out_rows)]
    by_core = normed_out.reshape(n_x, 2, rows, cols)
    w_out = after(w_out, weights_split[0])

    def outward(values):
        return jnp.einsum("qtc,cd->qtd", values, w_out, preferred_element_type=F32)

    out_sent = outward(by_core[:, 1])
    out_kept = outward(by_core[:, 0])

    d_parts, g_x, g_skip = None, [], []
    waits = list(weights_split)
    split_early = []
    for t in range(n_steps):
        first, last = t == 0, t == n_steps - 1

        def block(*dims, at=(0, 0)):
            return pl.BlockSpec((1,) + dims, lambda q, at=at: (q,) + at)

        def flat(*dims, at=(0, 0)):
            return pl.BlockSpec(dims, lambda q, at=at: at)

        tile_at = 0 if last else LAST // WIDE + t
        operands = [
            (values_x, block(rows, WIDE, at=(0, t))), (bc, block(rows, state2)),
            (d_y, block(rows, WIDE, at=(0, t))), (incoming, block(STATE, WIDE, at=(0, t))),
            (later, block(STATE, WIDE, at=(0, t))),
            (col_table, block(1, rows, 128, at=(t, 0, 0))), (row_table, block(SEG_ROW + 8, rows)),
            (skip_l, flat(8, WIDE, at=(0, t))), (proj, block(long, WIDE, at=(0, tile_at))),
            (taps_x, flat(8, WIDE, at=(0, t))),
        ]
        if not first:
            operands.append((d_parts, block(rows, 2 * state2)))
        if last:
            operands += [
                (proj, block(long, 128, at=(0, keys_at + i))) for i in range(3)
            ] + [(taps_b, flat(8, state2)), (head_rows, flat(8, 128))]
        used = len(operands)
        operands += [(d_all, anywhere)] + [(v, anywhere) for v in waits]
        d_tile = 0 if last else (LAST + cols) // WIDE + t
        made = [
            (block(long, LAST if last else WIDE, at=(0, d_tile)), d_all.shape, BF),
            (block(8, WIDE), (groups, 8, WIDE), F32), (block(8, WIDE), (groups, 8, WIDE), F32),
        ]
        if last:
            made += [
                (block(8, state2), (groups, 8, state2), F32), (block(8, 128), (groups, 8, 128), F32),
            ]
        else:
            made += [(block(rows, 2 * state2), (groups, rows, 2 * state2), F32)]

        def body(*refs, t=t, first=first, last=last, used=used, n_out=len(made)):
            mix_back_kernel(
                *refs[:used], *refs[-n_out - 6 :], base=2 * PAIRS * t, first=first, last=last
            )

        outs = pl.pallas_call(
            body,
            grid=(groups,),
            in_specs=[spec for _, spec in operands],
            out_specs=[spec for spec, _, _ in made],
            out_shape=[jax.ShapeDtypeStruct(s, d) for _, s, d in made],
            scratch_shapes=[pltpu.VMEM((rows, WIDE), F32)]
            + [pltpu.VMEM((GROUP, GROUP), F32)] * 3
            + [pltpu.VMEM((GROUP, WIDE), BF), pltpu.VMEM((8, rows), F32)],
            input_output_aliases={used: 0},
            compiler_params=params(1),
            cost_estimate=cost(100 * big * GROUP, 16 * big),
            name="mix_back",
        )(*[v for v, _ in operands])
        d_all = outs[0]
        g_x.append(outs[1])
        g_skip.append(outs[2])
        if last:
            g_b, g_head = outs[3:]
        else:
            d_parts = outs[3]
            low = LAST + cols + t * WIDE
            split_early.append(split(grad_of(d_all, low, low + WIDE), in_rows))
            if first:
                weight_sums = [sum_over_b(v) for v in weights_split]
                out_own, out_others = sum_over_cores(out_kept, out_sent)
            waits = [split_early[-1]] + weight_sums * first + out_others * first
    if n_steps == 1:
        weight_sums = [sum_over_b(v) for v in weights_split]
        out_own, out_others = sum_over_cores(out_kept, out_sent)

    weight_totals = [sum_over_a(v) for v in weight_sums]
    stream = tokens.astype(F32)
    output = (stream + sum_to_owner(out_own, out_others)).astype(BF)
    early_sums = [sum_over_b(v, d_all) for v in split_early]

    if aligned:
        gate_part = weight_totals[0][:, :cols].reshape(groups, in_rows, cols)
        both = weight_totals[0][:, cols:]
        grad_out_proj = jnp.concatenate([both[:out_rows], both[out_rows:]], axis=1)
    else:
        gate_part, grad_out_proj = weight_totals[0], weight_totals[1][0]

    def to_owners(v):
        return exchange(v.astype(BF), ("x", "core"))

    d_all = after(d_all, output, *weight_totals)
    spill = along(d_all[:, rows:], -1)
    grad_last = grad_of(d_all, 0, LAST)
    split_last = split(grad_last, in_rows)
    last_sum = sum_over_b(split_last)
    early_part = [sum_over_a(after(v, *weight_totals)) for v in early_sums]
    d_sent = after(d_all, split_last, spill, *early_part)
    end = d_sent[:, rows - HALO : rows] + spill
    d_sent = lax.dynamic_update_slice_in_dim(d_sent, end, rows - HALO, 1)
    early_part = to_owners(jnp.concatenate([gate_part] + early_part, axis=2))

    def inward(d_values, core, kind):
        d_by = d_values.reshape(n_x, 2, long, all_cols)[:, core]
        return jnp.einsum("qtc,dc->qtd", d_by, w_all, preferred_element_type=F32).astype(kind)

    in_sent = inward(d_sent, 1, BF)
    in_kept = inward(d_sent, 0, F32)
    in_own, in_both = sum_over_cores(in_kept, after(in_sent, last_sum, early_part))
    in_others = [shift(v, "x", -sx - 1) for sx, v in enumerate(in_both)]

    def by_rows(wide=width):
        return pl.BlockSpec((128, wide), lambda i: (i, 0))

    grad_tokens = pl.pallas_call(
        norm_back_kernel,
        grid=(rows // 128,),
        in_specs=[by_rows()] * (3 + len(in_others)) + [pl.BlockSpec((8, width), lambda i: (0, 0))],
        out_specs=by_rows(),
        out_shape=shape(rows, width),
        compiler_params=params(1),
        name="input_norm_back",
    )(tokens, cotangent, in_own, *in_others, jnp.broadcast_to(gain_in, (8, width)))

    pieces = [to_owners(sum_over_a(after(last_sum, in_kept, *in_both))), early_part]
    grad_in_proj, gain_products = pl.pallas_call(
        lambda *refs: unpack_kernel(*refs, cols=cols, heads=heads),
        grid=(1,),
        in_specs=[pl.BlockSpec(p.shape, lambda i: (0, 0, 0)) for p in pieces]
        + [pl.BlockSpec(in_proj.shape, lambda i: (0, 0))],
        out_specs=[
            pl.BlockSpec(in_proj.shape, lambda i: (0, 0)), pl.BlockSpec((in_rows, 128), lambda i: (0, 0)),
        ],
        out_shape=[shape(*in_proj.shape), shape(in_rows, 128)],
        compiler_params=params(1),
        name="unpack_gradient",
    )(*pieces, in_proj)
    grad_norm = gain_products[:, 0] / norm_gain.astype(F32)

    def placed(v):
        out = jnp.zeros((groups,) + v.shape, F32)
        return lax.dynamic_update_slice_in_dim(out, v[None], me, 0)

    g_x = jnp.sum(jnp.concatenate(g_x, axis=2), axis=0)[: CONV + 1]
    g_b = jnp.sum(g_b, axis=0)[: CONV + 1]
    g_skip = jnp.sum(jnp.concatenate([g[:, 0] for g in g_skip], axis=1), axis=0)
    grad_skip_g = jnp.sum(g_skip.reshape(1, heads, HEADDIM), axis=2)
    g_head = jnp.sum(g_head, axis=0)[:2, :heads]
    pieces = [
        placed(g_x), g_b, placed(jnp.sum(gate_sums[:, 0], axis=0)),
        placed(jnp.concatenate([g_head, grad_skip_g], axis=0)),
    ]
    flat = jnp.concatenate([p.reshape(-1) for p in pieces])
    count = flat.shape[0]
    flat = jnp.pad(flat, (0, -count % 1024)).reshape(-1, 128)
    marks = [grad_last, split_last, in_sent, in_kept, in_own]
    flat = sum_over(flat, ("x", "a", "b", "core"), marks).reshape(-1)
    at, back = 0, []
    for p in pieces:
        back.append(flat[at : at + p.size].reshape(p.shape))
        at += p.size
    conv_x, conv_b, gate_all, head_all = back
    conv_sum = jnp.concatenate([conv_x.transpose(1, 0, 2).reshape(CONV + 1, INNER), conv_b], axis=1)
    conv_own = lax.dynamic_slice_in_dim(conv_sum, index * n_conv, n_conv, 1)
    grad_gate = lax.dynamic_slice_in_dim(gate_all.reshape(-1), index * n_gate, n_gate, 0)
    head_all = head_all.transpose(1, 0, 2).reshape(3, HEADS)
    return (
        output, grad_tokens, grad_in_proj, conv_own[:CONV], conv_own[CONV], grad_out_proj,
        grad_norm, grad_gate, head_all[0], head_all[1], head_all[2],
    )


def solution(mesh):
    n_dp, n_seq = mesh.shape["dp"], mesh.shape["seq"]
    slow = 4 if n_seq % 4 == 0 else 1
    finer = Mesh(
        mesh.devices.reshape(n_dp // 2, 2, slow, n_seq // slow), ("x", "core", "a", "b")
    )
    every = ("x", "core", "a", "b")
    rows, flat, second, copied = P(every, None), P(every), P(None, every), P()
    in_specs = (rows, flat, rows, second, flat, rows, flat, flat, copied, copied, copied, rows)
    out_specs = (rows, rows, rows, second, flat, rows, flat, flat, copied, copied, copied)
    return jax.shard_map(
        on_device, mesh=finer, in_specs=in_specs, out_specs=out_specs, check_vma=False
    )
```

```python
import jax
import jax.numpy as jnp
from jax import lax
from jax.experimental import pallas as pl
from jax.experimental.pallas import tpu as pltpu
from jax.sharding import Mesh
from jax.sharding import PartitionSpec as P

INNER = 3072
HEADDIM = 64
STATE = 128
CONV = 4
GROUP = 256
HEADS = 48
XBC = 3328
LONGEST = 1024
HALO = 16
TILE = 128
PAIRS = 3
WIDE = PAIRS * 128
LAST = WIDE + 3 * 128

EPSILON = 1e-05
BF = jnp.bfloat16
F32 = jnp.float32
NEVER = -1e30

CUM, DT, CARRY, ENDN, SAME, SEG = 0, 16, 32, 48, 64, 67
SEG_ROW = 16


def shift(v, axis, step):
    n = lax.axis_size(axis)
    return lax.ppermute(v, axis, [(i, (i + step) % n) for i in range(n)])


def along(v, step):
    n = lax.axis_size("a") * lax.axis_size("b")
    route = [(i, i + step) for i in range(n) if 0 <= i + step < n]
    return lax.ppermute(v, ("a", "b"), route)


def exchange(v, axes):
    return lax.all_to_all(v, axes, 0, 0, tiled=True)


def group_of(sx, sc):
    x, c, n = lax.axis_index("x"), lax.axis_index("core"), lax.axis_size("x")
    return lax.rem(x + sx + n, n) * 2 + (c + sc) % 2


def position_of(sa, sb):
    na, nb = lax.axis_size("a"), lax.axis_size("b")
    a, b = lax.axis_index("a"), lax.axis_index("b")
    return lax.rem(a + sa + na, na) * nb + lax.rem(b + sb + nb, nb)


def after(v, *others):
    def nothing(*refs):
        pass

    anywhere = pl.BlockSpec(memory_space=pl.ANY)
    return pl.pallas_call(
        nothing,
        in_specs=[anywhere] * (1 + len(others)),
        out_specs=anywhere,
        out_shape=jax.ShapeDtypeStruct(v.shape, v.dtype),
        input_output_aliases={0: 0},
        name="in_order",
    )(v, *others)


def gather_over_x(v):
    return [v] + [shift(v, "x", sx) for sx in range(1, lax.axis_size("x"))]


def gather_over_cores(along_x, *others):
    slots = []
    for sx, here in enumerate(along_x):
        here = after(here, *others) if sx else here
        slots += [here, shift(here, "core", 1)]
    return slots


def sum_over_cores(kept, sent):
    both = kept + shift(sent.astype(BF), "core", 1).astype(F32)
    return both[0], [both[sx].astype(BF) for sx in range(1, lax.axis_size("x"))]


def sum_to_owner(own, others):
    total = own
    for sx in range(1, lax.axis_size("x")):
        total = total + shift(others[sx - 1], "x", -sx).astype(F32)
    return total


def sum_over_group(v):
    n = lax.axis_size("x")
    v = v.reshape((n, 2) + v.shape[1:])
    v = v + shift(v, "core", 1)[:, ::-1]
    total = v
    for step in range(1, n):
        total = total + jnp.roll(shift(v, "x", step), step, axis=0)
    return total.reshape((n * 2,) + v.shape[2:])


def gather_over_a(block):
    return exchange(jnp.broadcast_to(block[None], (lax.axis_size("a"),) + block.shape), "a")


def gather_over_b(v):
    return [v] + [shift(v, "b", sb) for sb in range(1, lax.axis_size("b"))]


def sum_over_b(parts, *others):
    total = (after(parts[0], *others) if others else parts[0]).astype(F32)
    for rb in range(1, lax.axis_size("b")):
        total = total + shift(parts[rb], "b", rb).astype(F32)
    return total.astype(BF)


def sum_over_a(parts):
    return jnp.sum(exchange(parts, "a").astype(F32), axis=0)


def sum_over(v, axes, marks=()):
    marks = list(marks)
    for axis in axes:
        step, n = 1, lax.axis_size(axis)
        while step < n:
            moved = lax.ppermute(v, axis, [(i, i ^ step) for i in range(n)])
            v = (after(v, marks.pop(0)) if marks else v) + moved
            step *= 2
    return v


def nn(a, b):
    return lax.dot_general(a, b, (((1,), (0,)), ((), ())), preferred_element_type=F32)


def nt(a, b):
    return lax.dot_general(a, b, (((1,), (1,)), ((), ())), preferred_element_type=F32)


def tn(a, b):
    return lax.dot_general(a, b, (((0,), (0,)), ((), ())), preferred_element_type=F32)


def low_half(rows):
    return lax.broadcasted_iota(jnp.int32, (rows, 128), 1) < HEADDIM


def spread(table, kind, pair):
    at = kind + 2 * pair
    return jnp.where(low_half(table.shape[0]), table[:, at : at + 1], table[:, at + 1 : at + 2])


def lane_wise(table, kind):
    high = table.astype(BF)
    low = (table - high.astype(F32)).astype(BF)
    head_of = lax.broadcasted_iota(jnp.int32, (128, WIDE), 1) // HEADDIM + kind
    pick = (head_of == lax.broadcasted_iota(jnp.int32, (128, WIDE), 0)).astype(BF)
    return nn(jnp.concatenate([high, low], axis=1), jnp.concatenate([pick, pick], axis=0))


def lanes_of(pair):
    return slice(pair * 128, (pair + 1) * 128)


def rows_of(chunk):
    return slice(chunk * GROUP, (chunk + 1) * GROUP)


def end_of(chunk):
    return slice((chunk + 1) * GROUP - 1, (chunk + 1) * GROUP)


def from_start(carry, chunks):
    out, run = [carry[rows_of(0)]], carry[end_of(0)]
    for c in range(1, chunks):
        out.append(carry[rows_of(c)] * run)
        run = run * carry[end_of(c)]
    return jnp.concatenate(out, axis=0)


def to_block_end(endn, table, chunks):
    out, run = [endn[rows_of(chunks - 1)]], None
    for c in range(chunks - 2, -1, -1):
        keep = lane_wise(table[(c + 2) * GROUP - 8 : (c + 2) * GROUP], CARRY)[7:]
        run = keep if run is None else run * keep
        out.insert(0, endn[rows_of(c)] * run)
    return jnp.concatenate(out, axis=0)


def earlier_rows(v, k):
    return pltpu.roll(v, k, 0)[: v.shape[0] - HALO]


def convolved(v, taps, same):
    rows = v.shape[0] - HALO
    pre = taps[CONV : CONV + 1] + taps[CONV - 1 : CONV] * v[:rows]
    for k in range(1, CONV):
        pre = pre + same[k - 1] * (taps[CONV - 1 - k : CONV - k] * earlier_rows(v, k))
    return pre


def rounded(v):
    return v.astype(BF).astype(F32)


def same_columns(table):
    rows = table.shape[0]
    return [
        jnp.broadcast_to(table[:, SAME + k : SAME + k + 1], (rows, 128)) for k in range(CONV - 1)
    ]


def pack_kernel(weight_ref, first_ref, cols, heads):
    state2 = 2 * STATE
    rows = weight_ref.shape[0]
    steps = weight_ref[:, INNER + XBC :].astype(F32)
    steps = jnp.concatenate([steps, jnp.zeros((rows, 128 - steps.shape[1]), F32)], axis=1)
    lane = lax.broadcasted_iota(jnp.int32, (rows, 128), 1)
    for r in range(first_ref.shape[0]):
        at, early = r * cols, cols - WIDE
        tail = INNER + at + early
        first_ref[r, :, :WIDE] = weight_ref[:, tail : tail + WIDE]
        first_ref[r, :, WIDE : WIDE + state2] = weight_ref[:, 2 * INNER : INNER + XBC]
        mine = pltpu.roll(steps, (128 - r * heads) % 128, 1)
        first_ref[r, :, WIDE + state2 : LAST] = jnp.where(lane < heads, mine, 0.0).astype(BF)
        if early:
            first_ref[r, :, LAST : LAST + early] = weight_ref[:, INNER + at : INNER + at + early]
        first_ref[r, :, LAST + early :] = weight_ref[:, at : at + cols]


def unpack_kernel(last_ref, early_ref, weight_ref, out_ref, gain_ref, cols, heads):
    state2 = 2 * STATE
    shared, steps = None, None
    lane = lax.broadcasted_iota(jnp.int32, (out_ref.shape[0], 128), 1)
    for r in range(last_ref.shape[0]):
        at, early = r * cols, cols - WIDE
        tail = INNER + at + early
        out_ref[:, at : at + cols] = early_ref[r, :, :cols].astype(F32)
        out_ref[:, tail : tail + WIDE] = last_ref[r, :, :WIDE].astype(F32)
        if early:
            out_ref[:, INNER + at : tail] = early_ref[r, :, cols:].astype(F32)
        both = last_ref[r, :, WIDE : WIDE + state2].astype(F32)
        shared = both if shared is None else shared + both
        step = jnp.where(lane < heads, last_ref[r, :, WIDE + state2 :].astype(F32), 0.0)
        step = pltpu.roll(step, r * heads, 1) if r else step
        steps = step if steps is None else steps + step
    out_ref[:, 2 * INNER : INNER + XBC] = shared
    out_ref[:, INNER + XBC :] = steps[:, : out_ref.shape[1] - INNER - XBC]
    products = out_ref[...] * weight_ref[...].astype(F32)
    gain_ref[...] = jnp.broadcast_to(jnp.sum(products, axis=1, keepdims=True), gain_ref.shape)


def place_kernel(at_ref, *refs, moves, n_in):
    for source, row, lane, target, to, more, to_lane, count, wide in moves:
        if more is not None:
            to = pl.multiple_of(to + at_ref[more] * count, 16)
        piece = refs[source][row : row + count, lane : lane + wide]
        refs[n_in + target][pl.ds(to, count), to_lane : to_lane + wide] = piece


def norm_kernel(*refs):
    gain_ref, out_ref = refs[-2], refs[-1]
    for r in range(len(refs) - 2):
        v = refs[r][...].astype(F32)
        scale = lax.rsqrt(jnp.mean(v * v, axis=-1, keepdims=True) + EPSILON)
        out_ref[r] = (v * scale * gain_ref[0:1, :]).astype(BF)


def norm_back_kernel(tokens_ref, cot_ref, *refs):
    gain_ref, out_ref = refs[-2], refs[-1]
    total = refs[0][...]
    for ref in refs[1:-2]:
        total = total + ref[...].astype(F32)
    inner = total * gain_ref[0:1, :]
    v = tokens_ref[...].astype(F32)
    r = lax.rsqrt(jnp.mean(v * v, axis=-1, keepdims=True) + EPSILON)
    pull = r * r * jnp.mean(inner * v, axis=-1, keepdims=True)
    out_ref[...] = cot_ref[...].astype(F32) + r * (inner - v * pull)


def table_kernel(dt_ref, seg_ref, par_ref, ct_ref, rt_ref, heads):
    rows = dt_ref.shape[1]
    chunks = rows // GROUP
    lane = lax.broadcasted_iota(jnp.int32, (rows, 128), 1)
    v = dt_ref[0] + par_ref[0:1, :]
    step = jnp.where(lane < heads, jnp.maximum(v, 0.0) + jnp.log1p(jnp.exp(-jnp.abs(v))), 0.0)
    decay = -par_ref[1:2, :] * step
    aux = jnp.concatenate([seg_ref[0], jnp.zeros((120, rows), F32)], axis=0).T
    seg, entering = aux[:, 3:4], aux[:, 4:5]
    cums, carries, ends = [], [], []
    for c in range(chunks):
        cum = decay[rows_of(c)]
        step_rows = 1
        while step_rows < GROUP:
            cum = cum + jnp.concatenate(
                [jnp.zeros((step_rows, 128), F32), cum[: GROUP - step_rows]], axis=0
            )
            step_rows *= 2
        here = seg[rows_of(c)]
        held = entering[rows_of(0)] > 0.5 if c == 0 else here == seg[end_of(c - 1)]
        cums.append(cum)
        carries.append(jnp.where(held, jnp.exp(cum), 0.0))
        ends.append(jnp.where(here == seg[end_of(c)], jnp.exp(cum[GROUP - 1 :] - cum), 0.0))
    kept = lane < heads
    cum = jnp.concatenate(cums, axis=0)
    carry = jnp.where(kept, jnp.concatenate(carries, axis=0), 0.0)
    endn = jnp.where(kept, jnp.concatenate(ends, axis=0), 0.0)
    whole = cum + pltpu.roll(step, DT, 1) + pltpu.roll(carry, CARRY, 1) + pltpu.roll(endn, ENDN, 1)
    aux = pltpu.roll(jnp.where(lane < 4, aux, 0.0), SAME, 1)
    for t in range(ct_ref.shape[1]):
        mine = whole if t == 0 else pltpu.roll(whole, 128 - 2 * PAIRS * t, 1)
        ct_ref[0, t] = jnp.where((lane >= SAME) & (lane < SAME + 4), aux, mine)
    rt_ref[0, :SEG_ROW] = cum.T[:SEG_ROW]
    rt_ref[0, SEG_ROW:] = jnp.broadcast_to(seg_ref[0, 3:4, :], (8, rows))


def conv_kernel(xm_ref, bm_ref, cm_ref, tx_ref, tb_ref, ct_ref, x_ref, bc_ref, own_ref):
    table = ct_ref[0, 0]
    chunks = table.shape[0] // GROUP
    same = same_columns(table)

    @pl.when(pl.program_id(1) == 0)
    def _():
        for i, main in enumerate((bm_ref, cm_ref)):
            pre = convolved(rounded(main[0]), tb_ref[:, lanes_of(i)], same)
            bc_ref[0, :, lanes_of(i)] = (pre * jax.nn.sigmoid(pre)).astype(BF)

    weighted = []
    left = to_block_end(lane_wise(table, ENDN), table, chunks) * lane_wise(table, DT)
    for j in range(PAIRS):
        at = lanes_of(j)
        pre = convolved(rounded(xm_ref[0, :, at]), tx_ref[:, at], same)
        x = pre * jax.nn.sigmoid(pre)
        x_ref[0, :, at] = x
        weighted.append((left[:, at] * x).astype(BF))
    own_ref[0] = tn(bc_ref[0, :, :STATE], jnp.concatenate(weighted, axis=1))


def causal(table, segrow, chunk, transposed):
    seg_c = table[rows_of(chunk), SEG : SEG + 1]
    seg_r = segrow[:, rows_of(chunk)]
    down = lax.broadcasted_iota(jnp.int32, (GROUP, GROUP), 0)
    right = lax.broadcasted_iota(jnp.int32, (GROUP, GROUP), 1)
    order = (down <= right) if transposed else (down >= right)
    return jnp.where((seg_c == seg_r) & order, 0.0, NEVER)


def halves_of(v, half):
    return [jnp.where(half, v, 0.0).astype(BF), jnp.where(half, 0.0, v).astype(BF)]


def mix_kernel(x_ref, bc_ref, ct_ref, rt_ref, skip_ref, y_ref, score, mask):
    table = ct_ref[0, 0]
    chunks = x_ref.shape[1] // GROUP
    base = pl.program_id(1) * (2 * PAIRS)

    @pl.when(pl.program_id(1) == 0)
    def _():
        for c in range(chunks):
            score[c] = nt(bc_ref[0, rows_of(c), STATE:], bc_ref[0, rows_of(c), :STATE])
            mask[c] = causal(table, rt_ref[0, SEG_ROW : SEG_ROW + 1, :], c, False)

    dts, endns = lane_wise(table, DT), lane_wise(table, ENDN)
    carries = [lane_wise(table[rows_of(c)], CARRY) for c in range(1, chunks)]
    states = None
    for c in range(chunks):
        rows = rows_of(c)
        x = x_ref[0, rows, :]
        xd = x * dts[rows]
        xdb = xd.astype(BF)
        y_in = skip_ref[0:1, :] * x
        if c:
            y_in = y_in + carries[c - 1] * nn(bc_ref[0, rows, STATE:], states.astype(BF))
        if c + 1 < chunks:
            added = tn(bc_ref[0, rows, :STATE], (endns[rows] * xd).astype(BF))
            states = added if c == 0 else carries[c - 1][GROUP - 1 :] * states + added
        for j in range(PAIRS):
            at = lanes_of(j)
            cum_rows = [rt_ref[0, pl.ds(base + 2 * j + e, 1), :] for e in range(2)]
            for top in range(0, GROUP, TILE):
                here, live = slice(top, top + TILE), slice(0, top + TILE)
                tile_rows = slice(c * GROUP + top, c * GROUP + top + TILE)
                scores, masks = score[c, here, live], mask[c, here, live]
                mixing = []
                for e in range(2):
                    h = 2 * j + e
                    row = cum_rows[e][:, c * GROUP : c * GROUP + top + TILE]
                    decay = jnp.exp(table[tile_rows, CUM + h : CUM + h + 1] - row + masks)
                    mixing.append((scores * decay).astype(BF))
                y = nn(jnp.concatenate(mixing, axis=0), xdb[live, at])
                y_ref[0, tile_rows, at] = y_in[here, at] + jnp.where(low_half(TILE), y[:TILE], y[TILE:])


def gate_kernel(yl_ref, bc_ref, inc_ref, z_ref, dn_ref, gain_ref, ct_ref, y_ref, sums_ref, held):
    table = ct_ref[0, 0]
    chunks = table.shape[0] // GROUP
    from_state = nn(bc_ref[0, :, STATE:], inc_ref[0].astype(BF))
    squares, pulled = None, None
    reach = from_start(lane_wise(table, CARRY), chunks)
    for j in range(PAIRS):
        at = lanes_of(j)
        y = yl_ref[0, :, at] + reach[:, at] * from_state[:, at]
        y_ref[0, :, at] = y
        z = z_ref[0, :, at]
        gated = y * (z * jax.nn.sigmoid(z))
        square, pull = gated * gated, dn_ref[0, :, at] * gain_ref[0:1, at] * gated
        squares = square if j == 0 else squares + square
        pulled = pull if j == 0 else pulled + pull
    lane = lax.broadcasted_iota(jnp.int32, squares.shape, 1)
    squares = jnp.sum(squares, axis=1, keepdims=True)
    pulled = jnp.sum(pulled, axis=1, keepdims=True)
    both = jnp.where(lane == 0, squares, jnp.where(lane == 1, pulled, 0.0))
    first = pl.program_id(1) == 0

    @pl.when(first)
    def _():
        held[...] = both

    @pl.when(jnp.logical_not(first))
    def _():
        held[...] += both

    @pl.when(pl.program_id(1) == pl.num_programs(1) - 1)
    def _():
        sums_ref[0] = held[...].T[:8]


def gate_back_kernel(
    y_ref, z_ref, dn_ref, gain_ref, sums_ref, bc_ref, ct_ref, out_ref, dy_ref, dz_ref, pull_ref, gg_ref
):
    table = ct_ref[0, 0]
    chunks = table.shape[0] // GROUP
    sums = jnp.concatenate([sums_ref[0], jnp.zeros((120, table.shape[0]), F32)], axis=0).T
    r = lax.rsqrt(sums[:, 0:1] * (1.0 / INNER) + EPSILON)
    along_unit = r * (1.0 / INNER) * sums[:, 1:2]
    pulled = []
    reach = from_start(lane_wise(table, CARRY), chunks)
    for j in range(PAIRS):
        at = lanes_of(j)
        gain = gain_ref[0:1, at]
        y, z, dn = y_ref[0, :, at], z_ref[0, :, at], dn_ref[0, :, at]
        sig = jax.nn.sigmoid(z)
        silu = z * sig
        unit = y * silu * r
        out_ref[0, :, at] = (unit * gain).astype(BF)
        dg = r * (dn * gain - unit * along_unit)
        dy = dg * silu
        dy_ref[0, :, at] = dy
        dz_ref[0, : y.shape[0], at] = (dg * y * (sig * (1.0 + z * (1.0 - sig)))).astype(BF)
        dz_ref[0, y.shape[0] :, at] = jnp.zeros((HALO, 128), BF)
        pulled.append((reach[:, at] * dy).astype(BF))
        grad = jnp.sum(dn * unit, axis=0, keepdims=True)
        gg_ref[0, :, at] = jnp.broadcast_to(grad, (8, 128))
    pull_ref[0] = tn(bc_ref[0, :, STATE:], jnp.concatenate(pulled, axis=1))


def conv_back(d_conv, v, taps, same):
    rows, width = d_conv.shape
    pre = convolved(v, taps, same)
    sig = jax.nn.sigmoid(pre)
    d_pre = d_conv * (sig * (1.0 + pre * (1.0 - sig)))
    none = jnp.zeros((HALO, width), F32)
    d_v = jnp.concatenate([taps[CONV - 1 : CONV] * d_pre, none], axis=0)
    grads = [jnp.zeros((1, width), F32)] * 8
    grads[CONV - 1] = jnp.sum(d_pre * v[:rows], axis=0, keepdims=True)
    grads[CONV] = jnp.sum(d_pre, axis=0, keepdims=True)
    for k in range(1, CONV):
        kept = same[k - 1] * d_pre
        grads[CONV - 1 - k] = jnp.sum(kept * earlier_rows(v, k), axis=0, keepdims=True)
        moved = pltpu.roll(jnp.concatenate([kept, none], axis=0), rows + HALO - k, 0)
        d_v = d_v + taps[CONV - 1 - k : CONV - k] * moved
    return d_v.astype(BF), jnp.concatenate(grads, axis=0)


def mix_back_kernel(*refs, base, first, last):
    x_ref, bc_ref, dy_ref, inc_ref, adj_ref, ct_ref, rt_ref, skip_ref, xm_ref, tx_ref = refs[:10]
    at_ref = 10
    if not first:
        before_ref = refs[at_ref]
        at_ref += 1
    if last:
        bm_ref, cm_ref, dt_ref, tb_ref, par_ref = refs[at_ref : at_ref + 5]
    if last:
        d_ref, gx_ref, gs_ref, gb_ref, gh_ref = refs[-11:-6]
    else:
        d_ref, gx_ref, gs_ref, part_ref = refs[-10:-6]
    d_x, score_ref, mask_ref, d_score_ref, d_step_ref, cross_ref = refs[-6:]

    table = ct_ref[0, 0]
    chunks = x_ref.shape[1] // GROUP
    cross_ref[2 * PAIRS :] = jnp.zeros((8 - 2 * PAIRS, cross_ref.shape[1]), F32)
    down = lax.broadcasted_iota(jnp.int32, (GROUP, GROUP), 0)
    right = lax.broadcasted_iota(jnp.int32, (GROUP, GROUP), 1)
    before = (right < down).astype(BF)
    upto = (right >= down).astype(BF)
    upto_t, crossed = (down >= right).astype(BF), down < right
    same = same_columns(table)
    half = low_half(GROUP)
    head_of = lax.broadcasted_iota(jnp.int32, (WIDE, 128), 0) // HEADDIM + base
    pick = (head_of == lax.broadcasted_iota(jnp.int32, (WIDE, 128), 1)).astype(BF)

    carries = [lane_wise(table[rows_of(c)], CARRY) for c in range(chunks)]
    pulled = [carries[c] * dy_ref[0, rows_of(c), :] for c in range(chunks)]
    dts = [lane_wise(table[rows_of(c)], DT) for c in range(chunks)]
    xds = [x_ref[0, rows_of(c), :] * dts[c] for c in range(chunks)]
    endns = [lane_wise(table[rows_of(c)], ENDN) for c in range(chunks)]
    endings = [endns[c] * xds[c] for c in range(chunks)]
    states, adjoints = [inc_ref[0]], [adj_ref[0]]
    for c in range(chunks - 1):
        added = tn(bc_ref[0, rows_of(c), :STATE], endings[c].astype(BF))
        states.append(carries[c][GROUP - 1 :] * states[-1] + added)
    for c in range(chunks - 1, 0, -1):
        added = tn(bc_ref[0, rows_of(c), STATE:], pulled[c].astype(BF))
        adjoints.insert(0, carries[c][GROUP - 1 :] * adjoints[0] + added)

    d_keys, d_reads, all_logs, all_steps = [], [], [], []
    for c in range(chunks):
        rows = rows_of(c)
        keys, reads = bc_ref[0, rows, :STATE], bc_ref[0, rows, STATE:]
        state_b, adj_b = states[c].astype(BF), adjoints[c].astype(BF)
        from_state = pulled[c] * nn(reads, state_b)
        to_end = nn(keys, adj_b)
        whole = carries[c][GROUP - 1 :] * jnp.sum(states[c] * adjoints[c], axis=0, keepdims=True)
        logs = nn(upto, nn(from_state.astype(BF), pick).astype(BF))
        logs = logs + nn(before, nn((endings[c] * to_end).astype(BF), pick).astype(BF))
        logs = logs + nn(jnp.broadcast_to(whole, (8, WIDE)).astype(BF), pick)[:1]
        d_k, d_r = nt(endings[c].astype(BF), adj_b), nt(pulled[c].astype(BF), state_b)
        score = nt(keys, reads)
        mask = causal(table, rt_ref[0, SEG_ROW : SEG_ROW + 1, :], c, True)
        score_ref[...], mask_ref[...] = score, mask
        for j in range(PAIRS):
            at = lanes_of(j)
            dy = dy_ref[0, rows, at]
            dyb = dy.astype(BF)
            parts = halves_of(xds[c][:, at], half)
            crossings = [None, None]
            for top in range(0, GROUP, TILE):
                here, live = slice(top, top + TILE), slice(top // 128 * 128, GROUP)
                tile_rows = slice(c * GROUP + top, c * GROUP + top + TILE)
                scores = score_ref[here, live]
                weighted = nt(jnp.concatenate([parts[0][here], parts[1][here]], axis=0), dyb[live])
                decays = []
                for e in range(2):
                    h = 2 * j + e
                    row = rt_ref[0, base + h : base + h + 1, rows][:, live]
                    decays.append(jnp.exp(row - table[tile_rows, CUM + h : CUM + h + 1] + mask_ref[here, live]))
                weighted = [decays[0] * weighted[:TILE], decays[1] * weighted[TILE:]]
                d_scores = weighted[0] + weighted[1]
                mixing = jnp.concatenate([(scores * v).astype(BF) for v in decays], axis=0)
                d_xd = nn(mixing, dyb[live])
                d_xd = [d_xd[:TILE], d_xd[TILE:]]
                after_t = nn(jnp.concatenate([(scores * v).astype(BF) for v in weighted], axis=0), upto_t[live])
                for e in range(2):
                    mine = jnp.where(crossed[here], after_t[e * TILE : (e + 1) * TILE], 0.0)
                    crossing = jnp.sum(mine, axis=0, keepdims=True)
                    crossings[e] = crossing if top == 0 else crossings[e] + crossing
                if j == 0:
                    d_score_ref[here, live] = d_scores
                else:
                    d_score_ref[here, live] += d_scores
                u = jnp.where(half[:TILE], d_xd[0], d_xd[1]) + endns[c][here, at] * to_end[here, at]
                x = x_ref[0, tile_rows, at]
                d_x[tile_rows, at] = dts[c][here, at] * u + skip_ref[0:1, at] * dy[here]
                d_step_ref[here, at] = (x * u).astype(BF)
            for e in range(2):
                cross_ref[2 * j + e : 2 * j + e + 1, rows] = crossings[e]
        all_logs.append(logs)
        all_steps.append(nn(d_step_ref[...], pick))
        if GROUP > 128:
            d_score_ref[128:, :128] = jnp.zeros((GROUP - 128, 128), F32)
        ds = d_score_ref[...].astype(BF)
        d_keys.append(d_k + nn(ds, reads))
        d_reads.append(d_r + tn(ds, keys))
    turned = jnp.concatenate([cross_ref[...], jnp.zeros((120, cross_ref.shape[1]), F32)], axis=0).T
    turned = pltpu.roll(turned, base, 1) if base else turned
    all_logs = [v + turned[rows_of(c)] for c, v in enumerate(all_logs)]

    for j in range(PAIRS):
        at = lanes_of(j)
        grad = jnp.sum(dy_ref[0, :, at] * x_ref[0, :, at], axis=0, keepdims=True)
        gs_ref[0, :, at] = jnp.broadcast_to(grad, (8, 128))
        d_rows, grads = conv_back(d_x[:, at], rounded(xm_ref[0, :, at]), tx_ref[:, at], same)
        d_ref[0, :, at], gx_ref[0, :, at] = d_rows, grads

    state2 = 2 * STATE
    for i, d_rows in enumerate((d_keys, d_reads)):
        at = lanes_of(i)
        whole = jnp.concatenate(d_rows, axis=0)
        if not first:
            whole = whole + before_ref[0, :, at]
        if last:
            main_ref = (bm_ref, cm_ref)[i]
            d_rows, grads = conv_back(whole, rounded(main_ref[0]), tb_ref[:, at], same)
            d_ref[0, :, lanes_of(PAIRS + i)], gb_ref[0, :, at] = d_rows, grads
        else:
            part_ref[0, :, at] = whole
    logs, steps = jnp.concatenate(all_logs, axis=0), jnp.concatenate(all_steps, axis=0)
    if not first:
        logs = logs + before_ref[0, :, state2 : state2 + 128]
        steps = steps + before_ref[0, :, state2 + 128 :]
    if last:
        rows = logs.shape[0]
        v = dt_ref[0, :rows] + par_ref[0:1, :]
        step_dt = jnp.maximum(v, 0.0) + jnp.log1p(jnp.exp(-jnp.abs(v)))
        d_dt = (steps - par_ref[1:2, :] * logs) * jax.nn.sigmoid(v)
        d_ref[0, :rows, lanes_of(PAIRS + 2)] = d_dt.astype(BF)
        d_ref[0, rows:, lanes_of(PAIRS + 2)] = jnp.zeros((HALO, 128), BF)
        by_bias = jnp.sum(d_dt, axis=0, keepdims=True)
        by_log = -jnp.sum(par_ref[1:2, :] * step_dt * logs, axis=0, keepdims=True)
        gh_ref[0] = jnp.concatenate([by_log, by_bias, jnp.zeros((6, 128), F32)], axis=0)
    else:
        part_ref[0, :, state2 : state2 + 128] = logs
        part_ref[0, :, state2 + 128 :] = steps


def split_kernel(at_ref, v_ref, out_ref):
    out_ref[0] = v_ref[:, 0].astype(BF)


def split_both_kernel(at_ref, v_ref, w_ref, out_ref):
    groups, rows, cols = v_ref.shape[0], v_ref.shape[2], v_ref.shape[3]
    many = w_ref.shape[2]
    for g in range(groups):
        out_ref[0, g * rows : (g + 1) * rows, :cols] = v_ref[g, 0].astype(BF)
    for half in range(2):
        here = w_ref[0, 0, :, half * cols : (half + 1) * cols].astype(BF)
        out_ref[0, half * many : (half + 1) * many, cols:] = here


def shape(*dims, dtype=F32):
    return jax.ShapeDtypeStruct(dims, dtype)


def params(n=2, limit=48):
    return pltpu.CompilerParams(
        dimension_semantics=("arbitrary",) * n, vmem_limit_bytes=limit * 2**20
    )


def cost(flops, size, part=1):
    return pl.CostEstimate(flops=int(flops) // part, bytes_accessed=int(size) // part, transcendentals=0)


def on_device(
    tokens, segment_ids, in_proj, conv_weight, conv_bias, out_proj, norm_gain, gate_gain,
    a_log, dt_bias, skip_d, cotangent,
):
    n_x = lax.axis_size("x")
    na, nb = lax.axis_size("a"), lax.axis_size("b")
    groups, positions = 2 * n_x, na * nb
    me, place = group_of(0, 0), position_of(0, 0)
    index = me * positions + place
    rows, width = tokens.shape
    long = rows + HALO
    heads = HEADS // groups
    cols = heads * HEADDIM
    n_steps = heads // (2 * PAIRS)
    state2 = 2 * STATE
    early = cols - WIDE
    first_cols, all_cols = LAST + early, LAST + cols + early
    in_rows, out_rows = in_proj.shape[0], out_proj.shape[0]
    aligned = in_rows % 16 == 0 and width == 2 * cols and 2 * out_rows == groups * in_rows
    anywhere = pl.BlockSpec(memory_space=pl.ANY)

    small = jnp.concatenate([norm_gain, gate_gain, conv_bias, conv_weight.reshape(-1)])
    n_norm, n_gate, n_conv = norm_gain.shape[0], gate_gain.shape[0], conv_bias.shape[0]
    small = jnp.pad(small, (0, -small.shape[0] % 128))
    every = jnp.zeros((groups * positions, small.shape[0]), BF)
    every = lax.dynamic_update_slice_in_dim(every, small[None], index, 0)

    packed = pl.pallas_call(
        lambda *refs: pack_kernel(*refs, cols=cols, heads=heads),
        grid=(1,),
        in_specs=[pl.BlockSpec(in_proj.shape, lambda i: (0, 0))],
        out_specs=pl.BlockSpec((groups, in_rows, all_cols), lambda i: (0, 0, 0)),
        out_shape=shape(groups, in_rows, all_cols, dtype=BF),
        compiler_params=params(1),
        name="pack_weights",
    )(in_proj)
    held = exchange(packed, ("x", "core"))
    every = sum_over(every, ("x", "core", "a"), [packed])
    block = held[:, :, :first_cols].reshape(-1, first_cols)
    block = after(block, every)
    first_over_a = [block] + [shift(block, "a", sa) for sa in range(1, na)]
    every = sum_over(every, ("b",))
    first_blocks = [v for here in first_over_a for v in gather_over_b(here)]

    ids_row = jnp.pad(segment_ids.astype(BF)[None], ((0, 15), (0, width - rows)))
    before = along(jnp.concatenate([tokens[rows - HALO :], ids_row], axis=0), 1)
    token_rows = jnp.concatenate([tokens, before[:HALO], ids_row[:8], before[HALO : HALO + 8]], axis=0)
    token_rows = gather_over_x(after(token_rows, every, held))
    slots = gather_over_cores(token_rows, *first_blocks)

    every = every.astype(F32)
    cuts = [n_norm, n_norm + n_gate, n_norm + n_gate + n_conv]
    gain_in = every[:, : cuts[0]].reshape(1, -1)
    gain_out = every[:, cuts[0] : cuts[1]].reshape(-1)
    bias_all = every[:, cuts[1] : cuts[2]].reshape(-1)
    taps_all = every[:, cuts[2] : cuts[2] + CONV * n_conv].reshape(-1, CONV, n_conv)
    taps_all = taps_all.transpose(1, 0, 2).reshape(CONV, XBC)
    conv_all = jnp.concatenate([taps_all, bias_all[None], jnp.zeros((3, XBC), F32)], axis=0)
    taps_x = lax.dynamic_slice_in_dim(conv_all, me * cols, cols, 1)
    taps_b = conv_all[:, INNER:]
    gain_g = jnp.broadcast_to(lax.dynamic_slice_in_dim(gain_out, me * cols, cols, 0), (8, cols))
    a_g = lax.dynamic_slice_in_dim(a_log, me * heads, heads, 0)
    bias_g = lax.dynamic_slice_in_dim(dt_bias, me * heads, heads, 0)
    skip_g = lax.dynamic_slice_in_dim(skip_d, me * heads, heads, 0)
    head_rows = jnp.pad(jnp.stack([bias_g, jnp.exp(a_g)]), ((0, 6), (0, 128 - heads)))
    skip_l = jnp.broadcast_to(jnp.repeat(skip_g, HEADDIM), (8, cols))

    tall = long // 3
    normed = pl.pallas_call(
        norm_kernel,
        grid=(long // tall,),
        in_specs=[pl.BlockSpec((tall, width), lambda i: (i, 0))] * groups
        + [pl.BlockSpec((8, width), lambda i: (0, 0))],
        out_specs=pl.BlockSpec((groups, tall, width), lambda i: (0, i, 0)),
        out_shape=shape(groups, long, width, dtype=BF),
        compiler_params=params(1),
        cost_estimate=cost(10 * groups * rows * width, 4 * groups * rows * width, 16),
        name="input_norm",
    )(*slots, jnp.broadcast_to(gain_in, (8, width)))
    ids = jnp.concatenate([s[long : long + 1, :rows] for s in slots], axis=0)
    halo_ids = jnp.concatenate([s[long + 8 : long + 9, rows - HALO : rows] for s in slots], axis=0)
    ids = jnp.concatenate([jnp.where(place == 0, jnp.asarray(-1, BF), halo_ids), ids], axis=1).astype(F32)
    seg = ids[:, HALO:]
    seg_rows = jnp.stack(
        [(ids[:, HALO - k : HALO - k + rows] == seg).astype(F32) for k in range(1, CONV)]
        + [seg, (seg == ids[:, HALO - 1 : HALO]).astype(F32)]
        + [jnp.zeros_like(seg)] * 3,
        axis=1,
    )

    b_behind = jnp.stack([lax.rem(lax.axis_index("b") - sb + nb, nb) for sb in range(nb)])
    behind = jnp.stack([position_of(-sa, -sb) for sa in range(na) for sb in range(nb)])

    def place_rows(blocks, moves, outs, at, *others):
        return pl.pallas_call(
            lambda *refs: place_kernel(*refs, moves=moves, n_in=len(blocks) + len(others)),
            grid_spec=pltpu.PrefetchScalarGridSpec(
                num_scalar_prefetch=1,
                grid=(1,),
                in_specs=[pl.BlockSpec(v.shape, lambda i, s: (0, 0)) for v in blocks]
                + [anywhere] * len(others),
                out_specs=[pl.BlockSpec(v.shape, lambda i, s: (0, 0)) for v in outs],
            ),
            out_shape=outs,
            compiler_params=params(1, 56),
            name="place_weights",
        )(at, *blocks, *others)

    def in_moves(source, target, own_lane, lane, wide, held_by, many):
        return [
            (
                source + sb, a * many + i * in_rows, own_lane,
                target, ((held_by + i) * positions + a * nb) * in_rows, sb, lane, in_rows, wide,
            )
            for sb in range(nb) for a in range(na) for i in range(min(groups, many // in_rows))
        ]

    def whole_rows(blocks, many, parts):
        out = jnp.zeros((parts, na, nb, many) + blocks[0].shape[-1:], BF)
        for sb in range(nb):
            v = blocks[sb].reshape(na, parts, many, -1).transpose(1, 0, 2, 3)[:, :, None]
            out = lax.dynamic_update_slice_in_dim(out, v, b_behind[sb], 2)
        return out.reshape(parts * positions * many, -1)

    def flat2(v):
        return v.reshape(-1, v.shape[-1])

    if aligned:
        moves = [
            (k, g * in_rows, 0, 0, g * positions * in_rows, k, 0, in_rows, first_cols)
            for k in range(positions) for g in range(groups)
        ]
        (w_first,) = place_rows(first_blocks, moves, [shape(width, first_cols, dtype=BF)], behind, normed)
    else:
        w_first = jnp.zeros((groups, positions, in_rows, first_cols), BF)
        for k in range(positions):
            v = first_blocks[k].reshape(groups, 1, in_rows, first_cols)
            w_first = lax.dynamic_update_slice_in_dim(w_first, v, behind[k], 1)
        w_first = w_first.reshape(width, first_cols)

    cot_rows = gather_over_x(after(cotangent, w_first))
    gate_block = held[:, :, first_cols:].reshape(-1, cols)
    if aligned:
        out_block = jnp.concatenate([out_proj[:, :cols], out_proj[:, cols:]], axis=0)
        gate_over_a = gather_over_a(after(gate_block, *first_blocks))
    else:
        gate_over_a, out_over_a = gather_over_a(gate_block), gather_over_a(out_proj)

    normed_rows = normed.reshape(groups * long, width)
    proj = jnp.dot(normed_rows, w_first, preferred_element_type=F32).reshape(groups, long, first_cols)
    keys_at = WIDE // 128

    def step_tile(t):
        return jnp.where(t == n_steps - 1, 0, LAST // WIDE + t)

    def tile(count):
        return pl.BlockSpec((1, count, WIDE), lambda q, t: (q, 0, t))

    def narrow(at):
        return pl.BlockSpec((1, long, 128), lambda q, t: (q, 0, at))

    def per_seq(count, wide):
        return pl.BlockSpec((1, count, wide), lambda q, t: (q, 0, 0))

    def lanes(count):
        return pl.BlockSpec((count, WIDE), lambda q, t: (0, t))

    by_step = pl.BlockSpec((1, 1, rows, 128), lambda q, t: (q, t, 0, 0))
    all_taps = pl.BlockSpec((8, state2), lambda q, t: (0, 0))

    col_table, row_table = pl.pallas_call(
        lambda *refs: table_kernel(*refs, heads=heads),
        grid=(groups,),
        in_specs=[
            pl.BlockSpec((1, rows, 128), lambda q: (q, 0, keys_at + 2)),
            pl.BlockSpec((1, 8, rows), lambda q: (q, 0, 0)),
            pl.BlockSpec((8, 128), lambda q: (0, 0)),
        ],
        out_specs=[
            pl.BlockSpec((1, n_steps, rows, 128), lambda q: (q, 0, 0, 0)),
            pl.BlockSpec((1, SEG_ROW + 8, rows), lambda q: (q, 0, 0)),
        ],
        out_shape=[shape(groups, n_steps, rows, 128), shape(groups, SEG_ROW + 8, rows)],
        compiler_params=params(1),
        cost_estimate=cost(100 * groups * rows * 128, 16 * groups * rows * 128, 16),
        name="token_table",
    )(proj, seg_rows, head_rows)

    if aligned:
        out_block = after(out_block, *first_blocks)
        out_over_a = [shift(out_block, "a", sa) for sa in range(1, na)]
        out_over_a = jnp.stack([out_block] + [after(v, col_table) for v in out_over_a])
    grid = (groups, n_steps)
    big = groups * rows * cols
    values_x, bc, own_state = pl.pallas_call(
        lambda *refs: conv_kernel(*refs[:6], *refs[-3:]),
        grid=grid,
        in_specs=[
            pl.BlockSpec((1, long, WIDE), lambda q, t: (q, 0, step_tile(t))),
            narrow(keys_at), narrow(keys_at + 1), lanes(8), all_taps, by_step,
        ],
        out_specs=[tile(rows), per_seq(rows, state2), tile(STATE)],
        out_shape=[
            shape(groups, rows, cols), shape(groups, rows, state2, dtype=BF), shape(groups, STATE, cols),
        ],
        compiler_params=params(),
        cost_estimate=cost(20 * big * STATE, 8 * big, 16),
        name="conv_and_state",
    )(proj, proj, proj, taps_x, taps_b, col_table)

    if aligned:
        out_blocks = gather_over_b(out_over_a)
        gate_blocks = gather_over_b(after(gate_over_a, col_table))
    else:
        gate_blocks, out_blocks = gather_over_b(gate_over_a), gather_over_b(out_over_a)

    hops = -(-(LONGEST - 1) // rows)
    kept = col_table[:, :, GROUP - 1, CARRY : CARRY + 2 * PAIRS]
    for c in range(1, rows // GROUP):
        kept = kept * col_table[:, :, (c + 1) * GROUP - 1, CARRY : CARRY + 2 * PAIRS]
    device_decay = jnp.repeat(kept.reshape(groups, heads), HEADDIM, axis=-1)[:, None]

    def entering(own, sign):
        sent = jnp.concatenate(
            [own, jnp.broadcast_to(device_decay, (groups, 16, cols))], axis=1
        ).astype(BF)
        total_in, weight = None, None
        for hop in range(1, hops + 1):
            got = along(sent, sign * hop).astype(F32)
            state, decay = got[:, :STATE], got[:, STATE : STATE + 1]
            total_in = state if hop == 1 else total_in + weight * state
            weight = decay if hop == 1 else weight * decay
        return total_in

    incoming = entering(own_state, 1)

    mixed_local = pl.pallas_call(
        lambda *refs: mix_kernel(*refs[:5], *refs[6:]),
        grid=grid,
        in_specs=[
            tile(rows), per_seq(rows, state2), by_step, per_seq(SEG_ROW + 8, rows), lanes(8), anywhere,
        ],
        out_specs=tile(rows),
        out_shape=shape(groups, rows, cols),
        scratch_shapes=[pltpu.VMEM((rows // GROUP, GROUP, GROUP), F32)] * 2,
        compiler_params=params(),
        cost_estimate=cost(80 * big * GROUP, 8 * big, 16),
        name="mix_within_block",
    )(values_x, bc, col_table, row_table, skip_l, out_blocks[-1])

    if aligned:
        many = groups * in_rows
        moves = in_moves(0, 0, 0, LAST, cols, 0, many)
        moves.append((nb, 0, 0, 0, 0, None, 0, width, LAST))
        moves.append((nb, 0, LAST, 0, 0, None, LAST + cols, width, early))
        blocks = [flat2(v) for v in gate_blocks] + [w_first]
        (w_all,) = place_rows(blocks, moves, [shape(width, all_cols, dtype=BF)], b_behind, mixed_local)
        moves = [
            (sb, sa * many + half * out_rows, 0, 0, 0, sa * nb + sb, half * cols, out_rows, cols)
            for sb in range(nb) for sa in range(na) for half in range(2)
        ]
        blocks = [flat2(v) for v in out_blocks]
        (w_out,) = place_rows(blocks, moves, [shape(cols, width, dtype=BF)], behind)
    else:
        w_out = whole_rows(out_blocks, out_rows, 1)
        w_gate = whole_rows(gate_blocks, in_rows, groups)
        w_all = jnp.concatenate([w_first[:, :LAST], w_gate, w_first[:, LAST:]], axis=1)

    cot = jnp.stack(gather_over_cores(cot_rows, mixed_local))
    gate_z = jnp.dot(normed_rows, w_all[:, LAST : LAST + cols], preferred_element_type=F32)
    gate_z = gate_z.reshape(groups, long, cols)
    d_normed = jnp.einsum("qtd,cd->qtc", cot, w_out, preferred_element_type=F32)

    mixed_y, sums = pl.pallas_call(
        gate_kernel,
        grid=grid,
        in_specs=[
            tile(rows), per_seq(rows, state2), tile(STATE), tile(rows), tile(rows), lanes(8), by_step,
        ],
        out_specs=[tile(rows), per_seq(8, rows)],
        out_shape=[shape(groups, rows, cols), shape(groups, 8, rows)],
        scratch_shapes=[pltpu.VMEM((rows, 128), F32)],
        compiler_params=params(),
        cost_estimate=cost(2 * big * STATE, 16 * big, 16),
        name="gate",
    )(mixed_local, bc, incoming, gate_z, d_normed, gain_g, col_table)
    sums = sum_over_group(sums)

    gate_tile = LAST // WIDE
    normed_out, d_y, d_all, pull, gate_sums = pl.pallas_call(
        gate_back_kernel,
        grid=grid,
        in_specs=[
            tile(rows), tile(rows), tile(rows), lanes(8), per_seq(8, rows), per_seq(rows, state2), by_step,
        ],
        out_specs=[
            tile(rows), tile(rows),
            pl.BlockSpec((1, long, WIDE), lambda q, t: (q, 0, gate_tile + t)), tile(STATE), tile(8),
        ],
        out_shape=[
            shape(groups, rows, cols, dtype=BF), shape(groups, rows, cols),
            shape(groups, long, all_cols, dtype=BF), shape(groups, STATE, cols), shape(groups, 8, cols),
        ],
        compiler_params=params(),
        cost_estimate=cost(2 * big * STATE, 20 * big),
        name="gate_back",
    )(mixed_y, gate_z, d_normed, gain_g, sums, bc, col_table)

    later = entering(pull, -1)

    ahead = jnp.stack([a * nb + lax.rem(lax.axis_index("b") + rb, nb) for rb in range(nb) for a in range(na)])

    def split(grad, many):
        shaped = grad.reshape(-1, positions, many, grad.shape[1])
        g, _, r, c = shaped.shape
        out = pl.pallas_call(
            split_kernel,
            grid_spec=pltpu.PrefetchScalarGridSpec(
                num_scalar_prefetch=1,
                grid=(positions,),
                in_specs=[pl.BlockSpec((g, 1, r, c), lambda k, at: (0, at[k], 0, 0))],
                out_specs=pl.BlockSpec((1, g, r, c), lambda k, at: (k, 0, 0, 0)),
            ),
            out_shape=shape(positions, g, r, c, dtype=BF),
            compiler_params=params(1),
            cost_estimate=cost(grad.size, 6 * grad.size),
            name="split_gradient",
        )(ahead, shaped)
        return out.reshape(nb, na, g, r, c)

    def split_both(grad, other):
        many = groups * in_rows
        return pl.pallas_call(
            split_both_kernel,
            grid_spec=pltpu.PrefetchScalarGridSpec(
                num_scalar_prefetch=1,
                grid=(positions,),
                in_specs=[
                    pl.BlockSpec((groups, 1, in_rows, cols), lambda k, at: (0, at[k], 0, 0)),
                    pl.BlockSpec((1, 1, out_rows, width), lambda k, at: (0, at[k], 0, 0)),
                ],
                out_specs=pl.BlockSpec((1, many, width), lambda k, at: (k, 0, 0)),
            ),
            out_shape=shape(positions, many, width, dtype=BF),
            compiler_params=params(1),
            cost_estimate=cost(2 * grad.size, 12 * grad.size),
            name="split_gradients",
        )(
            ahead, grad.reshape(groups, positions, in_rows, cols), other.reshape(1, positions, out_rows, width)
        ).reshape(nb, na, many, width)

    def grad_of(d_values, low, high):
        d_rows = d_values[:, :, low:high].reshape(groups * long, high - low)
        return jnp.dot(normed_rows.T, d_rows, preferred_element_type=F32)

    grad_out = jnp.einsum("qtc,qtd->cd", normed_out, cot, preferred_element_type=F32)
    grad_gate_cols = grad_of(d_all, LAST, LAST + cols)
    if aligned:
        weights_split = [split_both(grad_gate_cols, grad_out)]
    else:
        weights_split = [split(grad_gate_cols, in_rows), split(grad_out, out_rows)]
    by_core = normed_out.reshape(n_x, 2, rows, cols)
    w_out = after(w_out, weights_split[0])

    def outward(values):
        return jnp.einsum("qtc,cd->qtd", values, w_out, preferred_element_type=F32)

    out_sent = outward(by_core[:, 1])
    out_kept = outward(by_core[:, 0])

    d_parts, g_x, g_skip = None, [], []
    waits = list(weights_split)
    split_early = []
    for t in range(n_steps):
        first, last = t == 0, t == n_steps - 1

        def block(*dims, at=(0, 0)):
            return pl.BlockSpec((1,) + dims, lambda q, at=at: (q,) + at)

        def flat(*dims, at=(0, 0)):
            return pl.BlockSpec(dims, lambda q, at=at: at)

        tile_at = 0 if last else LAST // WIDE + t
        operands = [
            (values_x, block(rows, WIDE, at=(0, t))), (bc, block(rows, state2)),
            (d_y, block(rows, WIDE, at=(0, t))), (incoming, block(STATE, WIDE, at=(0, t))),
            (later, block(STATE, WIDE, at=(0, t))),
            (col_table, block(1, rows, 128, at=(t, 0, 0))), (row_table, block(SEG_ROW + 8, rows)),
            (skip_l, flat(8, WIDE, at=(0, t))), (proj, block(long, WIDE, at=(0, tile_at))),
            (taps_x, flat(8, WIDE, at=(0, t))),
        ]
        if not first:
            operands.append((d_parts, block(rows, 2 * state2)))
        if last:
            operands += [
                (proj, block(long, 128, at=(0, keys_at + i))) for i in range(3)
            ] + [(taps_b, flat(8, state2)), (head_rows, flat(8, 128))]
        used = len(operands)
        operands += [(d_all, anywhere)] + [(v, anywhere) for v in waits]
        d_tile = 0 if last else (LAST + cols) // WIDE + t
        made = [
            (block(long, LAST if last else WIDE, at=(0, d_tile)), d_all.shape, BF),
            (block(8, WIDE), (groups, 8, WIDE), F32), (block(8, WIDE), (groups, 8, WIDE), F32),
        ]
        if last:
            made += [
                (block(8, state2), (groups, 8, state2), F32), (block(8, 128), (groups, 8, 128), F32),
            ]
        else:
            made += [(block(rows, 2 * state2), (groups, rows, 2 * state2), F32)]

        def body(*refs, t=t, first=first, last=last, used=used, n_out=len(made)):
            mix_back_kernel(
                *refs[:used], *refs[-n_out - 6 :], base=2 * PAIRS * t, first=first, last=last
            )

        outs = pl.pallas_call(
            body,
            grid=(groups,),
            in_specs=[spec for _, spec in operands],
            out_specs=[spec for spec, _, _ in made],
            out_shape=[jax.ShapeDtypeStruct(s, d) for _, s, d in made],
            scratch_shapes=[pltpu.VMEM((rows, WIDE), F32)]
            + [pltpu.VMEM((GROUP, GROUP), F32)] * 3
            + [pltpu.VMEM((GROUP, WIDE), BF), pltpu.VMEM((8, rows), F32)],
            input_output_aliases={used: 0},
            compiler_params=params(1),
            cost_estimate=cost(100 * big * GROUP, 16 * big),
            name="mix_back",
        )(*[v for v, _ in operands])
        d_all = outs[0]
        g_x.append(outs[1])
        g_skip.append(outs[2])
        if last:
            g_b, g_head = outs[3:]
        else:
            d_parts = outs[3]
            low = LAST + cols + t * WIDE
            split_early.append(split(grad_of(d_all, low, low + WIDE), in_rows))
            if first:
                weight_sums = [sum_over_b(v) for v in weights_split]
                out_own, out_others = sum_over_cores(out_kept, out_sent)
            waits = [split_early[-1]] + weight_sums * first + out_others * first
    if n_steps == 1:
        weight_sums = [sum_over_b(v) for v in weights_split]
        out_own, out_others = sum_over_cores(out_kept, out_sent)

    weight_totals = [sum_over_a(v) for v in weight_sums]
    stream = tokens.astype(F32)
    output = (stream + sum_to_owner(out_own, out_others)).astype(BF)
    early_sums = [sum_over_b(v, d_all) for v in split_early]

    if aligned:
        gate_part = weight_totals[0][:, :cols].reshape(groups, in_rows, cols)
        both = weight_totals[0][:, cols:]
        grad_out_proj = jnp.concatenate([both[:out_rows], both[out_rows:]], axis=1)
    else:
        gate_part, grad_out_proj = weight_totals[0], weight_totals[1][0]

    def to_owners(v):
        return exchange(v.astype(BF), ("x", "core"))

    d_all = after(d_all, output, *weight_totals)
    spill = along(d_all[:, rows:], -1)
    grad_last = grad_of(d_all, 0, LAST)
    split_last = split(grad_last, in_rows)
    last_sum = sum_over_b(split_last)
    early_part = [sum_over_a(after(v, *weight_totals)) for v in early_sums]
    d_sent = after(d_all, split_last, spill, *early_part)
    end = d_sent[:, rows - HALO : rows] + spill
    d_sent = lax.dynamic_update_slice_in_dim(d_sent, end, rows - HALO, 1)
    early_part = to_owners(jnp.concatenate([gate_part] + early_part, axis=2))

    def inward(d_values, core, kind):
        d_by = d_values.reshape(n_x, 2, long, all_cols)[:, core]
        return jnp.einsum("qtc,dc->qtd", d_by, w_all, preferred_element_type=F32).astype(kind)

    in_sent = inward(d_sent, 1, BF)
    in_kept = inward(d_sent, 0, F32)
    in_own, in_both = sum_over_cores(in_kept, after(in_sent, last_sum, early_part))
    in_others = [shift(v, "x", -sx - 1) for sx, v in enumerate(in_both)]

    def by_rows(wide=width):
        return pl.BlockSpec((128, wide), lambda i: (i, 0))

    grad_tokens = pl.pallas_call(
        norm_back_kernel,
        grid=(rows // 128,),
        in_specs=[by_rows()] * (3 + len(in_others)) + [pl.BlockSpec((8, width), lambda i: (0, 0))],
        out_specs=by_rows(),
        out_shape=shape(rows, width),
        compiler_params=params(1),
        name="input_norm_back",
    )(tokens, cotangent, in_own, *in_others, jnp.broadcast_to(gain_in, (8, width)))

    pieces = [to_owners(sum_over_a(after(last_sum, in_kept, *in_both))), early_part]
    grad_in_proj, gain_products = pl.pallas_call(
        lambda *refs: unpack_kernel(*refs, cols=cols, heads=heads),
        grid=(1,),
        in_specs=[pl.BlockSpec(p.shape, lambda i: (0, 0, 0)) for p in pieces]
        + [pl.BlockSpec(in_proj.shape, lambda i: (0, 0))],
        out_specs=[
            pl.BlockSpec(in_proj.shape, lambda i: (0, 0)), pl.BlockSpec((in_rows, 128), lambda i: (0, 0)),
        ],
        out_shape=[shape(*in_proj.shape), shape(in_rows, 128)],
        compiler_params=params(1),
        name="unpack_gradient",
    )(*pieces, in_proj)
    grad_norm = gain_products[:, 0] / norm_gain.astype(F32)

    def placed(v):
        out = jnp.zeros((groups,) + v.shape, F32)
        return lax.dynamic_update_slice_in_dim(out, v[None], me, 0)

    g_x = jnp.sum(jnp.concatenate(g_x, axis=2), axis=0)[: CONV + 1]
    g_b = jnp.sum(g_b, axis=0)[: CONV + 1]
    g_skip = jnp.sum(jnp.concatenate([g[:, 0] for g in g_skip], axis=1), axis=0)
    grad_skip_g = jnp.sum(g_skip.reshape(1, heads, HEADDIM), axis=2)
    g_head = jnp.sum(g_head, axis=0)[:2, :heads]
    pieces = [
        placed(g_x), g_b, placed(jnp.sum(gate_sums[:, 0], axis=0)),
        placed(jnp.concatenate([g_head, grad_skip_g], axis=0)),
    ]
    flat = jnp.concatenate([p.reshape(-1) for p in pieces])
    count = flat.shape[0]
    flat = jnp.pad(flat, (0, -count % 1024)).reshape(-1, 128)
    marks = [grad_last, split_last, in_sent, in_kept, in_own]
    flat = sum_over(flat, ("x", "a", "b", "core"), marks).reshape(-1)
    at, back = 0, []
    for p in pieces:
        back.append(flat[at : at + p.size].reshape(p.shape))
        at += p.size
    conv_x, conv_b, gate_all, head_all = back
    conv_sum = jnp.concatenate([conv_x.transpose(1, 0, 2).reshape(CONV + 1, INNER), conv_b], axis=1)
    conv_own = lax.dynamic_slice_in_dim(conv_sum, index * n_conv, n_conv, 1)
    grad_gate = lax.dynamic_slice_in_dim(gate_all.reshape(-1), index * n_gate, n_gate, 0)
    head_all = head_all.transpose(1, 0, 2).reshape(3, HEADS)
    return (
        output, grad_tokens, grad_in_proj, conv_own[:CONV], conv_own[CONV], grad_out_proj,
        grad_norm, grad_gate, head_all[0], head_all[1], head_all[2],
    )


def solution(mesh):
    n_dp, n_seq = mesh.shape["dp"], mesh.shape["seq"]
    slow = 4 if n_seq % 4 == 0 else 1
    finer = Mesh(
        mesh.devices.reshape(n_dp // 2, 2, slow, n_seq // slow), ("x", "core", "a", "b")
    )
    every = ("x", "core", "a", "b")
    rows, flat, second, copied = P(every, None), P(every), P(None, every), P()
    in_specs = (rows, flat, rows, second, flat, rows, flat, flat, copied, copied, copied, rows)
    out_specs = (rows, rows, rows, second, flat, rows, flat, flat, copied, copied, copied)
    return jax.shard_map(
        on_device, mesh=finer, in_specs=in_specs, out_specs=out_specs, check_vma=False
    )
```
